128 devices in a mesh: band: 32 (over z, x, core), sub: 4 (over y).
Axes of the slice: x: 4, y: 4, z: 4, core: 2. Of those that a mesh axis runs over, the one named last changes fastest.
Arguments:
- level_set: float32 [8, 8, 8, 65536], P(None, None, None, ('band', 'sub')), may hold values from -6 to 6
- velocity: float32 [3, 8, 8, 8, 65536], P(None, None, None, None, ('band', 'sub')), may hold values from -3 to 3
- neighbours: int32 [6, 65536], P(None, ('band', 'sub')), may hold values from -1 to 65535, as said below
Outputs:
- advected: float32 [8, 8, 8, 65536], P(None, None, None, ('band', 'sub'))
- reinitialized: float32 [8, 8, 8, 65536], P(None, None, None, ('band', 'sub'))
The draws below stay inside these ranges and needn't reach their ends.
Inputs may be any that keep to these rules, and one draw needn't show every extreme that they name: `neighbours`: links are symmetric (if tile a is the +x neighbour of b then b is the -x neighbour of a, likewise for y and z). Tile t lives on device t // 512 of the flattened band+sub order. An x neighbour is on the same device or on the device whose band index is one less (for -x) or one more (for +x) with the same sub index; a y neighbour likewise on sub index one less or one more with the same band index; a z neighbour always on the same device. Between two devices adjacent along band there are exactly 16 * 16 x links, along sub exactly 2 * 16 y links.
All inputs are finite; a program needn't handle non-finite values. Where the reference program divides by a largest or mean magnitude, that divisor is 1e-20 or more.
Results may differ from the reference program's by a relative error of at most 0.0003.
Values sent between devices are 32-bit elements; how exact they have to be, the bound alone decides.
A program may use at most 64 MiB of HBM per device.

```python
import jax
import jax.numpy as jnp
from jax import lax

TILES_FIRST = 2
TILES_SECOND = 16
TILES_THIRD = 16
REINIT = 2
TILES_DEV = 512
TILES = 65536
N_BAND = 32
N_SUB = 4


def draw_neighbours(key, part):
    key = jax.random.fold_in(key, 11)
    devices = N_BAND * N_SUB
    per_device = TILES_FIRST * TILES_SECOND * TILES_THIRD
    keys = jax.random.split(jax.random.fold_in(key, 1), devices)
    perms = jax.vmap(lambda single: jax.random.permutation(single, per_device))(keys).astype(jnp.int32)
    rows_index = jnp.repeat(jnp.arange(devices, dtype=jnp.int32), per_device)
    inverse = jnp.zeros((devices, per_device), jnp.int32).at[rows_index, perms.reshape(-1)].set(jnp.tile(jnp.arange(per_device, dtype=jnp.int32), devices))
    ids = jnp.arange(devices * per_device, dtype=jnp.int32)
    device_of = ids // per_device
    place = perms.reshape(-1)
    coord_x = device_of // N_SUB * TILES_FIRST + place // (TILES_SECOND * TILES_THIRD)
    coord_y = device_of % N_SUB * TILES_SECOND + place // TILES_THIRD % TILES_SECOND
    coord_z = place % TILES_THIRD
    wide_x = TILES_FIRST * N_BAND
    wide_y = TILES_SECOND * N_SUB
    cut_x = jax.random.randint(jax.random.fold_in(key, 2), (wide_x, wide_y, TILES_THIRD), 0, 8) == 0
    cut_x = cut_x & ((jnp.arange(wide_x) + 1) % TILES_FIRST != 0)[:, None, None]
    cut_y = jax.random.randint(jax.random.fold_in(key, 3), (wide_x, wide_y, TILES_THIRD), 0, 8) == 0
    cut_y = cut_y & ((jnp.arange(wide_y) + 1) % TILES_SECOND != 0)[None, :, None]
    cut_z = jax.random.randint(jax.random.fold_in(key, 4), (wide_x, wide_y, TILES_THIRD), 0, 8) == 0

    def locate(spot_x, spot_y, spot_z):
        spot_x = jnp.clip(spot_x, 0, wide_x - 1)
        spot_y = jnp.clip(spot_y, 0, wide_y - 1)
        spot_z = jnp.clip(spot_z, 0, TILES_THIRD - 1)
        target = spot_x // TILES_FIRST * N_SUB + spot_y // TILES_SECOND
        inside = spot_x % TILES_FIRST * TILES_SECOND * TILES_THIRD + spot_y % TILES_SECOND * TILES_THIRD + spot_z
        return target * per_device + inverse[target, inside]
    low_x = jnp.clip(coord_x - 1, 0, wide_x - 1)
    low_y = jnp.clip(coord_y - 1, 0, wide_y - 1)
    low_z = jnp.clip(coord_z - 1, 0, TILES_THIRD - 1)
    valid = [(coord_x > 0) & ~cut_x[low_x, coord_y, coord_z], (coord_x < wide_x - 1) & ~cut_x[coord_x, coord_y, coord_z], (coord_y > 0) & ~cut_y[coord_x, low_y, coord_z], (coord_y < wide_y - 1) & ~cut_y[coord_x, coord_y, coord_z], (coord_z > 0) & ~cut_z[coord_x, coord_y, low_z], (coord_z < TILES_THIRD - 1) & ~cut_z[coord_x, coord_y, coord_z]]
    found = [locate(coord_x - 1, coord_y, coord_z), locate(coord_x + 1, coord_y, coord_z), locate(coord_x, coord_y - 1, coord_z), locate(coord_x, coord_y + 1, coord_z), locate(coord_x, coord_y, coord_z - 1), locate(coord_x, coord_y, coord_z + 1)]
    return jnp.stack([jnp.where(valid[side], found[side], -1) for side in range(6)]).astype(jnp.int32)


def draw_velocity(key, part):
    key = jax.random.fold_in(key, 23)
    raw = jax.random.uniform(key, (3, 8, 8, 8, TILES), jnp.float32, -1.0, 1.0)
    factor_key = jax.random.fold_in(key, 7)
    factor = jax.random.uniform(factor_key, (), jnp.float32, 0.8, 1.0)
    tile_device = (jnp.arange(TILES, dtype=jnp.int32) // (TILES_FIRST * TILES_SECOND * TILES_THIRD)).astype(jnp.float32)
    scale = 1.0 + 2.0 * tile_device / (N_BAND * N_SUB - 1)
    return (raw * scale * factor).astype(jnp.float32)


def block_levels(stream_key, shape, cuts, smallest, high):
    factor_of = 1.0
    for dim, parts in cuts:
        steps = jax.random.uniform(jax.random.fold_in(jax.random.fold_in(stream_key, 6), dim), (parts,), jnp.float32, smallest / len(cuts), high / len(cuts))
        factor_of = factor_of * jnp.repeat(jnp.exp(steps), shape[dim] // parts).reshape((-1,) + (1,) * (len(shape) - 1 - dim))
    return factor_of


def bell_draw(rng, shape, deviation, most, shards=(), kind=jnp.bfloat16):
    drawn = jax.random.normal(rng, shape, jnp.float32) * deviation
    if len(shards) > 0:
        drawn = block_levels(rng, shape, shards, -0.22, 0.18) * drawn
    return jnp.clip(drawn, min=-most, max=most).astype(kind)


def setup_inputs(seed: int = 0) -> dict:
    key_list = jax.random.split(jax.random.key(seed), 4)
    level_set = bell_draw(key_list[0], (8, 8, 8, TILES), 1.0, 6.0, ((3, 128),), jnp.float32)
    velocity = draw_velocity(jax.random.fold_in(key_list[3], 71), 0)
    neighbours = draw_neighbours(jax.random.fold_in(key_list[3], 71), 0)
    return {"level_set": level_set, "velocity": velocity, "neighbours": neighbours}


EPS = 1e-06
CFL = 0.5
DTAU = 0.3
ROOT_EPS = 1e-06

def weno_slope(diff_a, diff_b, diff_c, diff_d, diff_e):
    smooth_a = 13.0 / 12.0 * (diff_a - 2.0 * diff_b + diff_c) ** 2 + 0.25 * (diff_a - 4.0 * diff_b + 3.0 * diff_c) ** 2
    smooth_b = 13.0 / 12.0 * (diff_b - 2.0 * diff_c + diff_d) ** 2 + 0.25 * (diff_b - diff_d) ** 2
    smooth_c = 13.0 / 12.0 * (diff_c - 2.0 * diff_d + diff_e) ** 2 + 0.25 * (3.0 * diff_c - 4.0 * diff_d + diff_e) ** 2
    alpha_a = 0.1 / (EPS + smooth_a) ** 2
    alpha_b = 0.6 / (EPS + smooth_b) ** 2
    alpha_c = 0.3 / (EPS + smooth_c) ** 2
    total = alpha_a + alpha_b + alpha_c
    mixed = alpha_a * (diff_a / 3.0 - 7.0 * diff_b / 6.0 + 11.0 * diff_c / 6.0)
    mixed = mixed + alpha_b * (-diff_b / 6.0 + 5.0 * diff_c / 6.0 + diff_d / 3.0)
    mixed = mixed + alpha_c * (diff_c / 3.0 + 5.0 * diff_d / 6.0 - diff_e / 6.0)
    return mixed / total

def one_sided(padded, along):
    diffs = lax.slice_in_dim(padded, 1, 14, axis=along) - lax.slice_in_dim(padded, 0, 13, axis=along)
    pieces = [lax.slice_in_dim(diffs, start, start + 8, axis=along) for start in range(6)]
    backward = weno_slope(pieces[0], pieces[1], pieces[2], pieces[3], pieces[4])
    forward = weno_slope(pieces[5], pieces[4], pieces[3], pieces[2], pieces[1])
    return (backward, forward)

def advect_rate(padded, flow):
    total = jnp.zeros(flow.shape[1:], jnp.float32)
    for along in range(3):
        backward, forward = one_sided(padded[along], along)
        component = flow[along]
        total = total - component * jnp.where(component > 0, backward, forward)
    return total

def reinit_rate(padded, sign):
    squares = jnp.zeros(sign.shape, jnp.float32)
    for along in range(3):
        backward, forward = one_sided(padded[along], along)
        positive = jnp.maximum(jnp.maximum(backward, 0.0) ** 2, jnp.minimum(forward, 0.0) ** 2)
        negative = jnp.maximum(jnp.minimum(backward, 0.0) ** 2, jnp.maximum(forward, 0.0) ** 2)
        squares = squares + jnp.where(sign > 0, positive, negative)
    return sign * (1.0 - jnp.sqrt(squares + ROOT_EPS))

def face_slab(layers_all, ids, own_block, along, edge_at):
    fetched = jnp.take(layers_all, jnp.maximum(ids, 0), axis=3)
    edge_fill = jnp.repeat(lax.slice_in_dim(own_block, edge_at, edge_at + 1, axis=along), 3, axis=along)
    return jnp.where(ids < 0, edge_fill, fetched)

def rates(distance_grid, extra, neighbours, rate_fn):
    faces = [lax.slice_in_dim(distance_grid, start, start + 3, axis=along) for along in range(3) for start in (5, 0)]

    def per_block(block_id):
        start = block_id * TILES_DEV
        own_block = lax.dynamic_slice_in_dim(distance_grid, start, TILES_DEV, axis=3)
        ids = lax.dynamic_slice_in_dim(neighbours, start, TILES_DEV, axis=1)
        part_extra = lax.dynamic_slice_in_dim(extra, start, TILES_DEV, axis=extra.ndim - 1)
        padded = []
        for along in range(3):
            lower = face_slab(faces[2 * along], ids[2 * along], own_block, along, 0)
            upper = face_slab(faces[2 * along + 1], ids[2 * along + 1], own_block, along, 7)
            padded.append(jnp.concatenate([lower, own_block, upper], axis=along))
        return rate_fn(padded, part_extra)
    stacked = lax.map(per_block, jnp.arange(TILES // TILES_DEV, dtype=jnp.int32))
    return jnp.moveaxis(stacked, 0, 3).reshape(8, 8, 8, TILES)

def reference(level_set, velocity, neighbours):
    top_speed = jnp.max(lax.optimization_barrier(jnp.sum(jnp.abs(velocity), axis=0)))
    step_size = CFL / top_speed
    section_one = level_set + step_size * rates(level_set, velocity, neighbours, advect_rate)
    section_two = 0.75 * level_set + 0.25 * (section_one + step_size * rates(section_one, velocity, neighbours, advect_rate))
    advected = level_set / 3.0 + 2.0 / 3.0 * (section_two + step_size * rates(section_two, velocity, neighbours, advect_rate))
    sign = advected / jnp.sqrt(advected * advected + 1.0)
    current = advected
    for sweep in range(REINIT):
        current = current + DTAU * rates(current, sign, neighbours, reinit_rate)
    return (advected, current)
```

```python
import functools

import jax
import jax.numpy as jnp
from jax import lax
from jax.experimental import pallas as pl
from jax.experimental.pallas import tpu as pltpu
from jax.sharding import PartitionSpec as P

TILES_DEV = 512
SLOTS_X = 256
SLOTS_Y = 128
FACE = 192
STAGES = 3
REINIT = 2
STEPS = STAGES + REINIT
EPS = 1e-06
CFL = 0.5
DTAU = 0.3
ROOT_EPS = 1e-06
LANES = 128
GROUPS = TILES_DEV // LANES

F32 = jnp.float32
BF16 = jnp.bfloat16
MESH = pl.DeviceIdType.MESH


def differences(p):
    first = [p[k + 1] - p[k] for k in range(13)]
    second = [first[k + 1] - first[k] for k in range(12)]
    third = [second[k + 1] - second[k] for k in range(11)]
    fourth = [None] + [third[k] - third[k - 1] for k in range(1, 11)]
    square = [e * e for e in second]
    ind_a, ind_b, ind_c = {}, {}, {}
    for k in range(11):
        half = (0.5 * second[k]) * second[k + 1]
        base = third[k] * third[k] * (2.0 / 3.0) + 0.5 * EPS
        low = base - half
        if k <= 8:
            ind_a[k] = low + square[k + 1]
        if 1 <= k <= 9:
            ind_b[k] = base + half
        if k >= 2:
            ind_c[k] = low + square[k]
    return third, fourth, ind_a, ind_b, ind_c


def recip(x):
    return pl.reciprocal(x, approx=True)


def advect_line(p, flow):
    third, fourth, ind_a, ind_b, ind_c = differences(p)
    out = []
    for c in range(8):
        up = flow[c] > 0
        ra = recip(jnp.where(up, ind_a[c], ind_c[c + 3]))
        rb = recip(jnp.where(up, ind_b[c + 1], ind_b[c + 2]))
        rc = recip(jnp.where(up, ind_c[c + 2], ind_a[c + 1]))
        wa = ra * ra
        wb = rb * rb * 6.0
        wc = rc * rc * 3.0
        far = jnp.where(up, fourth[c + 1], fourth[c + 3])
        num = wa * (far + far) + wc * fourth[c + 2]
        corr = num * recip(wa + wb + wc)
        linear = 3.0 * (p[c + 4] - p[c + 2]) - jnp.where(up, third[c + 1], third[c + 2])
        out.append(flow[c] * linear - jnp.abs(flow[c]) * corr)
    return out


def reinit_line(p, sign):
    third, fourth, ind_a, ind_b, ind_c = differences(p)
    wa, wa3, wb, wc, wc3 = {}, {}, {}, {}, {}
    for k, v in ind_a.items():
        r = recip(v)
        wa[k] = r * r
        wa3[k] = wa[k] * 3.0
    for k, v in ind_b.items():
        r = recip(v)
        wb[k] = r * r * 6.0
    for k, v in ind_c.items():
        r = recip(v)
        wc[k] = r * r
        wc3[k] = wc[k] * 3.0
    twice = [None] + [f + f for f in fourth[1:]]
    out = []
    for c in range(8):
        linear = 3.0 * (p[c + 4] - p[c + 2])
        corr_b = (wa[c] * twice[c + 1] + wc3[c + 2] * fourth[c + 2]) * recip(wa[c] + wb[c + 1] + wc3[c + 2])
        corr_f = (wc[c + 3] * twice[c + 3] + wa3[c + 1] * fourth[c + 2]) * recip(wc[c + 3] + wb[c + 2] + wa3[c + 1])
        back = linear - third[c + 1] - corr_b
        fore = third[c + 2] - linear - corr_f
        m = jnp.maximum(jnp.maximum(sign[c] * back, sign[c] * fore), 0.0)
        out.append(m * m)
    return out


def split_rows(value):
    hi = value.astype(BF16)
    lo = (value - hi.astype(F32)).astype(BF16)
    return hi, lo


def kernel(
    n_band, n_sub, group,
    ls_ref, vel_ref, nb_ref, adv_out, out_ref,
    p0, pc, adv, sgn, vel, az, ay, halo, faces, local_m, pack_x, pack_y, unpack_x, unpack_y, tri, pres,
    nb_s, ids_s, krow, kcol, send_x, send_y, recv_x, recv_y, ar_send, ar_sub, ar_grp, ar_z, step_s,
    in_sem, out_sem, tx_sem, rx_sem, ar_tx, ar_rx,
):
    band = lax.axis_index("band")
    sub = lax.axis_index("sub")
    n_z = n_band // group
    band_up, band_dn = lax.rem(band + 1, n_band), lax.rem(band + n_band - 1, n_band)
    sub_up, sub_dn = lax.rem(sub + 1, n_sub), lax.rem(sub + n_sub - 1, n_sub)
    first_of_group = band - lax.rem(band, group)

    def sub_peer(d):
        return (band, lax.rem(sub + d, n_sub))

    def group_peer(d):
        return (first_of_group + lax.rem(lax.rem(band, group) + d, group), sub)

    def z_peer(d):
        return (lax.rem(band + d * group, n_band), sub)

    def lanes(g):
        return pl.ds(g * LANES, LANES)

    in_copies = []
    for g in range(GROUPS):
        in_copies.append(pltpu.make_async_copy(ls_ref.at[:, :, lanes(g)], p0.at[g], in_sem.at[g]))
    for k in range(3):
        for g in range(GROUPS):
            in_copies.append(
                pltpu.make_async_copy(vel_ref.at[k, :, :, lanes(g)], vel.at[k, g], in_sem.at[4 + 4 * k + g])
            )
    for copy in in_copies:
        copy.start()

    peers = [(band_up, sub), (band_dn, sub)]
    peers += [sub_peer(d) for d in range(1, n_sub)]
    peers += [group_peer(d) for d in range(1, group)]
    peers += [z_peer(d) for d in range(1, n_z)]
    barrier = pltpu.get_barrier_semaphore()
    for peer in peers:
        pl.semaphore_signal(barrier, inc=1, device_id=peer, device_id_type=MESH)

    nb_s[...] = jnp.full((8, TILES_DEV), -1, jnp.int32)
    nb_s[0:6, :] = nb_ref[...]
    nb = nb_s[...]
    base = (band * n_sub + sub) * TILES_DEV
    present = nb >= 0
    is_local = (nb >= base) & (nb < base + TILES_DEV)
    remote = present & jnp.logical_not(is_local)
    ids_s[0] = jnp.where(is_local, nb - base, -1)
    presf = jnp.where(present, 1.0, 0.0)
    for d in range(6):
        for g in range(GROUPS):
            pres[d, g] = jnp.broadcast_to(presf[d : d + 1, g * LANES : (g + 1) * LANES], (16, LANES))

    def fill(k, carry):
        rows = pl.ds(pl.multiple_of(16 * k, 16), 16)
        iota = lax.broadcasted_iota(jnp.int32, (16, TILES_DEV), 0) + 16 * k
        for d in range(6):
            local_m[d, rows, :] = jnp.where(iota == ids_s[0, d : d + 1, :], 1.0, 0.0).astype(BF16)
        lane = lax.broadcasted_iota(jnp.int32, (16, TILES_DEV), 1)
        tri[rows, :] = jnp.where(iota < lane, 1.0, 0.0).astype(BF16)
        return carry

    lax.fori_loop(0, TILES_DEV // 16, fill, 0)

    flags = jnp.where(remote, 1.0, 0.0)
    flags16 = jnp.concatenate([flags, jnp.zeros_like(flags)], axis=0).astype(BF16)
    place = jnp.dot(flags16, tri[...], preferred_element_type=F32)[0:8]
    keys = jnp.where(remote, nb.astype(F32), 1e9)
    krow[...] = jnp.zeros_like(krow)
    krow[0:4, :] = keys[0:4]
    krow[4:8, :] = jnp.where(remote, place, -1.0)[0:4]
    for c in range(GROUPS):
        kcol[c * LANES : (c + 1) * LANES, :] = krow[:, c * LANES : (c + 1) * LANES].T

    def count(k, carry):
        rows = pl.ds(pl.multiple_of(8 * k, 8), 8)
        return tuple(
            total + jnp.where(kcol[rows, d : d + 1] < krow[d : d + 1, :], 1.0, 0.0) for d, total in enumerate(carry)
        )

    zero = jnp.zeros((8, TILES_DEV), F32)
    counts = lax.fori_loop(0, TILES_DEV // 8, count, (zero,) * 4)
    for d in range(4):
        rank = jnp.sum(counts[d], axis=0, keepdims=True).astype(jnp.int32)
        ids_s[1, d : d + 1, :] = jnp.where(remote[d : d + 1], rank, -1)

    def fill_pack(k, carry):
        rows = pl.ds(pl.multiple_of(16 * k, 16), 16)
        lane_x = lax.broadcasted_iota(jnp.int32, (16, SLOTS_X), 1).astype(F32)
        lane_y = lax.broadcasted_iota(jnp.int32, (16, SLOTS_Y), 1).astype(F32)
        for d in range(2):
            pack_x[d, rows, :] = jnp.where(kcol[rows, 4 + d : 5 + d] == lane_x, 1.0, 0.0).astype(BF16)
            pack_y[d, rows, :] = jnp.where(kcol[rows, 6 + d : 7 + d] == lane_y, 1.0, 0.0).astype(BF16)
        return carry

    lax.fori_loop(0, TILES_DEV // 16, fill_pack, 0)

    def fill_unpack(d, dest):
        def body(k, carry):
            rows = pl.ds(pl.multiple_of(16 * k, 16), 16)
            iota = lax.broadcasted_iota(jnp.int32, (16, TILES_DEV), 0) + 16 * k
            dest[d % 2, rows, :] = jnp.where(iota == ids_s[1, d : d + 1, :], 1.0, 0.0).astype(BF16)
            return carry

        lax.fori_loop(0, dest.shape[1] // 16, body, 0)

    for d in range(4):
        fill_unpack(d, unpack_x if d < 2 else unpack_y)

    for copy in in_copies[:GROUPS]:
        copy.wait()

    def copy_in(x, carry):
        for g in range(GROUPS):
            pc[g, x] = p0[g, x]
        return carry

    lax.fori_loop(0, 8, copy_in, 0)
    for copy in in_copies[GROUPS:]:
        copy.wait()

    def speeds(idx, top):
        g, x = idx // 8, lax.rem(idx, 8)
        for y in range(8):
            rows = slice(8 * y, 8 * y + 8)
            total = jnp.abs(vel[0, g, x, rows, :]) + jnp.abs(vel[1, g, x, rows, :]) + jnp.abs(vel[2, g, x, rows, :])
            top = jnp.maximum(top, total)
        turned = [vel[2, g, x, pl.ds(z, 8, stride=8), :] for z in range(8)]
        for z in range(8):
            az[g, x, 8 * z : 8 * z + 8, :] = turned[z]
        return top

    top = lax.fori_loop(0, GROUPS * 8, speeds, jnp.zeros((8, LANES), F32))

    def turn_back(idx, carry):
        g, x = idx // 8, lax.rem(idx, 8)
        vel[2, g, x] = az[g, x]
        return carry

    lax.fori_loop(0, GROUPS * 8, turn_back, 0)

    pl.semaphore_wait(barrier, len(peers))

    def ar_copies(r):
        peer, slots, n = ((sub_peer, ar_sub, n_sub), (group_peer, ar_grp, group), (z_peer, ar_z, n_z))[r]
        first = (0, n_sub, n_sub + group)[r]
        return [
            pltpu.make_async_remote_copy(
                src_ref=ar_send.at[r],
                dst_ref=slots.at[d - 1],
                send_sem=ar_tx.at[first + d - 1],
                recv_sem=ar_rx.at[first + d - 1],
                device_id=peer(d),
                device_id_type=MESH,
            )
            for d in range(1, n)
        ], slots

    def ar_start(r, value):
        ar_send[r] = value
        for copy in ar_copies(r)[0]:
            copy.start()

    def ar_finish(r):
        value = ar_send[r]
        copies, slots = ar_copies(r)
        for k, copy in enumerate(copies):
            copy.wait()
            value = jnp.maximum(value, slots[k])
        return value

    ar_start(0, top)

    def exchange(t):
        targets = [(band_dn, sub), (band_up, sub), (band, sub_dn), (band, sub_up)]
        copies = []
        for d in range(4):
            src, dst = (send_x, recv_x) if d < 2 else (send_y, recv_y)
            copies.append(
                pltpu.make_async_remote_copy(
                    src_ref=src.at[d % 2],
                    dst_ref=dst.at[t, 1 - d % 2],
                    send_sem=tx_sem.at[d],
                    recv_sem=rx_sem.at[t, d],
                    device_id=targets[d],
                    device_id_type=MESH,
                )
            )
        return copies

    def put_face(d, row, g, value):
        hi, lo = split_rows(value)
        col = pl.ds(pl.multiple_of(g * LANES, LANES), LANES)
        faces[d, pl.ds(pl.multiple_of(row, 16), 16), col] = hi
        faces[d, pl.ds(pl.multiple_of(row + FACE, 16), 16), col] = lo

    def faces_x():
        def body(idx, carry):
            g, r = idx // 4, lax.rem(idx, 4)
            rows = pl.ds(pl.multiple_of(16 * r, 16), 16)
            for d, start in ((0, 5), (1, 0)):
                for l in range(3):
                    put_face(d, 64 * l + 16 * r, g, pc[g, start + l, rows, :])
            return carry

        lax.fori_loop(0, 4 * GROUPS, body, 0)

    def faces_y():
        def body(idx, carry):
            g, i = idx // 4, lax.rem(idx, 4)
            for d, start in ((2, 5), (3, 0)):
                for l in range(3):
                    y = start + l
                    value = pc[g, pl.ds(2 * i, 2), 8 * y : 8 * y + 8, :].reshape(16, LANES)
                    put_face(d, 64 * l + 16 * i, g, value)
            return carry

        lax.fori_loop(0, 4 * GROUPS, body, 0)

    def turned_pair(ref, g, i, k):
        return jnp.concatenate([ref[g, 2 * i + j, pl.ds(k, 8, stride=8), :] for j in range(2)], axis=0)

    def faces_z():
        def body(idx, carry):
            g, i = idx // 4, lax.rem(idx, 4)
            for d, start in ((4, 5), (5, 0)):
                for l in range(3):
                    put_face(d, 64 * l + 16 * i, g, turned_pair(pc, g, i, start + l))
            return carry

        lax.fori_loop(0, 4 * GROUPS, body, 0)

    def two_part_dot(lhs, rhs):
        res = jnp.dot(lhs, rhs, preferred_element_type=F32)
        return res[:FACE] + res[FACE:]

    def gather(d):
        res = two_part_dot(faces[d], local_m[d])
        for g in range(GROUPS):
            halo[d, g] = res[:, g * LANES : (g + 1) * LANES]

    def unpack(d, t):
        block = recv_x[t, d] if d < 2 else recv_y[t, d - 2]
        hi, lo = split_rows(block)
        matrix = unpack_x[d] if d < 2 else unpack_y[d - 2]
        res = two_part_dot(jnp.concatenate([hi, lo], axis=0), matrix)
        for g in range(GROUPS):
            halo[d, g] = halo[d, g] + res[:, g * LANES : (g + 1) * LANES]

    def padded(d, g, row, cells):
        rows = [pl.ds(pl.multiple_of(64 * l + row, 16), 16) for l in range(3)]
        there_lo = pres[d, g] > 0
        there_hi = pres[d + 1, g] > 0
        low = [jnp.where(there_lo, halo[d, g, rows[l], :], cells[0]) for l in range(3)]
        high = [jnp.where(there_hi, halo[d + 1, g, rows[l], :], cells[7]) for l in range(3)]
        return low + cells + high

    def pair(ref, g, i, k):
        return ref[g, pl.ds(2 * i, 2), 8 * k : 8 * k + 8, :].reshape(16, LANES)

    def z_lines(line, extra, g, i):
        cells = [turned_pair(pc, g, i, z) for z in range(8)]
        for z, value in enumerate(line(padded(4, g, 16 * i, cells), extra(g, i))):
            az[g, pl.ds(2 * i, 2), 8 * z : 8 * z + 8, :] = value.reshape(2, 8, LANES)

    def y_lines(line, extra, g, i):
        cells = [pair(pc, g, i, y) for y in range(8)]
        for y, value in enumerate(line(padded(2, g, 16 * i, cells), extra(g, i))):
            ay[g, pl.ds(2 * i, 2), 8 * y : 8 * y + 8, :] = (value + turned_pair(az, g, i, y)).reshape(2, 8, LANES)

    def x_lines(line, extra, finish, g, r):
        rows = pl.ds(pl.multiple_of(16 * r, 16), 16)
        cells = [pc[g, x, rows, :] for x in range(8)]
        for x, value in enumerate(line(padded(0, g, 16 * r, cells), extra(g, rows))):
            finish(g, x, rows, cells[x], value + ay[g, x, rows, :])

    def begin(t):
        faces_x()
        copies = exchange(t)
        send_x[0] = two_part_dot(faces[1], pack_x[0])
        copies[0].start()
        send_x[1] = two_part_dot(faces[0], pack_x[1])
        copies[1].start()
        faces_y()
        send_y[0] = two_part_dot(faces[3], pack_y[0])
        copies[2].start()
        send_y[1] = two_part_dot(faces[2], pack_y[1])
        copies[3].start()
        faces_z()
        gather(4)
        gather(5)
        return copies

    def run(t, line, extra_z, extra_y, extra_x, finish, after_z=None, after_y=None):
        copies = begin(t)

        def z_body(k, carry):
            gather(k)
            for i in range(4):
                z_lines(line, extra_z, k, i)
            return carry

        lax.fori_loop(0, 4, z_body, 0)
        if after_z is not None:
            after_z()
        copies[2].wait_recv()
        copies[3].wait_recv()
        unpack(2, t)
        unpack(3, t)

        def y_body(k, carry):
            y_lines(line, extra_y, k // 4, lax.rem(k, 4))
            return carry

        lax.fori_loop(0, 4 * GROUPS, y_body, 0)
        if after_y is not None:
            after_y()
        copies[0].wait_recv()
        copies[1].wait_recv()
        unpack(0, t)
        unpack(1, t)

        def x_body(k, carry):
            x_lines(line, extra_x, finish, k // 4, lax.rem(k, 4))
            return carry

        lax.fori_loop(0, 4 * GROUPS, x_body, 0)
        for copy in copies:
            copy.wait_send()

    def advect_step(t, carry):
        def after_z():
            @pl.when(t == 0)
            def _():
                ar_start(1, ar_finish(0))

        def after_y():
            @pl.when(t == 0)
            def _():
                ar_start(2, ar_finish(1))
                top = ar_finish(2)
                top = jnp.max(jnp.max(top, axis=1, keepdims=True), axis=0, keepdims=True)
                step_s[...] = jnp.broadcast_to((CFL / 6.0) / top, (16, LANES))

        old = jnp.where(t == 0, 0.0, jnp.where(t == 1, 0.75, 1.0 / 3.0))
        new = jnp.where(t == 0, 1.0, jnp.where(t == 1, 0.25, 2.0 / 3.0))

        def finish(g, x, rows, cell, total):
            value = old * p0[g, x, rows, :] + new * (cell - step_s[...] * total)
            pc[g, x, rows, :] = value
            adv[g, x, rows, :] = value
            sgn[g, x, rows, :] = jnp.where(value > 0, 1.0, -1.0)

        run(
            t,
            advect_line,
            lambda g, i: [pair(vel.at[2], g, i, z) for z in range(8)],
            lambda g, i: [pair(vel.at[1], g, i, y) for y in range(8)],
            lambda g, rows: [vel[0, g, x, rows, :] for x in range(8)],
            finish,
            after_z,
            after_y,
        )
        return carry

    lax.fori_loop(0, STAGES, advect_step, 0)

    adv_copies = [
        pltpu.make_async_copy(adv.at[g], adv_out.at[:, :, lanes(g)], out_sem.at[g]) for g in range(GROUPS)
    ]
    for copy in adv_copies:
        copy.start()

    def reinit_step(k, carry):
        def finish(g, x, rows, cell, total):
            v = adv[g, x, rows, :]
            sign = v * lax.rsqrt(v * v + 1.0)
            root = total * (1.0 / 36.0) + ROOT_EPS
            pc[g, x, rows, :] = cell + (DTAU * sign) * (1.0 - root * lax.rsqrt(root))

        run(
            STAGES + k,
            reinit_line,
            lambda g, i: [turned_pair(sgn, g, i, z) for z in range(8)],
            lambda g, i: [pair(sgn, g, i, y) for y in range(8)],
            lambda g, rows: [sgn[g, x, rows, :] for x in range(8)],
            finish,
        )
        return carry

    lax.fori_loop(0, REINIT, reinit_step, 0)

    out_copies = [
        pltpu.make_async_copy(pc.at[g], out_ref.at[:, :, lanes(g)], out_sem.at[GROUPS + g]) for g in range(GROUPS)
    ]
    for copy in out_copies:
        copy.start()
    for copy in adv_copies + out_copies:
        copy.wait()


def solution(mesh):
    n_band, n_sub = mesh.shape["band"], mesh.shape["sub"]
    group = min(8, n_band)
    n_z = n_band // group
    cells = (GROUPS, 8, 64, LANES)

    def local(level_set, velocity, neighbours):
        whole = jax.ShapeDtypeStruct((8, 64, TILES_DEV), F32)
        anywhere = pl.BlockSpec(memory_space=pl.ANY)
        advected, reinitialized = pl.pallas_call(
            functools.partial(kernel, n_band, n_sub, group),
            out_shape=(whole, whole),
            in_specs=[anywhere, anywhere, pl.BlockSpec(memory_space=pltpu.VMEM)],
            out_specs=(anywhere, anywhere),
            scratch_shapes=[
                pltpu.VMEM(cells, F32),
                pltpu.VMEM(cells, F32),
                pltpu.VMEM(cells, F32),
                pltpu.VMEM(cells, F32),
                pltpu.VMEM((3,) + cells, F32),
                pltpu.VMEM(cells, F32),
                pltpu.VMEM(cells, F32),
                pltpu.VMEM((6, GROUPS, FACE, LANES), F32),
                pltpu.VMEM((6, 2 * FACE, TILES_DEV), BF16),
                pltpu.VMEM((6, TILES_DEV, TILES_DEV), BF16),
                pltpu.VMEM((2, TILES_DEV, SLOTS_X), BF16),
                pltpu.VMEM((2, TILES_DEV, SLOTS_Y), BF16),
                pltpu.VMEM((2, SLOTS_X, TILES_DEV), BF16),
                pltpu.VMEM((2, SLOTS_Y, TILES_DEV), BF16),
                pltpu.VMEM((TILES_DEV, TILES_DEV), BF16),
                pltpu.VMEM((6, GROUPS, 16, LANES), F32),
                pltpu.VMEM((8, TILES_DEV), jnp.int32),
                pltpu.VMEM((2, 8, TILES_DEV), jnp.int32),
                pltpu.VMEM((LANES, TILES_DEV), F32),
                pltpu.VMEM((TILES_DEV, LANES), F32),
                pltpu.VMEM((2, FACE, SLOTS_X), F32),
                pltpu.VMEM((2, FACE, SLOTS_Y), F32),
                pltpu.VMEM((STEPS, 2, FACE, SLOTS_X), F32),
                pltpu.VMEM((STEPS, 2, FACE, SLOTS_Y), F32),
                pltpu.VMEM((3, 8, LANES), F32),
                pltpu.VMEM((max(1, n_sub - 1), 8, LANES), F32),
                pltpu.VMEM((max(1, group - 1), 8, LANES), F32),
                pltpu.VMEM((max(1, n_z - 1), 8, LANES), F32),
                pltpu.VMEM((16, LANES), F32),
                pltpu.SemaphoreType.DMA((16,)),
                pltpu.SemaphoreType.DMA((2 * GROUPS,)),
                pltpu.SemaphoreType.DMA((4,)),
                pltpu.SemaphoreType.DMA((STEPS, 4)),
                pltpu.SemaphoreType.DMA((n_sub + group + n_z,)),
                pltpu.SemaphoreType.DMA((n_sub + group + n_z,)),
            ],
            compiler_params=pltpu.CompilerParams(
                collective_id=0, has_side_effects=True, vmem_limit_bytes=56 * 2**20
            ),
        )(level_set.reshape(8, 64, TILES_DEV), velocity.reshape(3, 8, 64, TILES_DEV), neighbours)
        return advected.reshape(8, 8, 8, TILES_DEV), reinitialized.reshape(8, 8, 8, TILES_DEV)

    return jax.shard_map(
        local,
        mesh=mesh,
        in_specs=(
            P(None, None, None, ("band", "sub")),
            P(None, None, None, None, ("band", "sub")),
            P(None, ("band", "sub")),
        ),
        out_specs=(P(None, None, None, ("band", "sub")), P(None, None, None, ("band", "sub"))),
        check_vma=False,
    )
```

```python
import functools

import jax
import jax.numpy as jnp
from jax import lax
from jax.experimental import pallas as pl
from jax.experimental.pallas import tpu as pltpu
from jax.sharding import PartitionSpec as P

TILES_DEV = 512
SLOTS_X = 256
SLOTS_Y = 128
FACE = 192
STAGES = 3
REINIT = 2
STEPS = STAGES + REINIT
EPS = 1e-06
CFL = 0.5
DTAU = 0.3
ROOT_EPS = 1e-06
LANES = 128
GROUPS = TILES_DEV // LANES

F32 = jnp.float32
BF16 = jnp.bfloat16
MESH = pl.DeviceIdType.MESH


def differences(p):
    first = [p[k + 1] - p[k] for k in range(13)]
    second = [first[k + 1] - first[k] for k in range(12)]
    third = [second[k + 1] - second[k] for k in range(11)]
    fourth = [None] + [third[k] - third[k - 1] for k in range(1, 11)]
    square = [e * e for e in second]
    ind_a, ind_b, ind_c = {}, {}, {}
    for k in range(11):
        half = (0.5 * second[k]) * second[k + 1]
        base = third[k] * third[k] * (2.0 / 3.0) + 0.5 * EPS
        low = base - half
        if k <= 8:
            ind_a[k] = low + square[k + 1]
        if 1 <= k <= 9:
            ind_b[k] = base + half
        if k >= 2:
            ind_c[k] = low + square[k]
    return third, fourth, ind_a, ind_b, ind_c


def recip(x):
    return pl.reciprocal(x, approx=True)


def advect_line(p, flow):
    third, fourth, ind_a, ind_b, ind_c = differences(p)
    out = []
    for c in range(8):
        up = flow[c] > 0
        ra = recip(jnp.where(up, ind_a[c], ind_c[c + 3]))
        rb = recip(jnp.where(up, ind_b[c + 1], ind_b[c + 2]))
        rc = recip(jnp.where(up, ind_c[c + 2], ind_a[c + 1]))
        wa = ra * ra
        wb = rb * rb * 6.0
        wc = rc * rc * 3.0
        far = jnp.where(up, fourth[c + 1], fourth[c + 3])
        num = wa * (far + far) + wc * fourth[c + 2]
        corr = num * recip(wa + wb + wc)
        linear = 3.0 * (p[c + 4] - p[c + 2]) - jnp.where(up, third[c + 1], third[c + 2])
        out.append(flow[c] * linear - jnp.abs(flow[c]) * corr)
    return out


def reinit_line(p, sign):
    third, fourth, ind_a, ind_b, ind_c = differences(p)
    wa, wa3, wb, wc, wc3 = {}, {}, {}, {}, {}
    for k, v in ind_a.items():
        r = recip(v)
        wa[k] = r * r
        wa3[k] = wa[k] * 3.0
    for k, v in ind_b.items():
        r = recip(v)
        wb[k] = r * r * 6.0
    for k, v in ind_c.items():
        r = recip(v)
        wc[k] = r * r
        wc3[k] = wc[k] * 3.0
    twice = [None] + [f + f for f in fourth[1:]]
    out = []
    for c in range(8):
        linear = 3.0 * (p[c + 4] - p[c + 2])
        corr_b = (wa[c] * twice[c + 1] + wc3[c + 2] * fourth[c + 2]) * recip(wa[c] + wb[c + 1] + wc3[c + 2])
        corr_f = (wc[c + 3] * twice[c + 3] + wa3[c + 1] * fourth[c + 2]) * recip(wc[c + 3] + wb[c + 2] + wa3[c + 1])
        back = linear - third[c + 1] - corr_b
        fore = third[c + 2] - linear - corr_f
        m = jnp.maximum(jnp.maximum(sign[c] * back, sign[c] * fore), 0.0)
        out.append(m * m)
    return out


def split_rows(value):
    hi = value.astype(BF16)
    lo = (value - hi.astype(F32)).astype(BF16)
    return hi, lo


def kernel(
    n_band, n_sub, group,
    ls_ref, vel_ref, nb_ref, adv_out, out_ref,
    p0, pc, adv, sgn, vel, vz, az, ay, halo_x, halo_y, halo_z, faces_x, faces_y, faces_z,
    local_m, pack_x, pack_y, unpack_x, unpack_y, tri, pres,
    nb_s, ids_s, krow, kcol, send_x, send_y, recv_x, recv_y, ar_send, ar_sub, ar_grp, ar_z, step_s,
    in_sem, out_sem, tx_sem, rx_sem, ar_tx, ar_rx,
):
    band = lax.axis_index("band")
    sub = lax.axis_index("sub")
    n_z = n_band // group
    band_up, band_dn = lax.rem(band + 1, n_band), lax.rem(band + n_band - 1, n_band)
    sub_up, sub_dn = lax.rem(sub + 1, n_sub), lax.rem(sub + n_sub - 1, n_sub)
    first_of_group = band - lax.rem(band, group)

    def sub_peer(d):
        return (band, lax.rem(sub + d, n_sub))

    def group_peer(d):
        return (first_of_group + lax.rem(lax.rem(band, group) + d, group), sub)

    def z_peer(d):
        return (lax.rem(band + d * group, n_band), sub)

    def lanes(g):
        return pl.ds(g * LANES, LANES)

    in_copies = []
    for g in range(GROUPS):
        in_copies.append(pltpu.make_async_copy(ls_ref.at[:, :, lanes(g)], p0.at[g], in_sem.at[g]))
    for k in range(3):
        for g in range(GROUPS):
            in_copies.append(
                pltpu.make_async_copy(vel_ref.at[k, :, :, lanes(g)], vel.at[k, g], in_sem.at[4 + 4 * k + g])
            )
    for copy in in_copies:
        copy.start()

    peers = [(band_up, sub), (band_dn, sub)]
    peers += [sub_peer(d) for d in range(1, n_sub)]
    peers += [group_peer(d) for d in range(1, group)]
    peers += [z_peer(d) for d in range(1, n_z)]
    barrier = pltpu.get_barrier_semaphore()
    for peer in peers:
        pl.semaphore_signal(barrier, inc=1, device_id=peer, device_id_type=MESH)

    nb_s[...] = jnp.full((8, TILES_DEV), -1, jnp.int32)
    nb_s[0:6, :] = nb_ref[...]
    nb = nb_s[...]
    base = (band * n_sub + sub) * TILES_DEV
    present = nb >= 0
    is_local = (nb >= base) & (nb < base + TILES_DEV)
    remote = present & jnp.logical_not(is_local)
    ids_s[0] = jnp.where(is_local, nb - base, -1)
    presf = jnp.where(present, 1.0, 0.0)
    for d in range(6):
        for g in range(GROUPS):
            pres[d, g] = jnp.broadcast_to(presf[d : d + 1, g * LANES : (g + 1) * LANES], (16, LANES))

    def fill(k, carry):
        rows = pl.ds(pl.multiple_of(16 * k, 16), 16)
        iota = lax.broadcasted_iota(jnp.int32, (16, TILES_DEV), 0) + 16 * k
        for d in range(6):
            local_m[d, rows, :] = jnp.where(iota == ids_s[0, d : d + 1, :], 1.0, 0.0).astype(BF16)
        lane = lax.broadcasted_iota(jnp.int32, (16, TILES_DEV), 1)
        tri[rows, :] = jnp.where(iota < lane, 1.0, 0.0).astype(BF16)
        return carry

    lax.fori_loop(0, TILES_DEV // 16, fill, 0)

    flags = jnp.where(remote, 1.0, 0.0)
    flags16 = jnp.concatenate([flags, jnp.zeros_like(flags)], axis=0).astype(BF16)
    place = jnp.dot(flags16, tri[...], preferred_element_type=F32)[0:8]
    keys = jnp.where(remote, nb.astype(F32), 1e9)
    krow[...] = jnp.zeros_like(krow)
    krow[0:4, :] = keys[0:4]
    krow[4:8, :] = jnp.where(remote, place, -1.0)[0:4]
    for c in range(GROUPS):
        kcol[c * LANES : (c + 1) * LANES, :] = krow[:, c * LANES : (c + 1) * LANES].T

    def count(k, carry):
        for j in range(8):
            rows = pl.ds(pl.multiple_of(64 * k + 8 * j, 8), 8)
            carry = tuple(
                total + jnp.where(kcol[rows, d : d + 1] < krow[d : d + 1, :], 1.0, 0.0)
                for d, total in enumerate(carry)
            )
        return carry

    zero = jnp.zeros((8, TILES_DEV), F32)
    counts = lax.fori_loop(0, TILES_DEV // 64, count, (zero,) * 4)
    for d in range(4):
        rank = jnp.sum(counts[d], axis=0, keepdims=True).astype(jnp.int32)
        ids_s[1, d : d + 1, :] = jnp.where(remote[d : d + 1], rank, -1)

    def fill_pack(k, carry):
        lane_x = lax.broadcasted_iota(jnp.int32, (16, SLOTS_X), 1).astype(F32)
        lane_y = lax.broadcasted_iota(jnp.int32, (16, SLOTS_Y), 1).astype(F32)
        for j in range(4):
            rows = pl.ds(pl.multiple_of(64 * k + 16 * j, 16), 16)
            for d in range(2):
                pack_x[d, rows, :] = jnp.where(kcol[rows, 4 + d : 5 + d] == lane_x, 1.0, 0.0).astype(BF16)
                pack_y[d, rows, :] = jnp.where(kcol[rows, 6 + d : 7 + d] == lane_y, 1.0, 0.0).astype(BF16)
        return carry

    lax.fori_loop(0, TILES_DEV // 64, fill_pack, 0)

    def fill_unpack(d, dest):
        def body(k, carry):
            rows = pl.ds(pl.multiple_of(16 * k, 16), 16)
            iota = lax.broadcasted_iota(jnp.int32, (16, TILES_DEV), 0) + 16 * k
            dest[d % 2, rows, :] = jnp.where(iota == ids_s[1, d : d + 1, :], 1.0, 0.0).astype(BF16)
            return carry

        lax.fori_loop(0, dest.shape[1] // 16, body, 0)

    for d in range(4):
        fill_unpack(d, unpack_x if d < 2 else unpack_y)

    for copy in in_copies[:GROUPS]:
        copy.wait()

    def put_face(ref, d, row, g, hi, lo):
        col = pl.ds(pl.multiple_of(g * LANES, LANES), LANES)
        ref[d, pl.ds(row, 16), col] = hi
        ref[d, pl.ds(row + FACE, 16), col] = lo

    def put_faces_xy(g, r, values):
        parts = []
        for x in range(8):
            hi = values[x].astype(BF16)
            rest = values[x] - hi.astype(F32)
            parts.append(rest)
            if x not in (3, 4):
                put_face(faces_x, 0 if x > 4 else 1, 64 * (x - 5 if x > 4 else x) + 16 * r, g, hi, rest.astype(BF16))
        for j in range(2):
            y = 2 * r + j
            if y in (3, 4):
                continue
            for i in range(4):
                hi, lo = [
                    jnp.concatenate([part[2 * i + e][8 * j : 8 * j + 8] for e in range(2)], axis=0).astype(BF16)
                    for part in (values, parts)
                ]
                put_face(faces_y, 0 if y > 4 else 1, 64 * (y - 5 if y > 4 else y) + 16 * i, g, hi, lo)

    def copy_in(g, carry):
        for r in range(4):
            values = [p0[g, x, 16 * r : 16 * r + 16, :] for x in range(8)]
            for x in range(8):
                pc[g, x, 16 * r : 16 * r + 16, :] = values[x]
            put_faces_xy(g, r, values)
        return carry

    lax.fori_loop(0, GROUPS, copy_in, 0)
    for copy in in_copies[GROUPS:]:
        copy.wait()

    def speeds(idx, top):
        g, x = idx // 8, lax.rem(idx, 8)
        for y in range(8):
            rows = slice(8 * y, 8 * y + 8)
            total = jnp.abs(vel[0, g, x, rows, :]) + jnp.abs(vel[1, g, x, rows, :]) + jnp.abs(vel[2, g, x, rows, :])
            top = jnp.maximum(top, total)
        turned = [vel[2, g, x, pl.ds(z, 8, stride=8), :] for z in range(8)]
        for z in range(8):
            vz[g, x, 8 * z : 8 * z + 8, :] = turned[z]
        return top

    top = lax.fori_loop(0, GROUPS * 8, speeds, jnp.zeros((8, LANES), F32))

    pl.semaphore_wait(barrier, len(peers))

    def ar_copies(r):
        peer, slots, n = ((sub_peer, ar_sub, n_sub), (group_peer, ar_grp, group), (z_peer, ar_z, n_z))[r]
        first = (0, n_sub, n_sub + group)[r]
        return [
            pltpu.make_async_remote_copy(
                src_ref=ar_send.at[r],
                dst_ref=slots.at[d - 1],
                send_sem=ar_tx.at[first + d - 1],
                recv_sem=ar_rx.at[first + d - 1],
                device_id=peer(d),
                device_id_type=MESH,
            )
            for d in range(1, n)
        ], slots

    def ar_start(r, value):
        ar_send[r] = value
        for copy in ar_copies(r)[0]:
            copy.start()

    def ar_finish(r):
        value = ar_send[r]
        copies, slots = ar_copies(r)
        for k, copy in enumerate(copies):
            copy.wait()
            value = jnp.maximum(value, slots[k])
        return value

    ar_start(0, top)

    def exchange(t):
        targets = [(band_dn, sub), (band_up, sub), (band, sub_dn), (band, sub_up)]
        copies = []
        for d in range(4):
            src, dst = (send_x, recv_x) if d < 2 else (send_y, recv_y)
            copies.append(
                pltpu.make_async_remote_copy(
                    src_ref=src.at[d % 2],
                    dst_ref=dst.at[t, 1 - d % 2],
                    send_sem=tx_sem.at[d],
                    recv_sem=rx_sem.at[t, d],
                    device_id=targets[d],
                    device_id_type=MESH,
                )
            )
        return copies

    def turned_pair(ref, g, i, k):
        return jnp.concatenate([ref[g, 2 * i + j, pl.ds(k, 8, stride=8), :] for j in range(2)], axis=0)

    def put_faces_z():
        for g in range(GROUPS):
            for i in range(4):
                for d, start in ((0, 5), (1, 0)):
                    for l in range(3):
                        hi, lo = split_rows(turned_pair(pc, g, i, start + l))
                        put_face(faces_z, d, 64 * l + 16 * i, g, hi, lo)

    def two_part_dot(lhs, rhs):
        res = jnp.dot(lhs, rhs, preferred_element_type=F32)
        return res[:FACE] + res[FACE:]

    def gather(faces, d, matrix, halo):
        res = two_part_dot(faces[d], matrix)
        for g in range(GROUPS):
            halo[d, g] = res[:, g * LANES : (g + 1) * LANES]

    def unpack(block, d, matrix, halo):
        hi, lo = split_rows(block)
        res = two_part_dot(jnp.concatenate([hi, lo], axis=0), matrix)
        for g in range(GROUPS):
            halo[d, g] = halo[d, g] + res[:, g * LANES : (g + 1) * LANES]

    def padded(halo, there, g, row, cells):
        there_lo = pres[there, g] > 0
        there_hi = pres[there + 1, g] > 0
        low = [jnp.where(there_lo, halo[0, g, pl.ds(64 * l + row, 16), :], cells[0]) for l in range(3)]
        high = [jnp.where(there_hi, halo[1, g, pl.ds(64 * l + row, 16), :], cells[7]) for l in range(3)]
        return low + cells + high

    def pair(ref, g, i, k):
        return ref[g, 2 * i : 2 * i + 2, 8 * k : 8 * k + 8, :].reshape(16, LANES)

    def z_lines(line, extra, g):
        for i in range(4):
            cells = [turned_pair(pc, g, i, z) for z in range(8)]
            values = line(padded(halo_z, 4, g, 16 * i, cells), [extra(g, i, z) for z in range(8)])
            for z in range(8):
                az[g, 2 * i : 2 * i + 2, 8 * z : 8 * z + 8, :] = values[z].reshape(2, 8, LANES)

    def y_lines(line, extra, g):
        for i in range(4):
            cells = [pair(pc, g, i, y) for y in range(8)]
            values = line(padded(halo_y, 2, g, 16 * i, cells), [extra(g, i, y) for y in range(8)])
            for y in range(8):
                total = values[y] + turned_pair(az, g, i, y)
                ay[g, 2 * i : 2 * i + 2, 8 * y : 8 * y + 8, :] = total.reshape(2, 8, LANES)

    def x_lines(line, extra, finish, g):
        for r in range(4):
            rows = slice(16 * r, 16 * r + 16)
            cells = [pc[g, x, rows, :] for x in range(8)]
            values = line(padded(halo_x, 0, g, 16 * r, cells), [extra(g, x, rows) for x in range(8)])
            fresh = [finish(g, x, rows, cells[x], values[x] + ay[g, x, rows, :]) for x in range(8)]
            put_faces_xy(g, r, fresh)

    def run(t, line, extra_z, extra_y, extra_x, finish, after_z=None, after_y=None):
        copies = exchange(t)
        send_x[0] = two_part_dot(faces_x[1], pack_x[0])
        copies[0].start()
        send_x[1] = two_part_dot(faces_x[0], pack_x[1])
        copies[1].start()
        send_y[0] = two_part_dot(faces_y[1], pack_y[0])
        copies[2].start()
        send_y[1] = two_part_dot(faces_y[0], pack_y[1])
        copies[3].start()
        put_faces_z()
        gather(faces_z, 0, local_m[4], halo_z)
        gather(faces_z, 1, local_m[5], halo_z)

        def z_first(k, carry):
            gather(faces_y, k, local_m[2 + k], halo_y)
            z_lines(line, extra_z, k)
            return carry

        lax.fori_loop(0, 2, z_first, 0)
        copies[2].wait_recv()
        copies[3].wait_recv()

        def z_second(k, carry):
            gather(faces_x, k, local_m[k], halo_x)
            unpack(recv_y[t, k], k, unpack_y[k], halo_y)
            z_lines(line, extra_z, 2 + k)
            return carry

        lax.fori_loop(0, 2, z_second, 0)
        if after_z is not None:
            after_z()

        def y_first(k, carry):
            y_lines(line, extra_y, k)
            return carry

        lax.fori_loop(0, 2, y_first, 0)
        copies[0].wait_recv()
        copies[1].wait_recv()

        def y_second(k, carry):
            unpack(recv_x[t, k], k, unpack_x[k], halo_x)
            y_lines(line, extra_y, 2 + k)
            return carry

        lax.fori_loop(0, 2, y_second, 0)
        if after_y is not None:
            after_y()

        def x_all(k, carry):
            x_lines(line, extra_x, finish, k)
            return carry

        lax.fori_loop(0, GROUPS, x_all, 0)
        for copy in copies:
            copy.wait_send()

    def advect_step(t, carry):
        def after_z():
            @pl.when(t == 0)
            def _():
                ar_start(1, ar_finish(0))

        def after_y():
            @pl.when(t == 0)
            def _():
                ar_start(2, ar_finish(1))
                top = ar_finish(2)
                top = jnp.max(jnp.max(top, axis=1, keepdims=True), axis=0, keepdims=True)
                step_s[...] = jnp.broadcast_to((CFL / 6.0) / top, (16, LANES))

        old = jnp.where(t == 0, 0.0, jnp.where(t == 1, 0.75, 1.0 / 3.0))
        new = jnp.where(t == 0, 1.0, jnp.where(t == 1, 0.25, 2.0 / 3.0))

        def finish(g, x, rows, cell, total):
            value = old * p0[g, x, rows, :] + new * (cell - step_s[...] * total)
            pc[g, x, rows, :] = value
            adv[g, x, rows, :] = value
            sgn[g, x, rows, :] = jnp.where(value > 0, 1.0, -1.0)
            return value

        run(
            t,
            advect_line,
            lambda g, i, z: pair(vz, g, i, z),
            lambda g, i, y: pair(vel.at[1], g, i, y),
            lambda g, x, rows: vel[0, g, x, rows, :],
            finish,
            after_z,
            after_y,
        )
        return carry

    lax.fori_loop(0, STAGES, advect_step, 0)

    adv_copies = [
        pltpu.make_async_copy(adv.at[g], adv_out.at[:, :, lanes(g)], out_sem.at[g]) for g in range(GROUPS)
    ]
    for copy in adv_copies:
        copy.start()

    def reinit_step(k, carry):
        def finish(g, x, rows, cell, total):
            v = adv[g, x, rows, :]
            sign = v * lax.rsqrt(v * v + 1.0)
            root = total * (1.0 / 36.0) + ROOT_EPS
            value = cell + (DTAU * sign) * (1.0 - root * lax.rsqrt(root))
            pc[g, x, rows, :] = value
            return value

        run(
            STAGES + k,
            reinit_line,
            lambda g, i, z: turned_pair(sgn, g, i, z),
            lambda g, i, y: pair(sgn, g, i, y),
            lambda g, x, rows: sgn[g, x, rows, :],
            finish,
        )
        return carry

    lax.fori_loop(0, REINIT, reinit_step, 0)

    out_copies = [
        pltpu.make_async_copy(pc.at[g], out_ref.at[:, :, lanes(g)], out_sem.at[GROUPS + g]) for g in range(GROUPS)
    ]
    for copy in out_copies:
        copy.start()
    for copy in adv_copies + out_copies:
        copy.wait()


def hand_over(a_ref, b_ref, x_ref, y_ref, buf, sem):
    ins, outs = [], []
    for k in range(4):
        part = pl.ds(2 * k, 2)
        for i, (src, dst) in enumerate(((a_ref, x_ref), (b_ref, y_ref))):
            ins.append(pltpu.make_async_copy(src.at[part], buf.at[i, part], sem.at[0, 2 * k + i]))
            outs.append(pltpu.make_async_copy(buf.at[i, part], dst.at[part], sem.at[1, 2 * k + i]))
    for copy in ins:
        copy.start()
    for arrived, onward in zip(ins, outs):
        arrived.wait()
        onward.start()
    for copy in outs:
        copy.wait()


def solution(mesh):
    n_band, n_sub = mesh.shape["band"], mesh.shape["sub"]
    group = min(8, n_band)
    n_z = n_band // group
    cells = (GROUPS, 8, 64, LANES)

    def local(level_set, velocity, neighbours):
        whole = jax.ShapeDtypeStruct((8, 64, TILES_DEV), F32)
        anywhere = pl.BlockSpec(memory_space=pl.ANY)
        advected, reinitialized = pl.pallas_call(
            functools.partial(kernel, n_band, n_sub, group),
            out_shape=(whole, whole),
            in_specs=[anywhere, anywhere, pl.BlockSpec(memory_space=pltpu.VMEM)],
            out_specs=(anywhere, anywhere),
            scratch_shapes=[
                pltpu.VMEM(cells, F32),
                pltpu.VMEM(cells, F32),
                pltpu.VMEM(cells, F32),
                pltpu.VMEM(cells, F32),
                pltpu.VMEM((3,) + cells, F32),
                pltpu.VMEM(cells, F32),
                pltpu.VMEM(cells, F32),
                pltpu.VMEM(cells, F32),
                pltpu.VMEM((2, GROUPS, FACE, LANES), F32),
                pltpu.VMEM((2, GROUPS, FACE, LANES), F32),
                pltpu.VMEM((2, GROUPS, FACE, LANES), F32),
                pltpu.VMEM((2, 2 * FACE, TILES_DEV), BF16),
                pltpu.VMEM((2, 2 * FACE, TILES_DEV), BF16),
                pltpu.VMEM((2, 2 * FACE, TILES_DEV), BF16),
                pltpu.VMEM((6, TILES_DEV, TILES_DEV), BF16),
                pltpu.VMEM((2, TILES_DEV, SLOTS_X), BF16),
                pltpu.VMEM((2, TILES_DEV, SLOTS_Y), BF16),
                pltpu.VMEM((2, SLOTS_X, TILES_DEV), BF16),
                pltpu.VMEM((2, SLOTS_Y, TILES_DEV), BF16),
                pltpu.VMEM((TILES_DEV, TILES_DEV), BF16),
                pltpu.VMEM((6, GROUPS, 16, LANES), F32),
                pltpu.VMEM((8, TILES_DEV), jnp.int32),
                pltpu.VMEM((2, 8, TILES_DEV), jnp.int32),
                pltpu.VMEM((LANES, TILES_DEV), F32),
                pltpu.VMEM((TILES_DEV, LANES), F32),
                pltpu.VMEM((2, FACE, SLOTS_X), F32),
                pltpu.VMEM((2, FACE, SLOTS_Y), F32),
                pltpu.VMEM((STEPS, 2, FACE, SLOTS_X), F32),
                pltpu.VMEM((STEPS, 2, FACE, SLOTS_Y), F32),
                pltpu.VMEM((3, 8, LANES), F32),
                pltpu.VMEM((max(1, n_sub - 1), 8, LANES), F32),
                pltpu.VMEM((max(1, group - 1), 8, LANES), F32),
                pltpu.VMEM((max(1, n_z - 1), 8, LANES), F32),
                pltpu.VMEM((16, LANES), F32),
                pltpu.SemaphoreType.DMA((16,)),
                pltpu.SemaphoreType.DMA((2 * GROUPS,)),
                pltpu.SemaphoreType.DMA((4,)),
                pltpu.SemaphoreType.DMA((STEPS, 4)),
                pltpu.SemaphoreType.DMA((n_sub + group + n_z,)),
                pltpu.SemaphoreType.DMA((n_sub + group + n_z,)),
            ],
            compiler_params=pltpu.CompilerParams(
                collective_id=0, has_side_effects=True, vmem_limit_bytes=56 * 2**20
            ),
        )(level_set.reshape(8, 64, TILES_DEV), velocity.reshape(3, 8, 64, TILES_DEV), neighbours)
        advected, reinitialized = pl.pallas_call(
            hand_over,
            out_shape=(whole, whole),
            in_specs=[anywhere, anywhere],
            out_specs=(anywhere, anywhere),
            scratch_shapes=[pltpu.VMEM((2, 8, 64, TILES_DEV), F32), pltpu.SemaphoreType.DMA((2, 8))],
        )(advected, reinitialized)
        return advected.reshape(8, 8, 8, TILES_DEV), reinitialized.reshape(8, 8, 8, TILES_DEV)

    return jax.shard_map(
        local,
        mesh=mesh,
        in_specs=(
            P(None, None, None, ("band", "sub")),
            P(None, None, None, None, ("band", "sub")),
            P(None, ("band", "sub")),
        ),
        out_specs=(P(None, None, None, ("band", "sub")), P(None, None, None, ("band", "sub"))),
        check_vma=False,
    )
```

```python
import functools

import jax
import jax.numpy as jnp
from jax import lax
from jax.experimental import pallas as pl
from jax.experimental.pallas import tpu as pltpu
from jax.sharding import PartitionSpec as P

TILES_DEV = 512
SLOTS_X = 256
SLOTS_Y = 32
BLOCK = 48
STAGES = 3
REINIT = 2
STEPS = STAGES + REINIT
EPS = 1e-06
CFL = 0.5
DTAU = 0.3
ROOT_EPS = 1e-06
LANES = 128
GROUPS = TILES_DEV // LANES

F32 = jnp.float32
BF16 = jnp.bfloat16
MESH = pl.DeviceIdType.MESH


def differences(p):
    first = [p[k + 1] - p[k] for k in range(13)]
    second = [first[k + 1] - first[k] for k in range(12)]
    third = [second[k + 1] - second[k] for k in range(11)]
    fourth = [None] + [third[k] - third[k - 1] for k in range(1, 11)]
    square = [e * e for e in second]
    ind_a, ind_b, ind_c = {}, {}, {}
    for k in range(11):
        half = (0.5 * second[k]) * second[k + 1]
        base = third[k] * third[k] * (2.0 / 3.0) + 0.5 * EPS
        low = base - half
        if k <= 8:
            ind_a[k] = low + square[k + 1]
        if 1 <= k <= 9:
            ind_b[k] = base + half
        if k >= 2:
            ind_c[k] = low + square[k]
    return third, fourth, ind_a, ind_b, ind_c


def recip(x):
    return pl.reciprocal(x, approx=True)


def advect_line(p, flow):
    third, fourth, ind_a, ind_b, ind_c = differences(p)
    out = []
    for c in range(8):
        up = flow[c] > 0
        ra = recip(jnp.where(up, ind_a[c], ind_c[c + 3]))
        rb = recip(jnp.where(up, ind_b[c + 1], ind_b[c + 2]))
        rc = recip(jnp.where(up, ind_c[c + 2], ind_a[c + 1]))
        wa = ra * ra
        wb = rb * rb * 6.0
        wc = rc * rc * 3.0
        far = jnp.where(up, fourth[c + 1], fourth[c + 3])
        num = wa * (far + far) + wc * fourth[c + 2]
        corr = num * recip(wa + wb + wc)
        linear = 3.0 * (p[c + 4] - p[c + 2]) - jnp.where(up, third[c + 1], third[c + 2])
        out.append(flow[c] * linear - jnp.abs(flow[c]) * corr)
    return out


def reinit_line(p, sign):
    third, fourth, ind_a, ind_b, ind_c = differences(p)
    wa, wa3, wb, wc, wc3 = {}, {}, {}, {}, {}
    for k, v in ind_a.items():
        r = recip(v)
        wa[k] = r * r
        wa3[k] = wa[k] * 3.0
    for k, v in ind_b.items():
        r = recip(v)
        wb[k] = r * r * 6.0
    for k, v in ind_c.items():
        r = recip(v)
        wc[k] = r * r
        wc3[k] = wc[k] * 3.0
    twice = [None] + [f + f for f in fourth[1:]]
    out = []
    for c in range(8):
        linear = 3.0 * (p[c + 4] - p[c + 2])
        corr_b = (wa[c] * twice[c + 1] + wc3[c + 2] * fourth[c + 2]) * recip(wa[c] + wb[c + 1] + wc3[c + 2])
        corr_f = (wc[c + 3] * twice[c + 3] + wa3[c + 1] * fourth[c + 2]) * recip(wc[c + 3] + wb[c + 2] + wa3[c + 1])
        back = linear - third[c + 1] - corr_b
        fore = third[c + 2] - linear - corr_f
        m = jnp.maximum(jnp.maximum(sign[c] * back, sign[c] * fore), 0.0)
        out.append(m * m)
    return out


def split_rows(value):
    hi = value.astype(BF16)
    lo = (value - hi.astype(F32)).astype(BF16)
    return jnp.concatenate([hi, lo], axis=0)


def two_part_dot(lhs, rhs):
    res = jnp.dot(lhs, rhs, preferred_element_type=F32)
    blocks = res.shape[0] // (2 * BLOCK)
    return [
        res[2 * BLOCK * k : 2 * BLOCK * k + BLOCK] + res[2 * BLOCK * k + BLOCK : 2 * BLOCK * (k + 1)]
        for k in range(blocks)
    ]


def kernel(
    n_band, n_sub, low,
    ls_ref, vel_ref, nb_ref, adv_out, out_ref,
    p0, pc, adv, sgn, vel, vz, az, ay,
    local_x, local_y, halo_xa, halo_xb, halo_ya, halo_yb, halo_za, halo_zb, faces_xa, faces_xb, faces_y,
    local_m, pack_x, pack_y, unpack_x, unpack_y, tri, pres,
    nb_s, ids_s, krow, kcol, send_x, send_y, recv_x, recv_y, ar_send, ar_near, ar_far, step_s,
    in_sem, out_sem, tx_x, rx_x, tx_y, rx_y, ar_tx, ar_rx,
):
    band = lax.axis_index("band")
    sub = lax.axis_index("sub")
    n_high = n_band // low
    n_near = low * n_sub
    band_up, band_dn = lax.rem(band + 1, n_band), lax.rem(band + n_band - 1, n_band)
    sub_up, sub_dn = lax.rem(sub + 1, n_sub), lax.rem(sub + n_sub - 1, n_sub)
    band_low = lax.rem(band, low)

    def near_peer(d):
        return (band - band_low + lax.rem(band_low + d // n_sub, low), lax.rem(sub + d % n_sub, n_sub))

    def far_peer(d):
        return (lax.rem(band + d * low, n_band), sub)

    def lanes(g):
        return pl.ds(g * LANES, LANES)

    in_copies = []
    for k in range(3):
        for g in range(GROUPS):
            in_copies.append(
                pltpu.make_async_copy(vel_ref.at[k, :, :, lanes(g)], vel.at[k, g], in_sem.at[4 * k + g])
            )
    for g in range(GROUPS):
        in_copies.append(pltpu.make_async_copy(ls_ref.at[:, :, lanes(g)], p0.at[g], in_sem.at[12 + g]))
    for copy in in_copies:
        copy.start()

    peers = [(band_up, sub), (band_dn, sub)]
    peers += [near_peer(d) for d in range(1, n_near)]
    peers += [far_peer(d) for d in range(1, n_high)]
    barrier = pltpu.get_barrier_semaphore()
    for peer in peers:
        pl.semaphore_signal(barrier, inc=1, device_id=peer, device_id_type=MESH)

    nb_s[...] = jnp.full((8, TILES_DEV), -1, jnp.int32)
    nb_s[0:6, :] = nb_ref[...]
    nb = nb_s[...]
    base = (band * n_sub + sub) * TILES_DEV
    present = nb >= 0
    is_local = (nb >= base) & (nb < base + TILES_DEV)
    remote = present & jnp.logical_not(is_local)
    ids_s[0] = jnp.where(is_local, nb - base, -1)
    presf = jnp.where(present, 1.0, 0.0)
    for d in range(6):
        for g in range(GROUPS):
            pres[d, g] = jnp.broadcast_to(presf[d : d + 1, g * LANES : (g + 1) * LANES], (16, LANES))

    def fill_tri(k, carry):
        rows = pl.ds(pl.multiple_of(16 * k, 16), 16)
        iota = lax.broadcasted_iota(jnp.int32, (16, TILES_DEV), 0) + 16 * k
        lane = lax.broadcasted_iota(jnp.int32, (16, TILES_DEV), 1)
        tri[rows, :] = jnp.where(iota < lane, 1.0, 0.0).astype(BF16)
        return carry

    lax.fori_loop(0, TILES_DEV // 16, fill_tri, 0)
    flags = jnp.where(remote, 1.0, 0.0)
    flags16 = jnp.concatenate([flags, jnp.zeros_like(flags)], axis=0).astype(BF16)
    place = jnp.dot(flags16, tri[...], preferred_element_type=F32)[0:8]
    keys = jnp.where(remote, nb.astype(F32), 1e9)
    krow[...] = jnp.zeros_like(krow)
    krow[0:4, :] = keys[0:4]
    krow[4:8, :] = jnp.where(remote, place, -1.0)[0:4]
    for c in range(GROUPS):
        kcol[c * LANES : (c + 1) * LANES, :] = krow[:, c * LANES : (c + 1) * LANES].T

    for copy in in_copies[: 3 * GROUPS]:
        copy.wait()

    def speeds(idx, top):
        g, x = idx // 8, lax.rem(idx, 8)
        for y in range(8):
            rows = slice(8 * y, 8 * y + 8)
            total = jnp.abs(vel[0, g, x, rows, :]) + jnp.abs(vel[1, g, x, rows, :]) + jnp.abs(vel[2, g, x, rows, :])
            top = jnp.maximum(top, total)
        for z in range(8):
            vz[g, x, 8 * z : 8 * z + 8, :] = vel[2, g, x, pl.ds(z, 8, stride=8), :]
        return top

    top = lax.fori_loop(0, GROUPS * 8, speeds, jnp.zeros((8, LANES), F32))

    pl.semaphore_wait(barrier, len(peers))

    def ar_copies(r):
        peer, slots, n = ((near_peer, ar_near, n_near), (far_peer, ar_far, n_high))[r]
        first = (0, n_near)[r]
        return [
            pltpu.make_async_remote_copy(
                src_ref=ar_send.at[r],
                dst_ref=slots.at[d - 1],
                send_sem=ar_tx.at[first + d - 1],
                recv_sem=ar_rx.at[first + d - 1],
                device_id=peer(d),
                device_id_type=MESH,
            )
            for d in range(1, n)
        ], slots

    def ar_start(r, value):
        ar_send[r] = value
        for copy in ar_copies(r)[0]:
            copy.start()

    def ar_finish(r):
        value = ar_send[r]
        copies, slots = ar_copies(r)
        for k, copy in enumerate(copies):
            copy.wait()
            value = jnp.maximum(value, slots[k])
        return value

    ar_start(0, top)

    def copy_x(t, d, r):
        return pltpu.make_async_remote_copy(
            src_ref=send_x.at[d, r],
            dst_ref=recv_x.at[t, 1 - d, r],
            send_sem=tx_x.at[d, r],
            recv_sem=rx_x.at[t, d, r],
            device_id=((band_dn, sub), (band_up, sub))[d],
            device_id_type=MESH,
        )

    def copy_y(t, d):
        return pltpu.make_async_remote_copy(
            src_ref=send_y.at[d],
            dst_ref=recv_y.at[t, 1 - d],
            send_sem=tx_y.at[d],
            recv_sem=rx_y.at[t, d],
            device_id=((band, sub_dn), (band, sub_up))[d],
            device_id_type=MESH,
        )

    def fill_pack(k, carry):
        lane_x = lax.broadcasted_iota(jnp.int32, (16, SLOTS_X), 1).astype(F32)
        lane_y = lax.broadcasted_iota(jnp.int32, (16, LANES), 1).astype(F32)
        for j in range(4):
            rows = pl.ds(pl.multiple_of(64 * k + 16 * j, 16), 16)
            for d in range(2):
                pack_x[d, rows, :] = jnp.where(kcol[rows, 4 + d : 5 + d] == lane_x, 1.0, 0.0).astype(BF16)
                pack_y[d, rows, :] = jnp.where(kcol[rows, 6 + d : 7 + d] == lane_y, 1.0, 0.0).astype(BF16)
        return carry

    lax.fori_loop(0, TILES_DEV // 64, fill_pack, 0)

    def put_face(ref, lead, l, col, hi, lo):
        ref[(*lead, pl.ds(16 * l, 16), col)] = hi
        ref[(*lead, pl.ds(BLOCK + 16 * l, 16), col)] = lo

    def put_faces_xy(g, q, odd, values):
        col = pl.ds(g * LANES, LANES)
        parts = []
        for x in range(8):
            hi = values[x].astype(BF16)
            rest = values[x] - hi.astype(F32)
            parts.append(rest)
            if x not in (3, 4):
                put_face(faces_xb if odd else faces_xa, (0 if x > 4 else 1, q), x - 5 if x > 4 else x, col, hi, rest.astype(BF16))
        for j in range(2):
            for i in range(4):
                hi, lo = [
                    jnp.concatenate([part[2 * i + e][8 * j : 8 * j + 8] for e in range(2)], axis=0).astype(BF16)
                    for part in (values, parts)
                ]
                row = 2 * odd + j
                faces_y[q, i, pl.ds(16 * row, 16), col] = hi
                faces_y[q, i, pl.ds(64 + 16 * row, 16), col] = lo

    def pack_block_x(ref, q, r):
        for d in range(2):
            send_x[d, r] = two_part_dot(ref[1 - d, q], pack_x[d])[0]

    def copy_in(q, carry):
        for odd in range(2):
            for g in range(GROUPS):
                rows = pl.ds(pl.multiple_of(32 * q + 16 * odd, 16), 16)
                values = [p0[g, x, rows, :] for x in range(8)]
                for x in range(8):
                    pc[g, x, rows, :] = values[x]
                put_faces_xy(g, q, odd, values)
            pack_block_x(faces_xb if odd else faces_xa, q, 2 * q + odd)
            for d in range(2):
                copy_x(0, d, 2 * q + odd).start()
        return carry

    for copy in in_copies[3 * GROUPS :]:
        copy.wait()
    lax.fori_loop(0, 2, copy_in, 0)

    def fill(k, carry):
        for j in range(2):
            rows = pl.ds(pl.multiple_of(32 * k + 16 * j, 16), 16)
            iota = lax.broadcasted_iota(jnp.int32, (16, TILES_DEV), 0) + (32 * k + 16 * j)
            for d in range(6):
                local_m[d, rows, :] = jnp.where(iota == ids_s[0, d : d + 1, :], 1.0, 0.0).astype(BF16)
        return carry

    lax.fori_loop(0, TILES_DEV // 32, fill, 0)

    def count(k, carry):
        for j in range(8):
            rows = pl.ds(pl.multiple_of(64 * k + 8 * j, 8), 8)
            carry = tuple(
                total + jnp.where(kcol[rows, d : d + 1] < krow[d : d + 1, :], 1.0, 0.0)
                for d, total in enumerate(carry)
            )
        return carry

    zero = jnp.zeros((8, TILES_DEV), F32)
    counts = lax.fori_loop(0, TILES_DEV // 64, count, (zero,) * 4)
    for d in range(4):
        rank = jnp.sum(counts[d], axis=0, keepdims=True).astype(jnp.int32)
        ids_s[1, d : d + 1, :] = jnp.where(remote[d : d + 1], rank, -1)

    def fill_unpack(dest, first):
        def body(k, carry):
            for j in range(2):
                rows = pl.ds(pl.multiple_of(32 * k + 16 * j, 16), 16)
                iota = lax.broadcasted_iota(jnp.int32, (16, TILES_DEV), 0) + (32 * k + 16 * j)
                for d in range(2):
                    dest[d, rows, :] = jnp.where(iota == ids_s[1, first + d : first + d + 1, :], 1.0, 0.0).astype(BF16)
            return carry

        lax.fori_loop(0, dest.shape[1] // 32, body, 0)

    fill_unpack(unpack_x, 0)
    fill_unpack(unpack_y, 2)

    def turned_pair(ref, g, i, k):
        return jnp.concatenate([ref[g, 2 * i + j, pl.ds(k, 8, stride=8), :] for j in range(2)], axis=0)

    def pair(ref, g, i, k):
        return ref[g, pl.ds(2 * i, 2), 8 * k : 8 * k + 8, :].reshape(16, LANES)

    def face_y(d, i):
        first = 16 * (1 - d)
        return jnp.concatenate(
            [faces_y[1 - d, i, pl.ds(pl.multiple_of(64 * part + first, 16), BLOCK), :] for part in range(2)], axis=0
        )

    def put_halo(halo, d, res, local):
        for g in range(GROUPS):
            part = res[:, g * LANES : (g + 1) * LANES]
            halo[d, g] = part if local is None else part + local[g]

    def prepare_z(i, halo):
        for d, start in ((0, 5), (1, 0)):
            value = jnp.concatenate(
                [
                    jnp.concatenate([turned_pair(pc, g, i, start + l) for g in range(GROUPS)], axis=1)
                    for l in range(3)
                ],
                axis=0,
            )
            put_halo(halo, d, two_part_dot(split_rows(value), local_m[4 + d])[0], None)

    def prepare_y(t, i, halo):
        for d in range(2):
            block = pltpu.roll(recv_y[t, d], lax.rem((4 - i) * SLOTS_Y, LANES), 1)
            res = two_part_dot(split_rows(block), unpack_y[d])[0]
            put_halo(halo, d, res, [local_y[d, g, i] for g in range(GROUPS)])

    def prepare_x(t, r, q, odd, halo):
        for d in range(2):
            res = two_part_dot(split_rows(recv_x[t, d, r]), unpack_x[d])[0]
            put_halo(halo, d, res, [local_x[d, g, odd, q] for g in range(GROUPS)])

    def gather_y(d):
        faces = jnp.concatenate([face_y(d, i) for i in range(4)], axis=0)
        for i, res in enumerate(two_part_dot(faces, local_m[2 + d])):
            for g in range(GROUPS):
                local_y[d, g, i] = res[:, g * LANES : (g + 1) * LANES]

    def gather_x(d):
        faces = jnp.concatenate([ref[d, q] for ref in (faces_xa, faces_xb) for q in range(2)], axis=0)
        for k, res in enumerate(two_part_dot(faces, local_m[d])):
            for g in range(GROUPS):
                local_x[d, g, k // 2, k % 2] = res[:, g * LANES : (g + 1) * LANES]

    def padded(halo, there, g, cells):
        there_lo = pres[there, g] > 0
        there_hi = pres[there + 1, g] > 0
        before = [jnp.where(there_lo, halo[0, g, 16 * l : 16 * l + 16, :], cells[0]) for l in range(3)]
        after = [jnp.where(there_hi, halo[1, g, 16 * l : 16 * l + 16, :], cells[7]) for l in range(3)]
        return before + cells + after

    def z_lines(line, extra, i, halo):
        for g in range(GROUPS):
            cells = [turned_pair(pc, g, i, z) for z in range(8)]
            values = line(padded(halo, 4, g, cells), [extra(g, i, z) for z in range(8)])
            for z in range(8):
                az[g, pl.ds(2 * i, 2), 8 * z : 8 * z + 8, :] = values[z].reshape(2, 8, LANES)

    def y_lines(line, extra, i, halo):
        for g in range(GROUPS):
            cells = [pair(pc, g, i, y) for y in range(8)]
            values = line(padded(halo, 2, g, cells), [extra(g, i, y) for y in range(8)])
            for y in range(8):
                total = values[y] + turned_pair(az, g, i, y)
                ay[g, pl.ds(2 * i, 2), 8 * y : 8 * y + 8, :] = total.reshape(2, 8, LANES)

    def x_lines(line, extra, finish, q, odd, halo):
        rows = pl.ds(pl.multiple_of(32 * q + 16 * odd, 16), 16)
        ahead = [pc[0, x, rows, :] for x in range(8)]
        for g in range(GROUPS):
            cells = ahead
            if g + 1 < GROUPS:
                ahead = [pc[g + 1, x, rows, :] for x in range(8)]
            values = line(padded(halo, 0, g, cells), [extra(g, x, rows) for x in range(8)])
            fresh = [finish(g, x, rows, cells[x], values[x] + ay[g, x, rows, :]) for x in range(8)]
            put_faces_xy(g, q, odd, fresh)

    def run(t, line, extra_z, extra_y, extra_x, finish, after_z=None, after_y=None):
        for d in range(2):
            parts = [two_part_dot(face_y(1 - d, i), pack_y[d])[0] for i in range(4)]
            send_y[d] = sum(pltpu.roll(parts[i], i * SLOTS_Y, 1) if i else parts[i] for i in range(4))
            copy_y(t, d).start()
        prepare_z(0, halo_za)

        def z_body(q, carry):
            prepare_z(2 * q + 1, halo_zb)
            gather_y(q)
            z_lines(line, extra_z, 2 * q, halo_za)
            prepare_z(lax.rem(2 * q + 2, 4), halo_za)
            z_lines(line, extra_z, 2 * q + 1, halo_zb)
            return carry

        lax.fori_loop(0, 2, z_body, 0)
        if after_z is not None:
            after_z()
        for d in range(2):
            copy_y(t, d).wait()
        prepare_y(t, 0, halo_ya)

        def y_body(q, carry):
            prepare_y(t, 2 * q + 1, halo_yb)
            gather_x(q)
            y_lines(line, extra_y, 2 * q, halo_ya)
            prepare_y(t, lax.rem(2 * q + 2, 4), halo_ya)
            y_lines(line, extra_y, 2 * q + 1, halo_yb)
            return carry

        lax.fori_loop(0, 2, y_body, 0)
        if after_y is not None:
            after_y()

        def wait_x(r):
            for d in range(2):
                copy_x(t, d, r).wait_recv()

        for r in range(4):
            for d in range(2):
                copy_x(t, d, r).wait_send()
        wait_x(0)
        prepare_x(t, 0, 0, 0, halo_xa)

        def x_body(q, carry):
            wait_x(2 * q + 1)
            prepare_x(t, 2 * q + 1, q, 1, halo_xb)
            pack_block_x(faces_xb, lax.rem(q + 1, 2), lax.rem(2 * q + 3, 4))
            x_lines(line, extra_x, finish, q, 0, halo_xa)

            @pl.when((q > 0) & (t + 1 < STEPS))
            def _():
                for d in range(2):
                    copy_x(t + 1, d, 1).start()

            @pl.when(q == 0)
            def _():
                wait_x(2)

            prepare_x(t, lax.rem(2 * q + 2, 4), lax.rem(q + 1, 2), 0, halo_xa)
            pack_block_x(faces_xa, q, 2 * q)
            x_lines(line, extra_x, finish, q, 1, halo_xb)

            @pl.when(t + 1 < STEPS)
            def _():
                for d in range(2):
                    copy_x(t + 1, d, 2 * q).start()

            return carry

        lax.fori_loop(0, 2, x_body, 0)
        pack_block_x(faces_xb, 1, 3)

        @pl.when(t + 1 < STEPS)
        def _():
            for d in range(2):
                copy_x(t + 1, d, 3).start()

    def advect_step(t, carry):
        def after_z():
            @pl.when(t == 0)
            def _():
                ar_start(1, ar_finish(0))

        def after_y():
            @pl.when(t == 0)
            def _():
                top = ar_finish(1)
                top = jnp.max(jnp.max(top, axis=1, keepdims=True), axis=0, keepdims=True)
                step_s[...] = jnp.broadcast_to((CFL / 6.0) / top, (16, LANES))

        old = jnp.where(t == 0, 0.0, jnp.where(t == 1, 0.75, 1.0 / 3.0))
        new = jnp.where(t == 0, 1.0, jnp.where(t == 1, 0.25, 2.0 / 3.0))

        def finish(g, x, rows, cell, total):
            value = old * p0[g, x, rows, :] + new * (cell - step_s[...] * total)
            pc[g, x, rows, :] = value
            adv[g, x, rows, :] = value
            sgn[g, x, rows, :] = jnp.where(value > 0, 1.0, -1.0)
            return value

        run(
            t,
            advect_line,
            lambda g, i, z: pair(vz, g, i, z),
            lambda g, i, y: pair(vel.at[1], g, i, y),
            lambda g, x, rows: vel[0, g, x, rows, :],
            finish,
            after_z,
            after_y,
        )
        return carry

    lax.fori_loop(0, STAGES, advect_step, 0)

    adv_copies = [
        pltpu.make_async_copy(adv.at[g], adv_out.at[:, :, lanes(g)], out_sem.at[g]) for g in range(GROUPS)
    ]
    for copy in adv_copies:
        copy.start()

    def reinit_step(k, carry):
        def finish(g, x, rows, cell, total):
            v = adv[g, x, rows, :]
            sign = v * lax.rsqrt(v * v + 1.0)
            root = total * (1.0 / 36.0) + ROOT_EPS
            value = cell + (DTAU * sign) * (1.0 - root * lax.rsqrt(root))
            pc[g, x, rows, :] = value
            return value

        run(
            STAGES + k,
            reinit_line,
            lambda g, i, z: turned_pair(sgn, g, i, z),
            lambda g, i, y: pair(sgn, g, i, y),
            lambda g, x, rows: sgn[g, x, rows, :],
            finish,
        )
        return carry

    lax.fori_loop(0, REINIT, reinit_step, 0)

    out_copies = [
        pltpu.make_async_copy(pc.at[g], out_ref.at[:, :, lanes(g)], out_sem.at[GROUPS + g]) for g in range(GROUPS)
    ]
    for copy in out_copies:
        copy.start()
    for copy in adv_copies + out_copies:
        copy.wait()


def hand_over(a_ref, b_ref, x_ref, y_ref, buf, sem):
    ins, outs = [], []
    for k in range(4):
        part = pl.ds(2 * k, 2)
        for i, (src, dst) in enumerate(((a_ref, x_ref), (b_ref, y_ref))):
            ins.append(pltpu.make_async_copy(src.at[part], buf.at[i, part], sem.at[0, 2 * k + i]))
            outs.append(pltpu.make_async_copy(buf.at[i, part], dst.at[part], sem.at[1, 2 * k + i]))
    for copy in ins:
        copy.start()
    for arrived, onward in zip(ins, outs):
        arrived.wait()
        onward.start()
    for copy in outs:
        copy.wait()


def solution(mesh):
    n_band, n_sub = mesh.shape["band"], mesh.shape["sub"]
    low = min(4, n_band)
    cells = (GROUPS, 8, 64, LANES)

    def local(level_set, velocity, neighbours):
        whole = jax.ShapeDtypeStruct((8, 64, TILES_DEV), F32)
        anywhere = pl.BlockSpec(memory_space=pl.ANY)
        advected, reinitialized = pl.pallas_call(
            functools.partial(kernel, n_band, n_sub, low),
            out_shape=(whole, whole),
            in_specs=[anywhere, anywhere, pl.BlockSpec(memory_space=pltpu.VMEM)],
            out_specs=(anywhere, anywhere),
            scratch_shapes=[
                pltpu.VMEM(cells, F32),
                pltpu.VMEM(cells, F32),
                pltpu.VMEM(cells, F32),
                pltpu.VMEM(cells, F32),
                pltpu.VMEM((3,) + cells, F32),
                pltpu.VMEM(cells, F32),
                pltpu.VMEM(cells, F32),
                pltpu.VMEM(cells, F32),
                pltpu.VMEM((2, GROUPS, 2, 2, BLOCK, LANES), F32),
                pltpu.VMEM((2, GROUPS, 4, BLOCK, LANES), F32),
                *[pltpu.VMEM((2, GROUPS, BLOCK, LANES), F32)] * 6,
                *[pltpu.VMEM((2, 2, 2 * BLOCK, TILES_DEV), BF16)] * 2,
                pltpu.VMEM((2, 4, 128, TILES_DEV), BF16),
                pltpu.VMEM((6, TILES_DEV, TILES_DEV), BF16),
                pltpu.VMEM((2, TILES_DEV, SLOTS_X), BF16),
                pltpu.VMEM((2, TILES_DEV, LANES), BF16),
                pltpu.VMEM((2, SLOTS_X, TILES_DEV), BF16),
                pltpu.VMEM((2, LANES, TILES_DEV), BF16),
                pltpu.VMEM((TILES_DEV, TILES_DEV), BF16),
                pltpu.VMEM((6, GROUPS, 16, LANES), F32),
                pltpu.VMEM((8, TILES_DEV), jnp.int32),
                pltpu.VMEM((2, 8, TILES_DEV), jnp.int32),
                pltpu.VMEM((LANES, TILES_DEV), F32),
                pltpu.VMEM((TILES_DEV, LANES), F32),
                pltpu.VMEM((2, 4, BLOCK, SLOTS_X), F32),
                pltpu.VMEM((2, BLOCK, LANES), F32),
                pltpu.VMEM((STEPS, 2, 4, BLOCK, SLOTS_X), F32),
                pltpu.VMEM((STEPS, 2, BLOCK, LANES), F32),
                pltpu.VMEM((2, 8, LANES), F32),
                pltpu.VMEM((max(1, low * n_sub - 1), 8, LANES), F32),
                pltpu.VMEM((max(1, n_band // low - 1), 8, LANES), F32),
                pltpu.VMEM((16, LANES), F32),
                pltpu.SemaphoreType.DMA((16,)),
                pltpu.SemaphoreType.DMA((2 * GROUPS,)),
                pltpu.SemaphoreType.DMA((2, 4)),
                pltpu.SemaphoreType.DMA((STEPS, 2, 4)),
                pltpu.SemaphoreType.DMA((2,)),
                pltpu.SemaphoreType.DMA((STEPS, 2)),
                pltpu.SemaphoreType.DMA((low * n_sub + n_band // low,)),
                pltpu.SemaphoreType.DMA((low * n_sub + n_band // low,)),
            ],
            compiler_params=pltpu.CompilerParams(
                collective_id=0, has_side_effects=True, vmem_limit_bytes=56 * 2**20
            ),
        )(level_set.reshape(8, 64, TILES_DEV), velocity.reshape(3, 8, 64, TILES_DEV), neighbours)
        advected, reinitialized = pl.pallas_call(
            hand_over,
            out_shape=(whole, whole),
            in_specs=[anywhere, anywhere],
            out_specs=(anywhere, anywhere),
            scratch_shapes=[pltpu.VMEM((2, 8, 64, TILES_DEV), F32), pltpu.SemaphoreType.DMA((2, 8))],
        )(advected, reinitialized)
        return advected.reshape(8, 8, 8, TILES_DEV), reinitialized.reshape(8, 8, 8, TILES_DEV)

    return jax.shard_map(
        local,
        mesh=mesh,
        in_specs=(
            P(None, None, None, ("band", "sub")),
            P(None, None, None, None, ("band", "sub")),
            P(None, ("band", "sub")),
        ),
        out_specs=(P(None, None, None, ("band", "sub")), P(None, None, None, ("band", "sub"))),
        check_vma=False,
    )
```

```python
import functools

import jax
import jax.numpy as jnp
from jax import lax
from jax.experimental import pallas as pl
from jax.experimental.pallas import tpu as pltpu
from jax.sharding import PartitionSpec as P

TILES_DEV = 512
SLOTS_X = 256
SLOTS_Y = 32
BLOCK = 48
STAGES = 3
REINIT = 2
STEPS = STAGES + REINIT
EPS = 1e-06
CFL = 0.5
DTAU = 0.3
ROOT_EPS = 1e-06
LANES = 128
GROUPS = TILES_DEV // LANES

F32 = jnp.float32
BF16 = jnp.bfloat16
MESH = pl.DeviceIdType.MESH


def differences(p):
    first = [p[k + 1] - p[k] for k in range(13)]
    second = [first[k + 1] - first[k] for k in range(12)]
    third = [second[k + 1] - second[k] for k in range(11)]
    fourth = [None] + [third[k] - third[k - 1] for k in range(1, 11)]
    square = [e * e for e in second]
    ind_a, ind_b, ind_c = {}, {}, {}
    for k in range(11):
        half = (0.5 * second[k]) * second[k + 1]
        base = third[k] * third[k] * (2.0 / 3.0) + 0.5 * EPS
        low = base - half
        if k <= 8:
            ind_a[k] = low + square[k + 1]
        if 1 <= k <= 9:
            ind_b[k] = base + half
        if k >= 2:
            ind_c[k] = low + square[k]
    return third, fourth, ind_a, ind_b, ind_c


def recip(x):
    return pl.reciprocal(x, approx=True)


def advect_line(p, flow):
    third, fourth, ind_a, ind_b, ind_c = differences(p)
    out = []
    for c in range(8):
        up = flow[c] > 0
        ra = recip(jnp.where(up, ind_a[c], ind_c[c + 3]))
        rb = recip(jnp.where(up, ind_b[c + 1], ind_b[c + 2]))
        rc = recip(jnp.where(up, ind_c[c + 2], ind_a[c + 1]))
        wa = ra * ra
        wb = rb * rb * 6.0
        wc = rc * rc * 3.0
        far = jnp.where(up, fourth[c + 1], fourth[c + 3])
        num = wa * (far + far) + wc * fourth[c + 2]
        corr = num * recip(wa + wb + wc)
        linear = 3.0 * (p[c + 4] - p[c + 2]) - jnp.where(up, third[c + 1], third[c + 2])
        out.append(flow[c] * linear - jnp.abs(flow[c]) * corr)
    return out


def reinit_line(p, sign):
    third, fourth, ind_a, ind_b, ind_c = differences(p)
    wa, wa3, wb, wc, wc3 = {}, {}, {}, {}, {}
    for k, v in ind_a.items():
        r = recip(v)
        wa[k] = r * r
        wa3[k] = wa[k] * 3.0
    for k, v in ind_b.items():
        r = recip(v)
        wb[k] = r * r * 6.0
    for k, v in ind_c.items():
        r = recip(v)
        wc[k] = r * r
        wc3[k] = wc[k] * 3.0
    twice = [None] + [f + f for f in fourth[1:]]
    out = []
    for c in range(8):
        linear = 3.0 * (p[c + 4] - p[c + 2])
        corr_b = (wa[c] * twice[c + 1] + wc3[c + 2] * fourth[c + 2]) * recip(wa[c] + wb[c + 1] + wc3[c + 2])
        corr_f = (wc[c + 3] * twice[c + 3] + wa3[c + 1] * fourth[c + 2]) * recip(wc[c + 3] + wb[c + 2] + wa3[c + 1])
        back = linear - third[c + 1] - corr_b
        fore = third[c + 2] - linear - corr_f
        m = jnp.maximum(jnp.maximum(sign[c] * back, sign[c] * fore), 0.0)
        out.append(m * m)
    return out


def split_rows(value):
    hi = value.astype(BF16)
    lo = (value - hi.astype(F32)).astype(BF16)
    return jnp.concatenate([hi, lo], axis=0)


def two_part_dot(lhs, rhs):
    res = jnp.dot(lhs, rhs, preferred_element_type=F32)
    blocks = res.shape[0] // (2 * BLOCK)
    return [
        res[2 * BLOCK * k : 2 * BLOCK * k + BLOCK] + res[2 * BLOCK * k + BLOCK : 2 * BLOCK * (k + 1)]
        for k in range(blocks)
    ]


def kernel(
    n_band, n_sub, low,
    ls_ref, vel_ref, nb_ref, adv_out, out_ref,
    p0, pc, adv, sgn, vel, vz, az, ay,
    halo_xa, halo_xb, halo_ya, halo_yb, halo_za, halo_zb, faces_x, faces_y, faces_z, came_x, came_y,
    local_m, pack_x, pack_y, unpack_x, unpack_y, tri, pres,
    nb_s, ids_s, krow, kcol, send_x, send_y, recv_x, recv_y, ar_send, ar_near, ar_far, step_s,
    in_sem, out_sem, tx_x, rx_x, tx_y, rx_y, ar_tx, ar_rx,
):
    band = lax.axis_index("band")
    sub = lax.axis_index("sub")
    n_high = n_band // low
    n_near = low * n_sub
    band_up, band_dn = lax.rem(band + 1, n_band), lax.rem(band + n_band - 1, n_band)
    sub_up, sub_dn = lax.rem(sub + 1, n_sub), lax.rem(sub + n_sub - 1, n_sub)
    band_low = lax.rem(band, low)

    def near_peer(d):
        return (band - band_low + lax.rem(band_low + d // n_sub, low), lax.rem(sub + d % n_sub, n_sub))

    def far_peer(d):
        return (lax.rem(band + d * low, n_band), sub)

    def lanes(g):
        return pl.ds(g * LANES, LANES)

    in_copies = []
    for k in range(3):
        for g in range(GROUPS):
            in_copies.append(
                pltpu.make_async_copy(vel_ref.at[k, :, :, lanes(g)], vel.at[k, g], in_sem.at[4 * k + g])
            )
    for g in range(GROUPS):
        in_copies.append(pltpu.make_async_copy(ls_ref.at[:, :, lanes(g)], p0.at[g], in_sem.at[12 + g]))
    for copy in in_copies:
        copy.start()

    peers = [(band_up, sub), (band_dn, sub)]
    peers += [near_peer(d) for d in range(1, n_near)]
    peers += [far_peer(d) for d in range(1, n_high)]
    barrier = pltpu.get_barrier_semaphore()
    for peer in peers:
        pl.semaphore_signal(barrier, inc=1, device_id=peer, device_id_type=MESH)

    nb_s[...] = jnp.full((8, TILES_DEV), -1, jnp.int32)
    nb_s[0:6, :] = nb_ref[...]
    nb = nb_s[...]
    base = (band * n_sub + sub) * TILES_DEV
    present = nb >= 0
    is_local = (nb >= base) & (nb < base + TILES_DEV)
    remote = present & jnp.logical_not(is_local)
    ids_s[0] = jnp.where(is_local, nb - base, -1)
    presf = jnp.where(present, 1.0, 0.0)
    for d in range(6):
        for g in range(GROUPS):
            pres[d, g] = jnp.broadcast_to(presf[d : d + 1, g * LANES : (g + 1) * LANES], (16, LANES))

    def fill_tri(k, carry):
        rows = pl.ds(pl.multiple_of(16 * k, 16), 16)
        iota = lax.broadcasted_iota(jnp.int32, (16, TILES_DEV), 0) + 16 * k
        lane = lax.broadcasted_iota(jnp.int32, (16, TILES_DEV), 1)
        tri[rows, :] = jnp.where(iota < lane, 1.0, 0.0).astype(BF16)
        return carry

    lax.fori_loop(0, TILES_DEV // 16, fill_tri, 0)
    flags = jnp.where(remote, 1.0, 0.0)
    flags16 = jnp.concatenate([flags, jnp.zeros_like(flags)], axis=0).astype(BF16)
    place = jnp.dot(flags16, tri[...], preferred_element_type=F32)[0:8]
    keys = jnp.where(remote, nb.astype(F32), 1e9)
    krow[...] = jnp.zeros_like(krow)
    krow[0:4, :] = keys[0:4]
    krow[4:8, :] = jnp.where(remote, place, -1.0)[0:4]
    for c in range(GROUPS):
        kcol[c * LANES : (c + 1) * LANES, :] = krow[:, c * LANES : (c + 1) * LANES].T

    for copy in in_copies[: 3 * GROUPS]:
        copy.wait()

    def speeds(idx, top):
        g, x = idx // 8, lax.rem(idx, 8)
        for y in range(8):
            rows = slice(8 * y, 8 * y + 8)
            total = jnp.abs(vel[0, g, x, rows, :]) + jnp.abs(vel[1, g, x, rows, :]) + jnp.abs(vel[2, g, x, rows, :])
            top = jnp.maximum(top, total)
        for z in range(8):
            vz[g, x, 8 * z : 8 * z + 8, :] = vel[2, g, x, pl.ds(z, 8, stride=8), :]
        return top

    top = lax.fori_loop(0, GROUPS * 8, speeds, jnp.zeros((8, LANES), F32))

    pl.semaphore_wait(barrier, len(peers))

    def ar_copies(r):
        peer, slots, n = ((near_peer, ar_near, n_near), (far_peer, ar_far, n_high))[r]
        first = (0, n_near)[r]
        return [
            pltpu.make_async_remote_copy(
                src_ref=ar_send.at[r],
                dst_ref=slots.at[d - 1],
                send_sem=ar_tx.at[first + d - 1],
                recv_sem=ar_rx.at[first + d - 1],
                device_id=peer(d),
                device_id_type=MESH,
            )
            for d in range(1, n)
        ], slots

    def ar_start(r, value):
        ar_send[r] = value
        for copy in ar_copies(r)[0]:
            copy.start()

    def ar_finish(r):
        value = ar_send[r]
        copies, slots = ar_copies(r)
        for k, copy in enumerate(copies):
            copy.wait()
            value = jnp.maximum(value, slots[k])
        return value

    ar_start(0, top)

    def copy_x(t, d, r):
        return pltpu.make_async_remote_copy(
            src_ref=send_x.at[d, r],
            dst_ref=recv_x.at[t, 1 - d, r],
            send_sem=tx_x.at[d, r],
            recv_sem=rx_x.at[t, d, r],
            device_id=((band_dn, sub), (band_up, sub))[d],
            device_id_type=MESH,
        )

    def copy_y(t, d):
        return pltpu.make_async_remote_copy(
            src_ref=send_y.at[d],
            dst_ref=recv_y.at[t, 1 - d],
            send_sem=tx_y.at[d],
            recv_sem=rx_y.at[t, d],
            device_id=((band, sub_dn), (band, sub_up))[d],
            device_id_type=MESH,
        )

    def fill_pack(k, carry):
        lane_x = lax.broadcasted_iota(jnp.int32, (16, SLOTS_X), 1).astype(F32)
        lane_y = lax.broadcasted_iota(jnp.int32, (16, LANES), 1).astype(F32)
        for j in range(4):
            rows = pl.ds(pl.multiple_of(64 * k + 16 * j, 16), 16)
            for d in range(2):
                pack_x[d, rows, :] = jnp.where(kcol[rows, 4 + d : 5 + d] == lane_x, 1.0, 0.0).astype(BF16)
                pack_y[d, rows, :] = jnp.where(kcol[rows, 6 + d : 7 + d] == lane_y, 1.0, 0.0).astype(BF16)
        return carry

    lax.fori_loop(0, TILES_DEV // 64, fill_pack, 0)

    def put_face(ref, lead, l, col, hi, lo):
        ref[(*lead, pl.ds(pl.multiple_of(16 * l, 16), 16), col)] = hi
        ref[(*lead, pl.ds(pl.multiple_of(BLOCK + 16 * l, 16), 16), col)] = lo

    def outer_block(k):
        return [(pl.multiple_of(48 * k, 16), 16)], ((1 - k, k), (1 - k, k + 1))

    third_block = [(16, 8), (40, 8)], ((1, 2), (0, 0))
    fourth_block = [(24, 16)], ()

    def take(ref, lead, rows):
        pieces = [ref[(*lead, pl.ds(start, size), slice(None))] for start, size in rows]
        return pieces[0] if len(pieces) == 1 else jnp.concatenate(pieces, axis=0)

    def put(ref, lead, rows, value):
        first = 0
        for start, size in rows:
            ref[(*lead, pl.ds(start, size), slice(None))] = value[first : first + size]
            first += size

    def put_faces_xy(g, c, y_faces, values):
        col = pl.ds(g * LANES, LANES)
        parts = []
        for x in range(8):
            hi = values[x].astype(BF16)
            rest = values[x] - hi.astype(F32)
            parts.append(rest)
            if x not in (3, 4):
                put_face(faces_x, (0 if x > 4 else 1, c), x - 5 if x > 4 else x, col, hi, rest.astype(BF16))
        for j, (d, layer) in enumerate(y_faces):
            for i in range(4):
                hi, lo = [
                    jnp.concatenate([part[2 * i + e][8 * j : 8 * j + 8] for e in range(2)], axis=0).astype(BF16)
                    for part in (values, parts)
                ]
                put_face(faces_y, (d, i), layer, col, hi, lo)

    def pack_block_x(c):
        for d in range(2):
            send_x[d, c] = two_part_dot(faces_x[1 - d, c], pack_x[d])[0]

    def pack_y_faces():
        for d in range(2):
            parts = two_part_dot(faces_y[1 - d].reshape(8 * BLOCK, TILES_DEV), pack_y[d])
            send_y[d] = sum(pltpu.roll(parts[i], i * SLOTS_Y, 1) if i else parts[i] for i in range(4))

    def copy_in(c, block):
        rows, y_faces = block
        for g in range(GROUPS):
            values = [take(p0, (g, x), rows) for x in range(8)]
            for x in range(8):
                put(pc, (g, x), rows, values[x])
            put_faces_xy(g, c, y_faces, values)
        pack_block_x(c)
        for d in range(2):
            copy_x(0, d, c).start()

    def copy_in_outer(k, carry):
        copy_in(k, outer_block(k))
        return carry

    for copy in in_copies[3 * GROUPS :]:
        copy.wait()
    lax.fori_loop(0, 2, copy_in_outer, 0)
    copy_in(2, third_block)
    pack_y_faces()
    for d in range(2):
        copy_y(0, d).start()
    copy_in(3, fourth_block)

    def fill(k, carry):
        for j in range(2):
            rows = pl.ds(pl.multiple_of(32 * k + 16 * j, 16), 16)
            iota = lax.broadcasted_iota(jnp.int32, (16, TILES_DEV), 0) + (32 * k + 16 * j)
            for d in range(6):
                local_m[d, rows, :] = jnp.where(iota == ids_s[0, d : d + 1, :], 1.0, 0.0).astype(BF16)
        return carry

    lax.fori_loop(0, TILES_DEV // 32, fill, 0)

    def count(k, carry):
        for j in range(8):
            rows = pl.ds(pl.multiple_of(64 * k + 8 * j, 8), 8)
            carry = tuple(
                total + jnp.where(kcol[rows, d : d + 1] < krow[d : d + 1, :], 1.0, 0.0)
                for d, total in enumerate(carry)
            )
        return carry

    zero = jnp.zeros((8, TILES_DEV), F32)
    counts = lax.fori_loop(0, TILES_DEV // 64, count, (zero,) * 4)
    for d in range(4):
        rank = jnp.sum(counts[d], axis=0, keepdims=True).astype(jnp.int32)
        ids_s[1, d : d + 1, :] = jnp.where(remote[d : d + 1], rank, -1)

    def fill_unpack(dest, first):
        def body(k, carry):
            for j in range(2):
                rows = pl.ds(pl.multiple_of(32 * k + 16 * j, 16), 16)
                iota = lax.broadcasted_iota(jnp.int32, (16, TILES_DEV), 0) + (32 * k + 16 * j)
                for d in range(2):
                    dest[d, rows, :] = jnp.where(iota == ids_s[1, first + d : first + d + 1, :], 1.0, 0.0).astype(BF16)
            return carry

        lax.fori_loop(0, dest.shape[1] // 32, body, 0)

    fill_unpack(unpack_x, 0)
    fill_unpack(unpack_y, 2)

    def turned_pair(ref, g, i, k):
        return jnp.concatenate([ref[g, 2 * i + j, pl.ds(k, 8, stride=8), :] for j in range(2)], axis=0)

    def pair(ref, g, i, k):
        return ref[g, 2 * i : 2 * i + 2, 8 * k : 8 * k + 8, :].reshape(16, LANES)

    def put_faces_z():
        for g in range(GROUPS):
            col = pl.ds(g * LANES, LANES)
            for i in range(4):
                for d, start in ((0, 5), (1, 0)):
                    for l in range(3):
                        value = turned_pair(pc, g, i, start + l)
                        hi = value.astype(BF16)
                        put_face(faces_z, (d, i), l, col, hi, (value - hi.astype(F32)).astype(BF16))

    def group_of(res, g):
        return res[:, g * LANES : (g + 1) * LANES]

    def gather_z(d, half, halo):
        faces = faces_z[d].reshape(8 * BLOCK, TILES_DEV)
        for i, res in enumerate(two_part_dot(faces, local_m[4 + d, :, 2 * half * LANES : 2 * (half + 1) * LANES])):
            for g in range(2):
                halo[d, g, i] = group_of(res, g)

    def gather_y(d):
        for i, res in enumerate(two_part_dot(faces_y[d].reshape(8 * BLOCK, TILES_DEV), local_m[2 + d])):
            for g in range(GROUPS):
                (halo_ya, halo_yb)[g // 2][d, g % 2, i] = group_of(res, g)

    def gather_x(d):
        for r, res in enumerate(two_part_dot(faces_x[d].reshape(8 * BLOCK, TILES_DEV), local_m[d])):
            for g in range(GROUPS):
                (halo_xa, halo_xb)[r // 2][d, r % 2, g] = group_of(res, g)

    def split_y(t):
        for d in range(2):
            parts = split_rows(recv_y[t, d])
            wide = parts.astype(F32)
            for i in range(4):
                block = pltpu.roll(wide, LANES - i * SLOTS_Y, 1).astype(BF16) if i else parts
                came_y[d, 2 * BLOCK * i : 2 * BLOCK * (i + 1), :] = block

    def split_x(t, half):
        for d in range(2):
            for k in range(2):
                came_x[d, half, 2 * BLOCK * k : 2 * BLOCK * (k + 1), :] = split_rows(recv_x[t, d, 2 * half + k])

    def unpack_half_y(d, half, halo):
        matrix = unpack_y[d, :, 2 * half * LANES : 2 * (half + 1) * LANES]
        for i, res in enumerate(two_part_dot(came_y[d], matrix)):
            for g in range(2):
                halo[d, g, i] = halo[d, g, i] + group_of(res, g)

    def unpack_half_x(d, half, halo):
        for k, res in enumerate(two_part_dot(came_x[d, half], unpack_x[d])):
            for g in range(GROUPS):
                halo[d, k, g] = halo[d, k, g] + group_of(res, g)

    def padded(halo, a, b, there, g, cells):
        there_lo = pres[there, g] > 0
        there_hi = pres[there + 1, g] > 0
        before = [jnp.where(there_lo, halo[0, a, b, 16 * l : 16 * l + 16, :], cells[0]) for l in range(3)]
        after = [jnp.where(there_hi, halo[1, a, b, 16 * l : 16 * l + 16, :], cells[7]) for l in range(3)]
        return before + cells + after

    def z_lines(line, extra, half, k, halo):
        g = 2 * half + k
        for i in range(4):
            cells = [turned_pair(pc, g, i, z) for z in range(8)]
            values = line(padded(halo, k, i, 4, g, cells), [extra(g, i, z) for z in range(8)])
            for z in range(8):
                az[g, 2 * i : 2 * i + 2, 8 * z : 8 * z + 8, :] = values[z].reshape(2, 8, LANES)

    def y_lines(line, extra, half, k, halo):
        g = 2 * half + k
        for i in range(4):
            cells = [pair(pc, g, i, y) for y in range(8)]
            values = line(padded(halo, k, i, 2, g, cells), [extra(g, i, y) for y in range(8)])
            for y in range(8):
                total = values[y] + turned_pair(az, g, i, y)
                ay[g, 2 * i : 2 * i + 2, 8 * y : 8 * y + 8, :] = total.reshape(2, 8, LANES)

    def x_lines(line, extra, finish, c, block, halo, k, groups=range(GROUPS)):
        rows, y_faces = block
        ahead = [take(pc, (groups[0], x), rows) for x in range(8)]
        for g in groups:
            cells = ahead
            if g + 1 in groups:
                ahead = [take(pc, (g + 1, x), rows) for x in range(8)]
            values = line(padded(halo, k, g, 0, g, cells), [extra(g, x, rows) for x in range(8)])
            fresh = [finish(g, x, rows, cells[x], values[x] + take(ay, (g, x), rows)) for x in range(8)]
            put_faces_xy(g, c, y_faces, fresh)

    def twice(body):
        def step(k, carry):
            body(k)
            return carry

        lax.fori_loop(0, 2, step, 0)

    def run(t, line, extra_z, extra_y, extra_x, finish, after_z=None, after_y=None):
        put_faces_z()
        gather_z(0, 0, halo_za)
        gather_z(1, 0, halo_za)

        def z_first(k):
            gather_z(k, 1, halo_zb)
            z_lines(line, extra_z, 0, k, halo_za)

        def z_second(k):
            gather_y(k)
            z_lines(line, extra_z, 1, k, halo_zb)

        twice(z_first)
        twice(z_second)
        if after_z is not None:
            after_z()
        for d in range(2):
            copy_y(t, d).wait()
        split_y(t)
        unpack_half_y(0, 0, halo_ya)
        unpack_half_y(1, 0, halo_ya)

        def y_first(k):
            gather_x(k)
            unpack_half_y(k, 1, halo_yb)
            y_lines(line, extra_y, 0, k, halo_ya)

        def y_second(k):
            unpack_half_x(k, 0, halo_xa)
            y_lines(line, extra_y, 1, k, halo_yb)

        twice(y_first)
        for r in range(2):
            for d in range(2):
                copy_x(t, d, r).wait()
        split_x(t, 0)
        twice(y_second)
        if after_y is not None:
            after_y()
        for r in range(2, 4):
            for d in range(2):
                copy_x(t, d, r).wait()

        split_x(t, 1)

        def send_on(copies):
            @pl.when(t + 1 < STEPS)
            def _():
                for copy in copies():
                    copy.start()

        def x_outer(k):
            unpack_half_x(k, 1, halo_xb)
            pack_block_x(lax.rem(k + 3, 4))
            x_lines(line, extra_x, finish, k, outer_block(k), halo_xa, k)

        twice(x_outer)
        send_on(lambda: [copy_x(t + 1, d, 0) for d in range(2)])
        pack_block_x(1)
        x_lines(line, extra_x, finish, 2, third_block, halo_xb, 0)
        send_on(lambda: [copy_x(t + 1, d, 1) for d in range(2)])
        pack_y_faces()
        x_lines(line, extra_x, finish, 3, fourth_block, halo_xb, 1, range(2))
        send_on(lambda: [copy_y(t + 1, d) for d in range(2)])
        pack_block_x(2)
        x_lines(line, extra_x, finish, 3, fourth_block, halo_xb, 1, range(2, 4))
        send_on(lambda: [copy_x(t + 1, d, 2) for d in range(2)])
        pack_block_x(3)
        send_on(lambda: [copy_x(t + 1, d, 3) for d in range(2)])

    def advect_step(t, carry):
        def after_z():
            @pl.when(t == 0)
            def _():
                ar_start(1, ar_finish(0))

        def after_y():
            @pl.when(t == 0)
            def _():
                top = ar_finish(1)
                top = jnp.max(jnp.max(top, axis=1, keepdims=True), axis=0, keepdims=True)
                step_s[...] = jnp.broadcast_to((CFL / 6.0) / top, (16, LANES))

        old = jnp.where(t == 0, 0.0, jnp.where(t == 1, 0.75, 1.0 / 3.0))
        new = jnp.where(t == 0, 1.0, jnp.where(t == 1, 0.25, 2.0 / 3.0))

        def finish(g, x, rows, cell, total):
            value = old * take(p0, (g, x), rows) + new * (cell - step_s[...] * total)
            put(pc, (g, x), rows, value)
            put(adv, (g, x), rows, value)
            put(sgn, (g, x), rows, jnp.where(value > 0, 1.0, -1.0))
            return value

        run(
            t,
            advect_line,
            lambda g, i, z: pair(vz, g, i, z),
            lambda g, i, y: pair(vel.at[1], g, i, y),
            lambda g, x, rows: take(vel, (0, g, x), rows),
            finish,
            after_z,
            after_y,
        )
        return carry

    lax.fori_loop(0, STAGES, advect_step, 0)

    adv_copies = [
        pltpu.make_async_copy(adv.at[g], adv_out.at[:, :, lanes(g)], out_sem.at[g]) for g in range(GROUPS)
    ]
    for copy in adv_copies:
        copy.start()

    def reinit_step(k, carry):
        def finish(g, x, rows, cell, total):
            v = take(adv, (g, x), rows)
            sign = v * lax.rsqrt(v * v + 1.0)
            root = total * (1.0 / 36.0) + ROOT_EPS
            value = cell + (DTAU * sign) * (1.0 - root * lax.rsqrt(root))
            put(pc, (g, x), rows, value)
            return value

        run(
            STAGES + k,
            reinit_line,
            lambda g, i, z: turned_pair(sgn, g, i, z),
            lambda g, i, y: pair(sgn, g, i, y),
            lambda g, x, rows: take(sgn, (g, x), rows),
            finish,
        )
        return carry

    lax.fori_loop(0, REINIT, reinit_step, 0)

    out_copies = [
        pltpu.make_async_copy(pc.at[g], out_ref.at[:, :, lanes(g)], out_sem.at[GROUPS + g]) for g in range(GROUPS)
    ]
    for copy in out_copies:
        copy.start()
    for copy in adv_copies + out_copies:
        copy.wait()


def hand_over(a_ref, b_ref, x_ref, y_ref, buf, sem):
    ins, outs = [], []
    for k in range(4):
        part = pl.ds(2 * k, 2)
        for i, (src, dst) in enumerate(((a_ref, x_ref), (b_ref, y_ref))):
            ins.append(pltpu.make_async_copy(src.at[part], buf.at[i, part], sem.at[0, 2 * k + i]))
            outs.append(pltpu.make_async_copy(buf.at[i, part], dst.at[part], sem.at[1, 2 * k + i]))
    for copy in ins:
        copy.start()
    for arrived, onward in zip(ins, outs):
        arrived.wait()
        onward.start()
    for copy in outs:
        copy.wait()


def solution(mesh):
    n_band, n_sub = mesh.shape["band"], mesh.shape["sub"]
    low = min(4, n_band)
    cells = (GROUPS, 8, 64, LANES)

    def local(level_set, velocity, neighbours):
        whole = jax.ShapeDtypeStruct((8, 64, TILES_DEV), F32)
        anywhere = pl.BlockSpec(memory_space=pl.ANY)
        advected, reinitialized = pl.pallas_call(
            functools.partial(kernel, n_band, n_sub, low),
            out_shape=(whole, whole),
            in_specs=[anywhere, anywhere, pl.BlockSpec(memory_space=pltpu.VMEM)],
            out_specs=(anywhere, anywhere),
            scratch_shapes=[
                pltpu.VMEM(cells, F32),
                pltpu.VMEM(cells, F32),
                pltpu.VMEM(cells, F32),
                pltpu.VMEM(cells, F32),
                pltpu.VMEM((3,) + cells, F32),
                pltpu.VMEM(cells, F32),
                pltpu.VMEM(cells, F32),
                pltpu.VMEM(cells, F32),
                *[pltpu.VMEM((2, 2, GROUPS, BLOCK, LANES), F32)] * 2,
                *[pltpu.VMEM((2, 2, 4, BLOCK, LANES), F32)] * 4,
                pltpu.VMEM((2, 4, 2 * BLOCK, TILES_DEV), BF16),
                pltpu.VMEM((2, 4, 2 * BLOCK, TILES_DEV), BF16),
                pltpu.VMEM((2, 4, 2 * BLOCK, TILES_DEV), BF16),
                pltpu.VMEM((2, 2, 4 * BLOCK, SLOTS_X), BF16),
                pltpu.VMEM((2, 8 * BLOCK, LANES), BF16),
                pltpu.VMEM((6, TILES_DEV, TILES_DEV), BF16),
                pltpu.VMEM((2, TILES_DEV, SLOTS_X), BF16),
                pltpu.VMEM((2, TILES_DEV, LANES), BF16),
                pltpu.VMEM((2, SLOTS_X, TILES_DEV), BF16),
                pltpu.VMEM((2, LANES, TILES_DEV), BF16),
                pltpu.VMEM((TILES_DEV, TILES_DEV), BF16),
                pltpu.VMEM((6, GROUPS, 16, LANES), F32),
                pltpu.VMEM((8, TILES_DEV), jnp.int32),
                pltpu.VMEM((2, 8, TILES_DEV), jnp.int32),
                pltpu.VMEM((LANES, TILES_DEV), F32),
                pltpu.VMEM((TILES_DEV, LANES), F32),
                pltpu.VMEM((2, 4, BLOCK, SLOTS_X), F32),
                pltpu.VMEM((2, BLOCK, LANES), F32),
                pltpu.VMEM((STEPS, 2, 4, BLOCK, SLOTS_X), F32),
                pltpu.VMEM((STEPS, 2, BLOCK, LANES), F32),
                pltpu.VMEM((2, 8, LANES), F32),
                pltpu.VMEM((max(1, low * n_sub - 1), 8, LANES), F32),
                pltpu.VMEM((max(1, n_band // low - 1), 8, LANES), F32),
                pltpu.VMEM((16, LANES), F32),
                pltpu.SemaphoreType.DMA((16,)),
                pltpu.SemaphoreType.DMA((2 * GROUPS,)),
                pltpu.SemaphoreType.DMA((2, 4)),
                pltpu.SemaphoreType.DMA((STEPS, 2, 4)),
                pltpu.SemaphoreType.DMA((2,)),
                pltpu.SemaphoreType.DMA((STEPS, 2)),
                pltpu.SemaphoreType.DMA((low * n_sub + n_band // low,)),
                pltpu.SemaphoreType.DMA((low * n_sub + n_band // low,)),
            ],
            compiler_params=pltpu.CompilerParams(
                collective_id=0, has_side_effects=True, vmem_limit_bytes=56 * 2**20
            ),
        )(level_set.reshape(8, 64, TILES_DEV), velocity.reshape(3, 8, 64, TILES_DEV), neighbours)
        advected, reinitialized = pl.pallas_call(
            hand_over,
            out_shape=(whole, whole),
            in_specs=[anywhere, anywhere],
            out_specs=(anywhere, anywhere),
            scratch_shapes=[pltpu.VMEM((2, 8, 64, TILES_DEV), F32), pltpu.SemaphoreType.DMA((2, 8))],
        )(advected, reinitialized)
        return advected.reshape(8, 8, 8, TILES_DEV), reinitialized.reshape(8, 8, 8, TILES_DEV)

    return jax.shard_map(
        local,
        mesh=mesh,
        in_specs=(
            P(None, None, None, ("band", "sub")),
            P(None, None, None, None, ("band", "sub")),
            P(None, ("band", "sub")),
        ),
        out_specs=(P(None, None, None, ("band", "sub")), P(None, None, None, ("band", "sub"))),
        check_vma=False,
    )
```

```python
import functools

import jax
import jax.numpy as jnp
from jax import lax
from jax.experimental import pallas as pl
from jax.experimental.pallas import tpu as pltpu
from jax.sharding import PartitionSpec as P

TILES_DEV = 512
SLOTS_X = 256
SLOTS_Y = 32
BLOCK = 48
STAGES = 3
REINIT = 2
STEPS = STAGES + REINIT
EPS = 1e-06
CFL = 0.5
DTAU = 0.3
ROOT_EPS = 1e-06
LANES = 128
GROUPS = TILES_DEV // LANES

F32 = jnp.float32
BF16 = jnp.bfloat16
MESH = pl.DeviceIdType.MESH


class Line:
    def __init__(self, cell):
        self.cell, self.made = cell, {}

    def get(self, kind, k):
        if (kind, k) not in self.made:
            self.made[kind, k] = getattr(self, kind)(k)
        return self.made[kind, k]

    def first(self, k):
        return self.get("cell", k + 1) - self.get("cell", k)

    def second(self, k):
        return self.get("first", k + 1) - self.get("first", k)

    def third(self, k):
        return self.get("second", k + 1) - self.get("second", k)

    def fourth(self, k):
        return self.get("third", k) - self.get("third", k - 1)

    def square(self, k):
        return self.get("second", k) * self.get("second", k)

    def half(self, k):
        return (0.5 * self.get("second", k)) * self.get("second", k + 1)

    def base(self, k):
        return self.get("third", k) * self.get("third", k) * (2.0 / 3.0) + 0.5 * EPS

    def low(self, k):
        return self.get("base", k) - self.get("half", k)

    def ind_a(self, k):
        return self.get("low", k) + self.get("square", k + 1)

    def ind_b(self, k):
        return self.get("base", k) + self.get("half", k)

    def ind_c(self, k):
        return self.get("low", k) + self.get("square", k)

    def weight_a(self, k):
        r = recip(self.get("ind_a", k))
        return r * r

    def weight_b(self, k):
        r = recip(self.get("ind_b", k))
        return r * r * 6.0

    def weight_c(self, k):
        r = recip(self.get("ind_c", k))
        return r * r

    def triple_a(self, k):
        return self.get("weight_a", k) * 3.0

    def triple_c(self, k):
        return self.get("weight_c", k) * 3.0

    def twice(self, k):
        return self.get("fourth", k) + self.get("fourth", k)


def recip(x):
    return pl.reciprocal(x, approx=True)


def advect_line(cell, flow_of):
    get = Line(cell).get
    for c in range(8):
        flow = flow_of(c)
        up = flow > 0
        ra = recip(jnp.where(up, get("ind_a", c), get("ind_c", c + 3)))
        rb = recip(jnp.where(up, get("ind_b", c + 1), get("ind_b", c + 2)))
        rc = recip(jnp.where(up, get("ind_c", c + 2), get("ind_a", c + 1)))
        wa = ra * ra
        wb = rb * rb * 6.0
        wc = rc * rc * 3.0
        far = jnp.where(up, get("fourth", c + 1), get("fourth", c + 3))
        num = wa * (far + far) + wc * get("fourth", c + 2)
        corr = num * recip(wa + wb + wc)
        linear = 3.0 * (get("cell", c + 4) - get("cell", c + 2)) - jnp.where(up, get("third", c + 1), get("third", c + 2))
        yield flow * linear - jnp.abs(flow) * corr


def reinit_line(cell, sign_of):
    get = Line(cell).get
    for c in range(8):
        sign = sign_of(c)
        linear = 3.0 * (get("cell", c + 4) - get("cell", c + 2))
        mid = get("fourth", c + 2)
        wa, wb, wc = get("weight_a", c), get("weight_b", c + 1), get("triple_c", c + 2)
        corr_b = (wa * get("twice", c + 1) + wc * mid) * recip(wa + wb + wc)
        wa, wb, wc = get("weight_c", c + 3), get("weight_b", c + 2), get("triple_a", c + 1)
        corr_f = (wa * get("twice", c + 3) + wc * mid) * recip(wa + wb + wc)
        back = linear - get("third", c + 1) - corr_b
        fore = get("third", c + 2) - linear - corr_f
        m = jnp.maximum(jnp.maximum(sign * back, sign * fore), 0.0)
        yield m * m


def split_rows(value):
    hi = value.astype(BF16)
    lo = (value - hi.astype(F32)).astype(BF16)
    return jnp.concatenate([hi, lo], axis=0)


def two_part_dot(lhs, rhs):
    res = jnp.dot(lhs, rhs, preferred_element_type=F32)
    blocks = res.shape[0] // (2 * BLOCK)
    return [
        res[2 * BLOCK * k : 2 * BLOCK * k + BLOCK] + res[2 * BLOCK * k + BLOCK : 2 * BLOCK * (k + 1)]
        for k in range(blocks)
    ]


def kernel(
    n_band, n_sub, low,
    ls_ref, vel_ref, nb_ref, adv_out, out_ref,
    p0, pc, adv, sgn, vel, vz, az, ay,
    halo_xa, halo_xb, halo_ya, halo_yb, halo_za, halo_zb, faces_x, faces_y, faces_z, came_x, came_y,
    local_m, pack_x, pack_y, unpack_x, unpack_y, tri, pres,
    nb_s, ids_s, krow, kcol, send_x, send_y, recv_x, recv_y, ar_send, ar_near, ar_far, step_s,
    in_sem, out_sem, tx_x, rx_x, tx_y, rx_y, ar_tx, ar_rx,
):
    band = lax.axis_index("band")
    sub = lax.axis_index("sub")
    n_high = n_band // low
    n_near = low * n_sub
    band_up, band_dn = lax.rem(band + 1, n_band), lax.rem(band + n_band - 1, n_band)
    sub_up, sub_dn = lax.rem(sub + 1, n_sub), lax.rem(sub + n_sub - 1, n_sub)
    band_low = lax.rem(band, low)

    def near_peer(d):
        return (band - band_low + lax.rem(band_low + d // n_sub, low), lax.rem(sub + d % n_sub, n_sub))

    def far_peer(d):
        return (lax.rem(band + d * low, n_band), sub)

    def lanes(g):
        return pl.ds(g * LANES, LANES)

    in_copies = []
    for g in range(GROUPS):
        in_copies.append(pltpu.make_async_copy(ls_ref.at[:, :, lanes(g)], p0.at[g], in_sem.at[12 + g]))
    for k in range(3):
        for g in range(GROUPS):
            in_copies.append(
                pltpu.make_async_copy(vel_ref.at[k, :, :, lanes(g)], vel.at[k, g], in_sem.at[4 * k + g])
            )
    for copy in in_copies:
        copy.start()

    peers = [(band_up, sub), (band_dn, sub)]
    peers += [near_peer(d) for d in range(1, n_near)]
    peers += [far_peer(d) for d in range(1, n_high)]
    barrier = pltpu.get_barrier_semaphore()
    for peer in peers:
        pl.semaphore_signal(barrier, inc=1, device_id=peer, device_id_type=MESH)

    nb_s[...] = jnp.full((8, TILES_DEV), -1, jnp.int32)
    nb_s[0:6, :] = nb_ref[...]
    nb = nb_s[...]
    base = (band * n_sub + sub) * TILES_DEV
    present = nb >= 0
    is_local = (nb >= base) & (nb < base + TILES_DEV)
    remote = present & jnp.logical_not(is_local)
    ids_s[0] = jnp.where(is_local, nb - base, -1)
    presf = jnp.where(present, 1.0, 0.0)
    for d in range(6):
        for g in range(GROUPS):
            pres[d, g] = jnp.broadcast_to(presf[d : d + 1, g * LANES : (g + 1) * LANES], (16, LANES))

    def fill_tri(k, carry):
        rows = pl.ds(pl.multiple_of(16 * k, 16), 16)
        iota = lax.broadcasted_iota(jnp.int32, (16, TILES_DEV), 0) + 16 * k
        lane = lax.broadcasted_iota(jnp.int32, (16, TILES_DEV), 1)
        tri[rows, :] = jnp.where(iota < lane, 1.0, 0.0).astype(BF16)
        return carry

    lax.fori_loop(0, TILES_DEV // 16, fill_tri, 0)
    flags = jnp.where(remote, 1.0, 0.0)
    flags16 = jnp.concatenate([flags, jnp.zeros_like(flags)], axis=0).astype(BF16)
    place = jnp.dot(flags16, tri[...], preferred_element_type=F32)[0:8]
    keys = jnp.where(remote, nb.astype(F32), 1e9)
    krow[...] = jnp.zeros_like(krow)
    krow[0:4, :] = keys[0:4]
    krow[4:8, :] = jnp.where(remote, place, -1.0)[0:4]
    for c in range(GROUPS):
        kcol[c * LANES : (c + 1) * LANES, :] = krow[:, c * LANES : (c + 1) * LANES].T

    def ar_copies(r):
        peer, slots, n = ((near_peer, ar_near, n_near), (far_peer, ar_far, n_high))[r]
        first = (0, n_near)[r]
        return [
            pltpu.make_async_remote_copy(
                src_ref=ar_send.at[r],
                dst_ref=slots.at[d - 1],
                send_sem=ar_tx.at[first + d - 1],
                recv_sem=ar_rx.at[first + d - 1],
                device_id=peer(d),
                device_id_type=MESH,
            )
            for d in range(1, n)
        ], slots

    def ar_start(r, value):
        ar_send[r] = value
        for copy in ar_copies(r)[0]:
            copy.start()

    def ar_finish(r):
        value = ar_send[r]
        copies, slots = ar_copies(r)
        for k, copy in enumerate(copies):
            copy.wait()
            value = jnp.maximum(value, slots[k])
        return value

    def copy_x(t, d, r):
        return pltpu.make_async_remote_copy(
            src_ref=send_x.at[d, r],
            dst_ref=recv_x.at[t, 1 - d, r],
            send_sem=tx_x.at[d, r],
            recv_sem=rx_x.at[t, d, r],
            device_id=((band_dn, sub), (band_up, sub))[d],
            device_id_type=MESH,
        )

    def copy_y(t, d):
        return pltpu.make_async_remote_copy(
            src_ref=send_y.at[d],
            dst_ref=recv_y.at[t, 1 - d],
            send_sem=tx_y.at[d],
            recv_sem=rx_y.at[t, d],
            device_id=((band, sub_dn), (band, sub_up))[d],
            device_id_type=MESH,
        )

    def fill_pack(k, carry):
        lane_x = lax.broadcasted_iota(jnp.int32, (16, SLOTS_X), 1).astype(F32)
        lane_y = lax.broadcasted_iota(jnp.int32, (16, LANES), 1).astype(F32)
        for j in range(4):
            rows = pl.ds(pl.multiple_of(64 * k + 16 * j, 16), 16)
            for d in range(2):
                pack_x[d, rows, :] = jnp.where(kcol[rows, 4 + d : 5 + d] == lane_x, 1.0, 0.0).astype(BF16)
                pack_y[d, rows, :] = jnp.where(kcol[rows, 6 + d : 7 + d] == lane_y, 1.0, 0.0).astype(BF16)
        return carry

    lax.fori_loop(0, TILES_DEV // 64, fill_pack, 0)

    def put_face(ref, lead, l, col, hi, lo):
        ref[(*lead, pl.ds(pl.multiple_of(16 * l, 16), 16), col)] = hi
        ref[(*lead, pl.ds(pl.multiple_of(BLOCK + 16 * l, 16), 16), col)] = lo

    def outer_block(k):
        return [(pl.multiple_of(48 * k, 16), 16)], ((1 - k, k), (1 - k, k + 1))

    third_block = [(16, 8), (40, 8)], ((1, 2), (0, 0))
    fourth_block = [(24, 16)], ()

    def take(ref, lead, rows):
        pieces = [ref[(*lead, pl.ds(start, size), slice(None))] for start, size in rows]
        return pieces[0] if len(pieces) == 1 else jnp.concatenate(pieces, axis=0)

    def put(ref, lead, rows, value):
        first = 0
        for start, size in rows:
            ref[(*lead, pl.ds(start, size), slice(None))] = value[first : first + size]
            first += size

    def put_faces_xy(g, c, y_faces):
        col = pl.ds(g * LANES, LANES)
        kept = []

        def add(x, value):
            hi = value.astype(BF16)
            rest = value - hi.astype(F32)
            kept.append((value, rest))
            if x not in (3, 4):
                put_face(faces_x, (0 if x > 4 else 1, c), x - 5 if x > 4 else x, col, hi, rest.astype(BF16))
            if x % 2 == 0:
                return
            for j, (d, layer) in enumerate(y_faces):
                hi, lo = [
                    jnp.concatenate([part[8 * j : 8 * j + 8] for part in parts], axis=0).astype(BF16)
                    for parts in zip(*kept[x - 1 : x + 1])
                ]
                put_face(faces_y, (d, x // 2), layer, col, hi, lo)

        return add

    def pack_block_x(c):
        for d in range(2):
            send_x[d, c] = two_part_dot(faces_x[1 - d, c], pack_x[d])[0]

    def pack_y_faces():
        for d in range(2):
            parts = two_part_dot(faces_y[1 - d].reshape(8 * BLOCK, TILES_DEV), pack_y[d])
            send_y[d] = sum(pltpu.roll(parts[i], i * SLOTS_Y, 1) if i else parts[i] for i in range(4))

    def copy_in(c, block):
        rows, y_faces = block
        for g in range(GROUPS):
            faces = put_faces_xy(g, c, y_faces)
            for x in range(8):
                value = take(p0, (g, x), rows)
                put(pc, (g, x), rows, value)
                faces(x, value)
        pack_block_x(c)

    def copy_in_outer(k, carry):
        copy_in(k, outer_block(k))
        return carry

    for copy in in_copies[:GROUPS]:
        copy.wait()
    lax.fori_loop(0, 2, copy_in_outer, 0)
    copy_in(2, third_block)
    pack_y_faces()
    copy_in(3, fourth_block)

    for copy in in_copies[GROUPS:]:
        copy.wait()

    def speeds(idx, top):
        g, x = idx // 8, lax.rem(idx, 8)
        for y in range(8):
            rows = slice(8 * y, 8 * y + 8)
            total = jnp.abs(vel[0, g, x, rows, :]) + jnp.abs(vel[1, g, x, rows, :]) + jnp.abs(vel[2, g, x, rows, :])
            top = jnp.maximum(top, total)
        for z in range(8):
            vz[g, x, 8 * z : 8 * z + 8, :] = vel[2, g, x, pl.ds(z, 8, stride=8), :]
        return top

    top = lax.fori_loop(0, GROUPS * 8, speeds, jnp.zeros((8, LANES), F32))

    pl.semaphore_wait(barrier, len(peers))

    ar_start(0, top)
    for d in range(2):
        copy_y(0, d).start()
    for c in range(4):
        for d in range(2):
            copy_x(0, d, c).start()

    def fill(k, carry):
        for j in range(2):
            rows = pl.ds(pl.multiple_of(32 * k + 16 * j, 16), 16)
            iota = lax.broadcasted_iota(jnp.int32, (16, TILES_DEV), 0) + (32 * k + 16 * j)
            for d in range(6):
                local_m[d, rows, :] = jnp.where(iota == ids_s[0, d : d + 1, :], 1.0, 0.0).astype(BF16)
        return carry

    lax.fori_loop(0, TILES_DEV // 32, fill, 0)

    def count(k, carry):
        for j in range(8):
            rows = pl.ds(pl.multiple_of(64 * k + 8 * j, 8), 8)
            carry = tuple(
                total + jnp.where(kcol[rows, d : d + 1] < krow[d : d + 1, :], 1.0, 0.0)
                for d, total in enumerate(carry)
            )
        return carry

    zero = jnp.zeros((8, TILES_DEV), F32)
    counts = lax.fori_loop(0, TILES_DEV // 64, count, (zero,) * 4)
    for d in range(4):
        rank = jnp.sum(counts[d], axis=0, keepdims=True).astype(jnp.int32)
        ids_s[1, d : d + 1, :] = jnp.where(remote[d : d + 1], rank, -1)

    def fill_unpack(dest, first):
        def body(k, carry):
            for j in range(2):
                rows = pl.ds(pl.multiple_of(32 * k + 16 * j, 16), 16)
                iota = lax.broadcasted_iota(jnp.int32, (16, TILES_DEV), 0) + (32 * k + 16 * j)
                for d in range(2):
                    dest[d, rows, :] = jnp.where(iota == ids_s[1, first + d : first + d + 1, :], 1.0, 0.0).astype(BF16)
            return carry

        lax.fori_loop(0, dest.shape[1] // 32, body, 0)

    fill_unpack(unpack_x, 0)
    fill_unpack(unpack_y, 2)

    def turned_pair(ref, g, i, k):
        return jnp.concatenate([ref[g, 2 * i + j, pl.ds(k, 8, stride=8), :] for j in range(2)], axis=0)

    def pair(ref, g, i, k):
        return ref[g, 2 * i : 2 * i + 2, 8 * k : 8 * k + 8, :].reshape(16, LANES)

    def put_faces_z():
        for g in range(GROUPS):
            col = pl.ds(g * LANES, LANES)
            for i in range(4):
                for d, start in ((0, 5), (1, 0)):
                    for l in range(3):
                        value = turned_pair(pc, g, i, start + l)
                        hi = value.astype(BF16)
                        put_face(faces_z, (d, i), l, col, hi, (value - hi.astype(F32)).astype(BF16))

    def group_of(res, g):
        return res[:, g * LANES : (g + 1) * LANES]

    def gather_z(d, half, halo):
        faces = faces_z[d].reshape(8 * BLOCK, TILES_DEV)
        for i, res in enumerate(two_part_dot(faces, local_m[4 + d, :, 2 * half * LANES : 2 * (half + 1) * LANES])):
            for g in range(2):
                halo[d, g, i] = group_of(res, g)

    def gather_y(d):
        for i, res in enumerate(two_part_dot(faces_y[d].reshape(8 * BLOCK, TILES_DEV), local_m[2 + d])):
            for g in range(GROUPS):
                (halo_ya, halo_yb)[g // 2][d, g % 2, i] = group_of(res, g)

    def gather_x(d):
        for r, res in enumerate(two_part_dot(faces_x[d].reshape(8 * BLOCK, TILES_DEV), local_m[d])):
            for g in range(GROUPS):
                (halo_xa, halo_xb)[r // 2][d, r % 2, g] = group_of(res, g)

    def split_y(t):
        for d in range(2):
            parts = split_rows(recv_y[t, d])
            wide = parts.astype(F32)
            for i in range(4):
                block = pltpu.roll(wide, LANES - i * SLOTS_Y, 1).astype(BF16) if i else parts
                came_y[d, 2 * BLOCK * i : 2 * BLOCK * (i + 1), :] = block

    def split_x(t, half):
        for d in range(2):
            for k in range(2):
                came_x[d, half, 2 * BLOCK * k : 2 * BLOCK * (k + 1), :] = split_rows(recv_x[t, d, 2 * half + k])

    def unpack_half_y(d, half, halo):
        matrix = unpack_y[d, :, 2 * half * LANES : 2 * (half + 1) * LANES]
        for i, res in enumerate(two_part_dot(came_y[d], matrix)):
            for g in range(2):
                halo[d, g, i] = halo[d, g, i] + group_of(res, g)

    def unpack_half_x(d, half, halo):
        for k, res in enumerate(two_part_dot(came_x[d, half], unpack_x[d])):
            for g in range(GROUPS):
                halo[d, k, g] = halo[d, k, g] + group_of(res, g)

    def padded(halo, a, b, there, g, cells):
        def cell(k):
            if 3 <= k < 11:
                return cells(k - 3)
            side, l, edge = (0, k, 0) if k < 3 else (1, k - 11, 7)
            return jnp.where(pres[there + side, g] > 0, halo[side, a, b, 16 * l : 16 * l + 16, :], cells(edge))

        return cell

    def z_lines(line, extra, half, k, halo):
        g = 2 * half + k
        for i in range(4):
            cells = functools.partial(turned_pair, pc, g, i)
            for z, value in enumerate(line(padded(halo, k, i, 4, g, cells), functools.partial(extra, g, i))):
                az[g, 2 * i : 2 * i + 2, 8 * z : 8 * z + 8, :] = value.reshape(2, 8, LANES)

    def y_lines(line, extra, half, k, halo):
        g = 2 * half + k
        for i in range(4):
            cells = functools.partial(pair, pc, g, i)
            for y, value in enumerate(line(padded(halo, k, i, 2, g, cells), functools.partial(extra, g, i))):
                total = value + turned_pair(az, g, i, y)
                ay[g, 2 * i : 2 * i + 2, 8 * y : 8 * y + 8, :] = total.reshape(2, 8, LANES)

    def x_lines(line, extra, finish, c, block, halo, k, groups=range(GROUPS), last=False):
        rows, y_faces = block
        ahead = [take(pc, (groups[0], x), rows) for x in range(8)]
        for g in groups:
            cells = ahead
            if g + 1 in groups:
                ahead = [take(pc, (g + 1, x), rows) for x in range(8)]
            faces = put_faces_xy(g, c, y_faces)
            values = line(padded(halo, k, g, 0, g, cells.__getitem__), lambda x: extra(g, x, rows))
            for x, value in enumerate(values):
                fresh = finish(g, x, rows, cells[x], value + take(ay, (g, x), rows))
                if not last:
                    faces(x, fresh)

    def twice(body):
        def step(k, carry):
            body(k)
            return carry

        lax.fori_loop(0, 2, step, 0)

    def copy_out(g, start, size):
        rows = pl.ds(start, size)
        which = {0: 0, 48: 1, 16: 2}[start]
        return pltpu.make_async_copy(
            pc.at[g, :, rows], out_ref.at[:, rows, lanes(g)], out_sem.at[GROUPS * (1 + which) + g]
        )

    def run(t, line, extra_z, extra_y, extra_x, finish, after_z=None, after_y=None, last=False):
        put_faces_z()
        gather_z(0, 0, halo_za)
        gather_z(1, 0, halo_za)

        def z_first(k):
            gather_z(k, 1, halo_zb)
            z_lines(line, extra_z, 0, k, halo_za)

        def z_second(k):
            gather_y(k)
            z_lines(line, extra_z, 1, k, halo_zb)

        twice(z_first)
        twice(z_second)
        if after_z is not None:
            after_z()
        for d in range(2):
            copy_y(t, d).wait()
        split_y(t)
        unpack_half_y(0, 0, halo_ya)
        unpack_half_y(1, 0, halo_ya)

        def y_first(k):
            gather_x(k)
            unpack_half_y(k, 1, halo_yb)
            y_lines(line, extra_y, 0, k, halo_ya)

        def y_second(k):
            unpack_half_x(k, 0, halo_xa)
            y_lines(line, extra_y, 1, k, halo_yb)

        twice(y_first)
        for r in range(2):
            for d in range(2):
                copy_x(t, d, r).wait()
        split_x(t, 0)
        twice(y_second)
        if after_y is not None:
            after_y()
        for r in range(2, 4):
            for d in range(2):
                copy_x(t, d, r).wait()

        split_x(t, 1)

        def send_on(copies):
            for copy in copies():
                copy.start()

        def x_outer(k):
            unpack_half_x(k, 1, halo_xb)
            if not last:
                pack_block_x(lax.rem(k + 3, 4))
            x_lines(line, extra_x, finish, k, outer_block(k), halo_xa, k, last=last)

        twice(x_outer)
        if last:
            out = [copy_out(g, start, 16) for start in (0, 48) for g in range(GROUPS)]
            for copy in out:
                copy.start()
            x_lines(line, extra_x, finish, 2, third_block, halo_xb, 0, last=True)
            x_lines(line, extra_x, finish, 3, fourth_block, halo_xb, 1, last=True)
            out += [copy_out(g, 16, 32) for g in range(GROUPS)]
            for copy in out[2 * GROUPS :]:
                copy.start()
            for copy in out:
                copy.wait()
            return

        send_on(lambda: [copy_x(t + 1, d, 0) for d in range(2)])
        pack_block_x(1)
        x_lines(line, extra_x, finish, 2, third_block, halo_xb, 0)
        send_on(lambda: [copy_x(t + 1, d, 1) for d in range(2)])
        pack_y_faces()
        x_lines(line, extra_x, finish, 3, fourth_block, halo_xb, 1, range(2))
        send_on(lambda: [copy_y(t + 1, d) for d in range(2)])
        pack_block_x(2)
        x_lines(line, extra_x, finish, 3, fourth_block, halo_xb, 1, range(2, 4))
        send_on(lambda: [copy_x(t + 1, d, 2) for d in range(2)])
        pack_block_x(3)
        send_on(lambda: [copy_x(t + 1, d, 3) for d in range(2)])

    def advect_step(t, carry):
        def after_z():
            @pl.when(t == 0)
            def _():
                ar_start(1, ar_finish(0))

        def after_y():
            @pl.when(t == 0)
            def _():
                top = ar_finish(1)
                top = jnp.max(jnp.max(top, axis=1, keepdims=True), axis=0, keepdims=True)
                step_s[...] = jnp.broadcast_to((CFL / 6.0) / top, (16, LANES))

        old = jnp.where(t == 0, 0.0, jnp.where(t == 1, 0.75, 1.0 / 3.0))
        new = jnp.where(t == 0, 1.0, jnp.where(t == 1, 0.25, 2.0 / 3.0))

        def finish(g, x, rows, cell, total):
            value = old * take(p0, (g, x), rows) + new * (cell - step_s[...] * total)
            put(pc, (g, x), rows, value)
            put(adv, (g, x), rows, value)
            put(sgn, (g, x), rows, jnp.where(value > 0, 1.0, -1.0))
            return value

        run(
            t,
            advect_line,
            lambda g, i, z: pair(vz, g, i, z),
            lambda g, i, y: pair(vel.at[1], g, i, y),
            lambda g, x, rows: take(vel, (0, g, x), rows),
            finish,
            after_z,
            after_y,
        )
        return carry

    lax.fori_loop(0, STAGES, advect_step, 0)

    adv_copies = [
        pltpu.make_async_copy(adv.at[g], adv_out.at[:, :, lanes(g)], out_sem.at[g]) for g in range(GROUPS)
    ]
    for copy in adv_copies:
        copy.start()

    def reinit_step(k, last):
        def finish(g, x, rows, cell, total):
            v = take(adv, (g, x), rows)
            sign = v * lax.rsqrt(v * v + 1.0)
            root = total * (1.0 / 36.0) + ROOT_EPS
            value = cell + (DTAU * sign) * (1.0 - root * lax.rsqrt(root))
            put(pc, (g, x), rows, value)
            return value

        run(
            STAGES + k,
            reinit_line,
            lambda g, i, z: turned_pair(sgn, g, i, z),
            lambda g, i, y: pair(sgn, g, i, y),
            lambda g, x, rows: take(sgn, (g, x), rows),
            finish,
            last=last,
        )

    for k in range(REINIT):
        reinit_step(k, k == REINIT - 1)
    for copy in adv_copies:
        copy.wait()


def hand_over(a_ref, b_ref, x_ref, y_ref, buf, sem):
    ins, outs = [], []
    for k in range(4):
        part = pl.ds(2 * k, 2)
        for i, (src, dst) in enumerate(((a_ref, x_ref), (b_ref, y_ref))):
            ins.append(pltpu.make_async_copy(src.at[part], buf.at[i, part], sem.at[0, 2 * k + i]))
            outs.append(pltpu.make_async_copy(buf.at[i, part], dst.at[part], sem.at[1, 2 * k + i]))
    for copy in ins:
        copy.start()
    for arrived, onward in zip(ins, outs):
        arrived.wait()
        onward.start()
    for copy in outs:
        copy.wait()


def solution(mesh):
    n_band, n_sub = mesh.shape["band"], mesh.shape["sub"]
    low = min(4, n_band)
    cells = (GROUPS, 8, 64, LANES)

    def local(level_set, velocity, neighbours):
        whole = jax.ShapeDtypeStruct((8, 64, TILES_DEV), F32)
        anywhere = pl.BlockSpec(memory_space=pl.ANY)
        advected, reinitialized = pl.pallas_call(
            functools.partial(kernel, n_band, n_sub, low),
            out_shape=(whole, whole),
            in_specs=[anywhere, anywhere, pl.BlockSpec(memory_space=pltpu.VMEM)],
            out_specs=(anywhere, anywhere),
            scratch_shapes=[
                pltpu.VMEM(cells, F32),
                pltpu.VMEM(cells, F32),
                pltpu.VMEM(cells, F32),
                pltpu.VMEM(cells, F32),
                pltpu.VMEM((3,) + cells, F32),
                pltpu.VMEM(cells, F32),
                pltpu.VMEM(cells, F32),
                pltpu.VMEM(cells, F32),
                *[pltpu.VMEM((2, 2, GROUPS, BLOCK, LANES), F32)] * 2,
                *[pltpu.VMEM((2, 2, 4, BLOCK, LANES), F32)] * 4,
                pltpu.VMEM((2, 4, 2 * BLOCK, TILES_DEV), BF16),
                pltpu.VMEM((2, 4, 2 * BLOCK, TILES_DEV), BF16),
                pltpu.VMEM((2, 4, 2 * BLOCK, TILES_DEV), BF16),
                pltpu.VMEM((2, 2, 4 * BLOCK, SLOTS_X), BF16),
                pltpu.VMEM((2, 8 * BLOCK, LANES), BF16),
                pltpu.VMEM((6, TILES_DEV, TILES_DEV), BF16),
                pltpu.VMEM((2, TILES_DEV, SLOTS_X), BF16),
                pltpu.VMEM((2, TILES_DEV, LANES), BF16),
                pltpu.VMEM((2, SLOTS_X, TILES_DEV), BF16),
                pltpu.VMEM((2, LANES, TILES_DEV), BF16),
                pltpu.VMEM((TILES_DEV, TILES_DEV), BF16),
                pltpu.VMEM((6, GROUPS, 16, LANES), F32),
                pltpu.VMEM((8, TILES_DEV), jnp.int32),
                pltpu.VMEM((2, 8, TILES_DEV), jnp.int32),
                pltpu.VMEM((LANES, TILES_DEV), F32),
                pltpu.VMEM((TILES_DEV, LANES), F32),
                pltpu.VMEM((2, 4, BLOCK, SLOTS_X), F32),
                pltpu.VMEM((2, BLOCK, LANES), F32),
                pltpu.VMEM((STEPS, 2, 4, BLOCK, SLOTS_X), F32),
                pltpu.VMEM((STEPS, 2, BLOCK, LANES), F32),
                pltpu.VMEM((2, 8, LANES), F32),
                pltpu.VMEM((max(1, low * n_sub - 1), 8, LANES), F32),
                pltpu.VMEM((max(1, n_band // low - 1), 8, LANES), F32),
                pltpu.VMEM((16, LANES), F32),
                pltpu.SemaphoreType.DMA((16,)),
                pltpu.SemaphoreType.DMA((5 * GROUPS,)),
                pltpu.SemaphoreType.DMA((2, 4)),
                pltpu.SemaphoreType.DMA((STEPS, 2, 4)),
                pltpu.SemaphoreType.DMA((2,)),
                pltpu.SemaphoreType.DMA((STEPS, 2)),
                pltpu.SemaphoreType.DMA((low * n_sub + n_band // low,)),
                pltpu.SemaphoreType.DMA((low * n_sub + n_band // low,)),
            ],
            compiler_params=pltpu.CompilerParams(
                collective_id=0, has_side_effects=True, vmem_limit_bytes=56 * 2**20
            ),
        )(level_set.reshape(8, 64, TILES_DEV), velocity.reshape(3, 8, 64, TILES_DEV), neighbours)
        advected, reinitialized = pl.pallas_call(
            hand_over,
            out_shape=(whole, whole),
            in_specs=[anywhere, anywhere],
            out_specs=(anywhere, anywhere),
            scratch_shapes=[pltpu.VMEM((2, 8, 64, TILES_DEV), F32), pltpu.SemaphoreType.DMA((2, 8))],
        )(advected, reinitialized)
        return advected.reshape(8, 8, 8, TILES_DEV), reinitialized.reshape(8, 8, 8, TILES_DEV)

    return jax.shard_map(
        local,
        mesh=mesh,
        in_specs=(
            P(None, None, None, ("band", "sub")),
            P(None, None, None, None, ("band", "sub")),
            P(None, ("band", "sub")),
        ),
        out_specs=(P(None, None, None, ("band", "sub")), P(None, None, None, ("band", "sub"))),
        check_vma=False,
    )
```

```python
import functools

import jax
import jax.numpy as jnp
from jax import lax
from jax.experimental import pallas as pl
from jax.experimental.pallas import tpu as pltpu
from jax.sharding import PartitionSpec as P

TILES_DEV = 512
SLOTS_X = 256
SLOTS_Y = 32
BLOCK = 48
STAGES = 3
REINIT = 2
STEPS = STAGES + REINIT
EPS = 1e-06
CFL = 0.5
DTAU = 0.3
ROOT_EPS = 1e-06
LANES = 128
GROUPS = TILES_DEV // LANES

F32 = jnp.float32
BF16 = jnp.bfloat16
MESH = pl.DeviceIdType.MESH


class Line:
    def __init__(self, cell):
        self.cell, self.made = cell, {}

    def get(self, kind, k):
        if (kind, k) not in self.made:
            self.made[kind, k] = getattr(self, kind)(k)
        return self.made[kind, k]

    def first(self, k):
        return self.get("cell", k + 1) - self.get("cell", k)

    def second(self, k):
        return self.get("first", k + 1) - self.get("first", k)

    def third(self, k):
        return self.get("second", k + 1) - self.get("second", k)

    def fourth(self, k):
        return self.get("third", k) - self.get("third", k - 1)

    def square(self, k):
        return self.get("second", k) * self.get("second", k)

    def half(self, k):
        return (0.5 * self.get("second", k)) * self.get("second", k + 1)

    def base(self, k):
        return self.get("third", k) * self.get("third", k) * (2.0 / 3.0) + 0.5 * EPS

    def low(self, k):
        return self.get("base", k) - self.get("half", k)

    def ind_a(self, k):
        return self.get("low", k) + self.get("square", k + 1)

    def ind_b(self, k):
        return self.get("base", k) + self.get("half", k)

    def ind_c(self, k):
        return self.get("low", k) + self.get("square", k)

    def weight_a(self, k):
        r = recip(self.get("ind_a", k))
        return r * r

    def weight_b(self, k):
        r = recip(self.get("ind_b", k))
        return r * r * 6.0

    def weight_c(self, k):
        r = recip(self.get("ind_c", k))
        return r * r

    def triple_a(self, k):
        return self.get("weight_a", k) * 3.0

    def triple_c(self, k):
        return self.get("weight_c", k) * 3.0

    def twice(self, k):
        return self.get("fourth", k) + self.get("fourth", k)


def recip(x):
    return pl.reciprocal(x, approx=True)


def advect_line(cell, flow_of):
    get = Line(cell).get
    for c in range(8):
        flow, size = flow_of(c)
        up = flow > 0
        ra = recip(jnp.where(up, get("ind_a", c), get("ind_c", c + 3)))
        rb = recip(jnp.where(up, get("ind_b", c + 1), get("ind_b", c + 2)))
        rc = recip(jnp.where(up, get("ind_c", c + 2), get("ind_a", c + 1)))
        wa = ra * ra
        wb = rb * rb * 6.0
        wc = rc * rc * 3.0
        far = jnp.where(up, get("fourth", c + 1), get("fourth", c + 3))
        num = wa * (far + far) + wc * get("fourth", c + 2)
        corr = num * recip(wa + wb + wc)
        linear = 3.0 * (get("cell", c + 4) - get("cell", c + 2)) - jnp.where(up, get("third", c + 1), get("third", c + 2))
        yield flow * linear - size * corr


def reinit_line(cell, sign_of):
    get = Line(cell).get
    for c in range(8):
        sign = sign_of(c)
        linear = 3.0 * (get("cell", c + 4) - get("cell", c + 2))
        mid = get("fourth", c + 2)
        wa, wb, wc = get("weight_a", c), get("weight_b", c + 1), get("triple_c", c + 2)
        corr_b = (wa * get("twice", c + 1) + wc * mid) * recip(wa + wb + wc)
        wa, wb, wc = get("weight_c", c + 3), get("weight_b", c + 2), get("triple_a", c + 1)
        corr_f = (wa * get("twice", c + 3) + wc * mid) * recip(wa + wb + wc)
        back = linear - get("third", c + 1) - corr_b
        fore = get("third", c + 2) - linear - corr_f
        m = jnp.maximum(jnp.maximum(sign * back, sign * fore), 0.0)
        yield m * m


def split_rows(value):
    hi = value.astype(BF16)
    lo = (value - hi.astype(F32)).astype(BF16)
    return jnp.concatenate([hi, lo], axis=0)


def two_part_dot(lhs, rhs):
    res = jnp.dot(lhs, rhs, preferred_element_type=F32)
    blocks = res.shape[0] // (2 * BLOCK)
    return [
        res[2 * BLOCK * k : 2 * BLOCK * k + BLOCK] + res[2 * BLOCK * k + BLOCK : 2 * BLOCK * (k + 1)]
        for k in range(blocks)
    ]


def kernel(
    n_band, n_sub, low,
    ls_ref, vel_ref, nb_ref, adv_out, out_ref,
    p0, pc, adv, sgn, vel, vz, size, az, ay,
    halo_xa, halo_xb, halo_ya, halo_yb, halo_za, halo_zb, faces_x, faces_y, faces_z, came_x, came_y,
    local_m, pack_x, pack_y, unpack_x, unpack_y, tri, pres,
    nb_s, ids_s, krow, kcol, send_x, send_y, recv_x, recv_y, ar_send, ar_near, ar_far, step_s,
    in_sem, out_sem, tx_x, rx_x, tx_y, rx_y, ar_tx, ar_rx,
):
    band = lax.axis_index("band")
    sub = lax.axis_index("sub")
    n_high = n_band // low
    n_near = low * n_sub
    band_up, band_dn = lax.rem(band + 1, n_band), lax.rem(band + n_band - 1, n_band)
    sub_up, sub_dn = lax.rem(sub + 1, n_sub), lax.rem(sub + n_sub - 1, n_sub)
    band_low = lax.rem(band, low)

    def near_peer(d):
        return (band - band_low + lax.rem(band_low + d // n_sub, low), lax.rem(sub + d % n_sub, n_sub))

    def far_peer(d):
        return (lax.rem(band + d * low, n_band), sub)

    def lanes(g):
        return pl.ds(g * LANES, LANES)

    in_copies = []
    for g in range(GROUPS):
        in_copies.append(pltpu.make_async_copy(ls_ref.at[:, :, lanes(g)], p0.at[g], in_sem.at[12 + g]))
    for k in range(3):
        for g in range(GROUPS):
            in_copies.append(
                pltpu.make_async_copy(vel_ref.at[k, :, :, lanes(g)], vel.at[k, g], in_sem.at[4 * k + g])
            )
    for copy in in_copies:
        copy.start()

    peers = [(band_up, sub), (band_dn, sub)]
    peers += [near_peer(d) for d in range(1, n_near)]
    peers += [far_peer(d) for d in range(1, n_high)]
    barrier = pltpu.get_barrier_semaphore()
    for peer in peers:
        pl.semaphore_signal(barrier, inc=1, device_id=peer, device_id_type=MESH)

    nb_s[...] = jnp.full((8, TILES_DEV), -1, jnp.int32)
    nb_s[0:6, :] = nb_ref[...]
    nb = nb_s[...]
    base = (band * n_sub + sub) * TILES_DEV
    present = nb >= 0
    is_local = (nb >= base) & (nb < base + TILES_DEV)
    remote = present & jnp.logical_not(is_local)
    ids_s[0] = jnp.where(is_local, nb - base, -1)
    presf = jnp.where(present, 1.0, 0.0)
    for d in range(6):
        for g in range(GROUPS):
            pres[d, g] = jnp.broadcast_to(presf[d : d + 1, g * LANES : (g + 1) * LANES], (16, LANES))

    def fill_tri(k, carry):
        rows = pl.ds(pl.multiple_of(16 * k, 16), 16)
        iota = lax.broadcasted_iota(jnp.int32, (16, TILES_DEV), 0) + 16 * k
        lane = lax.broadcasted_iota(jnp.int32, (16, TILES_DEV), 1)
        tri[rows, :] = jnp.where(iota < lane, 1.0, 0.0).astype(BF16)
        return carry

    lax.fori_loop(0, TILES_DEV // 16, fill_tri, 0)
    flags = jnp.where(remote, 1.0, 0.0)
    flags16 = jnp.concatenate([flags, jnp.zeros_like(flags)], axis=0).astype(BF16)
    place = jnp.dot(flags16, tri[...], preferred_element_type=F32)[0:8]
    keys = jnp.where(remote, nb.astype(F32), 1e9)
    krow[...] = jnp.zeros_like(krow)
    krow[0:4, :] = keys[0:4]
    krow[4:8, :] = jnp.where(remote, place, -1.0)[0:4]
    for c in range(GROUPS):
        kcol[c * LANES : (c + 1) * LANES, :] = krow[:, c * LANES : (c + 1) * LANES].T

    def ar_copies(r):
        peer, slots, n = ((near_peer, ar_near, n_near), (far_peer, ar_far, n_high))[r]
        first = (0, n_near)[r]
        return [
            pltpu.make_async_remote_copy(
                src_ref=ar_send.at[r],
                dst_ref=slots.at[d - 1],
                send_sem=ar_tx.at[first + d - 1],
                recv_sem=ar_rx.at[first + d - 1],
                device_id=peer(d),
                device_id_type=MESH,
            )
            for d in range(1, n)
        ], slots

    def ar_start(r, value):
        ar_send[r] = value
        for copy in ar_copies(r)[0]:
            copy.start()

    def ar_finish(r):
        value = ar_send[r]
        copies, slots = ar_copies(r)
        for k, copy in enumerate(copies):
            copy.wait()
            value = jnp.maximum(value, slots[k])
        return value

    def copy_x(t, d, r):
        return pltpu.make_async_remote_copy(
            src_ref=send_x.at[d, r],
            dst_ref=recv_x.at[t, 1 - d, r],
            send_sem=tx_x.at[d, r],
            recv_sem=rx_x.at[t, d, r],
            device_id=((band_dn, sub), (band_up, sub))[d],
            device_id_type=MESH,
        )

    def copy_y(t, d):
        return pltpu.make_async_remote_copy(
            src_ref=send_y.at[d],
            dst_ref=recv_y.at[t, 1 - d],
            send_sem=tx_y.at[d],
            recv_sem=rx_y.at[t, d],
            device_id=((band, sub_dn), (band, sub_up))[d],
            device_id_type=MESH,
        )

    def fill_pack(k, carry):
        lane_x = lax.broadcasted_iota(jnp.int32, (16, SLOTS_X), 1).astype(F32)
        lane_y = lax.broadcasted_iota(jnp.int32, (16, LANES), 1).astype(F32)
        for j in range(4):
            rows = pl.ds(pl.multiple_of(64 * k + 16 * j, 16), 16)
            for d in range(2):
                pack_x[d, rows, :] = jnp.where(kcol[rows, 4 + d : 5 + d] == lane_x, 1.0, 0.0).astype(BF16)
                pack_y[d, rows, :] = jnp.where(kcol[rows, 6 + d : 7 + d] == lane_y, 1.0, 0.0).astype(BF16)
        return carry

    lax.fori_loop(0, TILES_DEV // 64, fill_pack, 0)

    def put_face(ref, lead, l, col, hi, lo):
        ref[(*lead, pl.ds(pl.multiple_of(16 * l, 16), 16), col)] = hi
        ref[(*lead, pl.ds(pl.multiple_of(BLOCK + 16 * l, 16), 16), col)] = lo

    def outer_block(k):
        return [(pl.multiple_of(48 * k, 16), 16)], ((1 - k, k), (1 - k, k + 1))

    third_block = [(16, 8), (40, 8)], ((1, 2), (0, 0))
    fourth_block = [(24, 16)], ()

    def take(ref, lead, rows):
        pieces = [ref[(*lead, pl.ds(start, size), slice(None))] for start, size in rows]
        return pieces[0] if len(pieces) == 1 else jnp.concatenate(pieces, axis=0)

    def put(ref, lead, rows, value):
        first = 0
        for start, size in rows:
            ref[(*lead, pl.ds(start, size), slice(None))] = value[first : first + size]
            first += size

    def put_faces_xy(g, c, y_faces):
        col = pl.ds(g * LANES, LANES)
        kept = []

        def add(x, value):
            hi = value.astype(BF16)
            rest = value - hi.astype(F32)
            kept.append((value, rest))
            if x not in (3, 4):
                put_face(faces_x, (0 if x > 4 else 1, c), x - 5 if x > 4 else x, col, hi, rest.astype(BF16))
            if x % 2 == 0:
                return
            for j, (d, layer) in enumerate(y_faces):
                hi, lo = [
                    jnp.concatenate([part[8 * j : 8 * j + 8] for part in parts], axis=0).astype(BF16)
                    for parts in zip(*kept[x - 1 : x + 1])
                ]
                put_face(faces_y, (d, x // 2), layer, col, hi, lo)

        return add

    def pack_block_x(c):
        for d in range(2):
            send_x[d, c] = two_part_dot(faces_x[1 - d, c], pack_x[d])[0]

    def pack_y_faces():
        for d in range(2):
            parts = two_part_dot(faces_y[1 - d].reshape(8 * BLOCK, TILES_DEV), pack_y[d])
            send_y[d] = sum(pltpu.roll(parts[i], i * SLOTS_Y, 1) if i else parts[i] for i in range(4))

    def copy_in(c, block):
        rows, y_faces = block
        for g in range(GROUPS):
            faces = put_faces_xy(g, c, y_faces)
            for x in range(8):
                value = take(p0, (g, x), rows)
                put(pc, (g, x), rows, value)
                faces(x, value)
        pack_block_x(c)

    def copy_in_outer(k, carry):
        copy_in(k, outer_block(k))
        return carry

    for copy in in_copies[:GROUPS]:
        copy.wait()
    lax.fori_loop(0, 2, copy_in_outer, 0)
    copy_in(2, third_block)
    pack_y_faces()
    copy_in(3, fourth_block)

    for copy in in_copies[GROUPS:]:
        copy.wait()

    def speeds(idx, top):
        g, x = idx // 8, lax.rem(idx, 8)
        for y in range(8):
            rows = slice(8 * y, 8 * y + 8)
            sizes = [jnp.abs(vel[k, g, x, rows, :]) for k in range(3)]
            top = jnp.maximum(top, sizes[0] + sizes[1] + sizes[2])
            size[0, g, x, rows, :] = sizes[0]
            size[1, g, x, rows, :] = sizes[1]
        for z in range(8):
            turned = vel[2, g, x, pl.ds(z, 8, stride=8), :]
            vz[g, x, 8 * z : 8 * z + 8, :] = turned
            size[2, g, x, 8 * z : 8 * z + 8, :] = jnp.abs(turned)
        return top

    top = lax.fori_loop(0, GROUPS * 8, speeds, jnp.zeros((8, LANES), F32))

    pl.semaphore_wait(barrier, len(peers))

    ar_start(0, top)
    for d in range(2):
        copy_y(0, d).start()
    for c in range(4):
        for d in range(2):
            copy_x(0, d, c).start()

    def fill(k, carry):
        for j in range(2):
            rows = pl.ds(pl.multiple_of(32 * k + 16 * j, 16), 16)
            iota = lax.broadcasted_iota(jnp.int32, (16, TILES_DEV), 0) + (32 * k + 16 * j)
            for d in range(6):
                local_m[d, rows, :] = jnp.where(iota == ids_s[0, d : d + 1, :], 1.0, 0.0).astype(BF16)
        return carry

    lax.fori_loop(0, TILES_DEV // 32, fill, 0)

    def count(k, carry):
        for j in range(8):
            rows = pl.ds(pl.multiple_of(64 * k + 8 * j, 8), 8)
            carry = tuple(
                total + jnp.where(kcol[rows, d : d + 1] < krow[d : d + 1, :], 1.0, 0.0)
                for d, total in enumerate(carry)
            )
        return carry

    zero = jnp.zeros((8, TILES_DEV), F32)
    counts = lax.fori_loop(0, TILES_DEV // 64, count, (zero,) * 4)
    for d in range(4):
        rank = jnp.sum(counts[d], axis=0, keepdims=True).astype(jnp.int32)
        ids_s[1, d : d + 1, :] = jnp.where(remote[d : d + 1], rank, -1)

    def fill_unpack(dest, first):
        def body(k, carry):
            for j in range(2):
                rows = pl.ds(pl.multiple_of(32 * k + 16 * j, 16), 16)
                iota = lax.broadcasted_iota(jnp.int32, (16, TILES_DEV), 0) + (32 * k + 16 * j)
                for d in range(2):
                    dest[d, rows, :] = jnp.where(iota == ids_s[1, first + d : first + d + 1, :], 1.0, 0.0).astype(BF16)
            return carry

        lax.fori_loop(0, dest.shape[1] // 32, body, 0)

    fill_unpack(unpack_x, 0)
    fill_unpack(unpack_y, 2)

    def turned_pair(ref, g, i, k):
        return jnp.concatenate([ref[g, 2 * i + j, pl.ds(k, 8, stride=8), :] for j in range(2)], axis=0)

    def pair(ref, g, i, k):
        return ref[g, 2 * i : 2 * i + 2, 8 * k : 8 * k + 8, :].reshape(16, LANES)

    def put_faces_z(groups):
        for g in groups:
            col = pl.ds(g * LANES, LANES)
            for i in range(4):
                for d, start in ((0, 5), (1, 0)):
                    for l in range(3):
                        value = turned_pair(pc, g, i, start + l)
                        hi = value.astype(BF16)
                        put_face(faces_z, (d, i), l, col, hi, (value - hi.astype(F32)).astype(BF16))

    def group_of(res, g):
        return res[:, g * LANES : (g + 1) * LANES]

    def gather_z(d, half, halo):
        faces = faces_z[d].reshape(8 * BLOCK, TILES_DEV)
        for i, res in enumerate(two_part_dot(faces, local_m[4 + d, :, 2 * half * LANES : 2 * (half + 1) * LANES])):
            for g in range(2):
                halo[d, g, i] = group_of(res, g)

    def gather_y(d):
        for i, res in enumerate(two_part_dot(faces_y[d].reshape(8 * BLOCK, TILES_DEV), local_m[2 + d])):
            for g in range(GROUPS):
                (halo_ya, halo_yb)[g // 2][d, g % 2, i] = group_of(res, g)

    def gather_x(d):
        for r, res in enumerate(two_part_dot(faces_x[d].reshape(8 * BLOCK, TILES_DEV), local_m[d])):
            for g in range(GROUPS):
                (halo_xa, halo_xb)[r // 2][d, r % 2, g] = group_of(res, g)

    def split_y(t):
        for d in range(2):
            parts = split_rows(recv_y[t, d])
            wide = parts.astype(F32)
            for i in range(4):
                block = pltpu.roll(wide, LANES - i * SLOTS_Y, 1).astype(BF16) if i else parts
                came_y[d, 2 * BLOCK * i : 2 * BLOCK * (i + 1), :] = block

    def split_x(t, half):
        for d in range(2):
            for k in range(2):
                came_x[d, half, 2 * BLOCK * k : 2 * BLOCK * (k + 1), :] = split_rows(recv_x[t, d, 2 * half + k])

    def unpack_half_y(d, half, halo):
        matrix = unpack_y[d, :, 2 * half * LANES : 2 * (half + 1) * LANES]
        for i, res in enumerate(two_part_dot(came_y[d], matrix)):
            for g in range(2):
                halo[d, g, i] = halo[d, g, i] + group_of(res, g)

    def unpack_half_x(d, half, halo):
        for k, res in enumerate(two_part_dot(came_x[d, half], unpack_x[d])):
            for g in range(GROUPS):
                halo[d, k, g] = halo[d, k, g] + group_of(res, g)

    def padded(halo, a, b, there, g, cells):
        masks = {}

        def cell(k):
            if 3 <= k < 11:
                return cells(k - 3)
            side, l, edge = (0, k, 0) if k < 3 else (1, k - 11, 7)
            if side not in masks:
                masks[side] = pres[there + side, g] > 0, cells(edge)
            return jnp.where(masks[side][0], halo[side, a, b, 16 * l : 16 * l + 16, :], masks[side][1])

        return cell

    def z_lines(line, extra, half, k, halo):
        g = 2 * half + k
        for i in range(4):
            cells = functools.partial(turned_pair, pc, g, i)
            for z, value in enumerate(line(padded(halo, k, i, 4, g, cells), functools.partial(extra, g, i))):
                az[g, 2 * i : 2 * i + 2, 8 * z : 8 * z + 8, :] = value.reshape(2, 8, LANES)

    def y_lines(line, extra, half, k, halo):
        g = 2 * half + k
        for i in range(4):
            cells = functools.partial(pair, pc, g, i)
            for y, value in enumerate(line(padded(halo, k, i, 2, g, cells), functools.partial(extra, g, i))):
                total = value + turned_pair(az, g, i, y)
                ay[g, 2 * i : 2 * i + 2, 8 * y : 8 * y + 8, :] = total.reshape(2, 8, LANES)

    def x_lines(line, extra, finish, c, block, halo, k, groups=range(GROUPS), last=False):
        rows, y_faces = block
        ahead = [take(pc, (groups[0], x), rows) for x in range(8)]
        for g in groups:
            cells = ahead
            if g + 1 in groups:
                ahead = [take(pc, (g + 1, x), rows) for x in range(8)]
            faces = put_faces_xy(g, c, y_faces)
            values = line(padded(halo, k, g, 0, g, cells.__getitem__), lambda x: extra(g, x, rows))
            for x, value in enumerate(values):
                fresh = finish(g, x, rows, cells[x], value + take(ay, (g, x), rows))
                if not last:
                    faces(x, fresh)

    def twice(body):
        def step(k, carry):
            body(k)
            return carry

        lax.fori_loop(0, 2, step, 0)

    def copy_out(g, start, size):
        rows = pl.ds(start, size)
        which = {0: 0, 48: 1, 16: 2}[start]
        return pltpu.make_async_copy(
            pc.at[g, :, rows], out_ref.at[:, rows, lanes(g)], out_sem.at[GROUPS * (1 + which) + g]
        )

    def run(t, line, extra_z, extra_y, extra_x, finish, after_z=None, after_y=None, last=False):
        gather_z(0, 0, halo_za)
        gather_z(1, 0, halo_za)

        def z_first(k):
            gather_z(k, 1, halo_zb)
            z_lines(line, extra_z, 0, k, halo_za)

        def z_second(k):
            gather_y(k)
            z_lines(line, extra_z, 1, k, halo_zb)

        twice(z_first)
        if after_z is not None:
            after_z()
        twice(z_second)
        for d in range(2):
            copy_y(t, d).wait()
        split_y(t)
        unpack_half_y(0, 0, halo_ya)
        unpack_half_y(1, 0, halo_ya)

        def y_first(k):
            gather_x(k)
            unpack_half_y(k, 1, halo_yb)
            y_lines(line, extra_y, 0, k, halo_ya)

        def y_second(k):
            unpack_half_x(k, 0, halo_xa)
            y_lines(line, extra_y, 1, k, halo_yb)

        twice(y_first)
        for r in range(2):
            for d in range(2):
                copy_x(t, d, r).wait()
        split_x(t, 0)
        twice(y_second)
        if after_y is not None:
            after_y()
        for r in range(2, 4):
            for d in range(2):
                copy_x(t, d, r).wait()

        split_x(t, 1)

        def send_on(copies):
            for copy in copies():
                copy.start()

        def x_outer(k):
            unpack_half_x(k, 1, halo_xb)
            if not last:
                pack_block_x(lax.rem(k + 3, 4))
            x_lines(line, extra_x, finish, k, outer_block(k), halo_xa, k, last=last)

        twice(x_outer)
        if last:
            out = [copy_out(g, start, 16) for start in (0, 48) for g in range(GROUPS)]
            for copy in out:
                copy.start()
            x_lines(line, extra_x, finish, 2, third_block, halo_xb, 0, last=True)
            x_lines(line, extra_x, finish, 3, fourth_block, halo_xb, 1, last=True)
            out += [copy_out(g, 16, 32) for g in range(GROUPS)]
            for copy in out[2 * GROUPS :]:
                copy.start()
            for copy in out:
                copy.wait()
            return

        send_on(lambda: [copy_x(t + 1, d, 0) for d in range(2)])
        pack_block_x(1)
        x_lines(line, extra_x, finish, 2, third_block, halo_xb, 0)
        send_on(lambda: [copy_x(t + 1, d, 1) for d in range(2)])
        pack_y_faces()
        x_lines(line, extra_x, finish, 3, fourth_block, halo_xb, 1, range(2))
        send_on(lambda: [copy_y(t + 1, d) for d in range(2)])
        pack_block_x(2)
        x_lines(line, extra_x, finish, 3, fourth_block, halo_xb, 1, range(2, 4))
        put_faces_z(range(2))
        send_on(lambda: [copy_x(t + 1, d, 2) for d in range(2)])
        pack_block_x(3)
        put_faces_z(range(2, 4))
        send_on(lambda: [copy_x(t + 1, d, 3) for d in range(2)])

    put_faces_z(range(GROUPS))

    def advect_step(t, carry):
        def after_z():
            @pl.when(t == 0)
            def _():
                ar_start(1, ar_finish(0))

        def after_y():
            @pl.when(t == 0)
            def _():
                top = ar_finish(1)
                top = jnp.max(jnp.max(top, axis=1, keepdims=True), axis=0, keepdims=True)
                step_s[...] = jnp.broadcast_to((CFL / 6.0) / top, (16, LANES))

        old = jnp.where(t == 0, 0.0, jnp.where(t == 1, 0.75, 1.0 / 3.0))
        new = jnp.where(t == 0, 1.0, jnp.where(t == 1, 0.25, 2.0 / 3.0))

        def finish(g, x, rows, cell, total):
            value = old * take(p0, (g, x), rows) + new * (cell - step_s[...] * total)
            put(pc, (g, x), rows, value)
            put(adv, (g, x), rows, value)
            put(sgn, (g, x), rows, jnp.where(value > 0, 1.0, -1.0))
            return value

        run(
            t,
            advect_line,
            lambda g, i, z: (pair(vz, g, i, z), pair(size.at[2], g, i, z)),
            lambda g, i, y: (pair(vel.at[1], g, i, y), pair(size.at[1], g, i, y)),
            lambda g, x, rows: (take(vel, (0, g, x), rows), take(size, (0, g, x), rows)),
            finish,
            after_z,
            after_y,
        )
        return carry

    lax.fori_loop(0, STAGES, advect_step, 0)

    adv_copies = [
        pltpu.make_async_copy(adv.at[g], adv_out.at[:, :, lanes(g)], out_sem.at[g]) for g in range(GROUPS)
    ]
    for copy in adv_copies:
        copy.start()

    def reinit_step(k, last):
        def finish(g, x, rows, cell, total):
            v = take(adv, (g, x), rows)
            sign = v * lax.rsqrt(v * v + 1.0)
            root = total * (1.0 / 36.0) + ROOT_EPS
            value = cell + (DTAU * sign) * (1.0 - root * lax.rsqrt(root))
            put(pc, (g, x), rows, value)
            return value

        run(
            STAGES + k,
            reinit_line,
            lambda g, i, z: turned_pair(sgn, g, i, z),
            lambda g, i, y: pair(sgn, g, i, y),
            lambda g, x, rows: take(sgn, (g, x), rows),
            finish,
            last=last,
        )

    for k in range(REINIT):
        reinit_step(k, k == REINIT - 1)
    for copy in adv_copies:
        copy.wait()


def hand_over(a_ref, b_ref, x_ref, y_ref, buf, sem):
    ins, outs = [], []
    for k in range(4):
        part = pl.ds(2 * k, 2)
        for i, (src, dst) in enumerate(((a_ref, x_ref), (b_ref, y_ref))):
            ins.append(pltpu.make_async_copy(src.at[part], buf.at[i, part], sem.at[0, 2 * k + i]))
            outs.append(pltpu.make_async_copy(buf.at[i, part], dst.at[part], sem.at[1, 2 * k + i]))
    for copy in ins:
        copy.start()
    for arrived, onward in zip(ins, outs):
        arrived.wait()
        onward.start()
    for copy in outs:
        copy.wait()


def solution(mesh):
    n_band, n_sub = mesh.shape["band"], mesh.shape["sub"]
    low = min(2, n_band)
    cells = (GROUPS, 8, 64, LANES)

    def local(level_set, velocity, neighbours):
        whole = jax.ShapeDtypeStruct((8, 64, TILES_DEV), F32)
        anywhere = pl.BlockSpec(memory_space=pl.ANY)
        advected, reinitialized = pl.pallas_call(
            functools.partial(kernel, n_band, n_sub, low),
            out_shape=(whole, whole),
            in_specs=[anywhere, anywhere, pl.BlockSpec(memory_space=pltpu.VMEM)],
            out_specs=(anywhere, anywhere),
            scratch_shapes=[
                pltpu.VMEM(cells, F32),
                pltpu.VMEM(cells, F32),
                pltpu.VMEM(cells, F32),
                pltpu.VMEM(cells, F32),
                pltpu.VMEM((3,) + cells, F32),
                pltpu.VMEM(cells, F32),
                pltpu.VMEM((3,) + cells, F32),
                pltpu.VMEM(cells, F32),
                pltpu.VMEM(cells, F32),
                *[pltpu.VMEM((2, 2, GROUPS, BLOCK, LANES), F32)] * 2,
                *[pltpu.VMEM((2, 2, 4, BLOCK, LANES), F32)] * 4,
                pltpu.VMEM((2, 4, 2 * BLOCK, TILES_DEV), BF16),
                pltpu.VMEM((2, 4, 2 * BLOCK, TILES_DEV), BF16),
                pltpu.VMEM((2, 4, 2 * BLOCK, TILES_DEV), BF16),
                pltpu.VMEM((2, 2, 4 * BLOCK, SLOTS_X), BF16),
                pltpu.VMEM((2, 8 * BLOCK, LANES), BF16),
                pltpu.VMEM((6, TILES_DEV, TILES_DEV), BF16),
                pltpu.VMEM((2, TILES_DEV, SLOTS_X), BF16),
                pltpu.VMEM((2, TILES_DEV, LANES), BF16),
                pltpu.VMEM((2, SLOTS_X, TILES_DEV), BF16),
                pltpu.VMEM((2, LANES, TILES_DEV), BF16),
                pltpu.VMEM((TILES_DEV, TILES_DEV), BF16),
                pltpu.VMEM((6, GROUPS, 16, LANES), F32),
                pltpu.VMEM((8, TILES_DEV), jnp.int32),
                pltpu.VMEM((2, 8, TILES_DEV), jnp.int32),
                pltpu.VMEM((LANES, TILES_DEV), F32),
                pltpu.VMEM((TILES_DEV, LANES), F32),
                pltpu.VMEM((2, 4, BLOCK, SLOTS_X), F32),
                pltpu.VMEM((2, BLOCK, LANES), F32),
                pltpu.VMEM((STEPS, 2, 4, BLOCK, SLOTS_X), F32),
                pltpu.VMEM((STEPS, 2, BLOCK, LANES), F32),
                pltpu.VMEM((2, 8, LANES), F32),
                pltpu.VMEM((max(1, low * n_sub - 1), 8, LANES), F32),
                pltpu.VMEM((max(1, n_band // low - 1), 8, LANES), F32),
                pltpu.VMEM((16, LANES), F32),
                pltpu.SemaphoreType.DMA((16,)),
                pltpu.SemaphoreType.DMA((5 * GROUPS,)),
                pltpu.SemaphoreType.DMA((2, 4)),
                pltpu.SemaphoreType.DMA((STEPS, 2, 4)),
                pltpu.SemaphoreType.DMA((2,)),
                pltpu.SemaphoreType.DMA((STEPS, 2)),
                pltpu.SemaphoreType.DMA((low * n_sub + n_band // low,)),
                pltpu.SemaphoreType.DMA((low * n_sub + n_band // low,)),
            ],
            compiler_params=pltpu.CompilerParams(
                collective_id=0, has_side_effects=True, vmem_limit_bytes=56 * 2**20
            ),
        )(level_set.reshape(8, 64, TILES_DEV), velocity.reshape(3, 8, 64, TILES_DEV), neighbours)
        advected, reinitialized = pl.pallas_call(
            hand_over,
            out_shape=(whole, whole),
            in_specs=[anywhere, anywhere],
            out_specs=(anywhere, anywhere),
            scratch_shapes=[pltpu.VMEM((2, 8, 64, TILES_DEV), F32), pltpu.SemaphoreType.DMA((2, 8))],
        )(advected, reinitialized)
        return advected.reshape(8, 8, 8, TILES_DEV), reinitialized.reshape(8, 8, 8, TILES_DEV)

    return jax.shard_map(
        local,
        mesh=mesh,
        in_specs=(
            P(None, None, None, ("band", "sub")),
            P(None, None, None, None, ("band", "sub")),
            P(None, ("band", "sub")),
        ),
        out_specs=(P(None, None, None, ("band", "sub")), P(None, None, None, ("band", "sub"))),
        check_vma=False,
    )
```

```python
import functools

import jax
import jax.numpy as jnp
from jax import lax
from jax.experimental import pallas as pl
from jax.experimental.pallas import tpu as pltpu
from jax.sharding import PartitionSpec as P

TILES_DEV = 512
SLOTS_X = 256
SLOTS_Y = 32
BLOCK = 48
STAGES = 3
REINIT = 2
STEPS = STAGES + REINIT
EPS = 1e-06
CFL = 0.5
DTAU = 0.3
ROOT_EPS = 1e-06
LANES = 128
GROUPS = TILES_DEV // LANES

F32 = jnp.float32
BF16 = jnp.bfloat16
MESH = pl.DeviceIdType.MESH


class Line:
    def __init__(self, cell):
        self.cell, self.made = cell, {}

    def get(self, kind, k):
        if (kind, k) not in self.made:
            self.made[kind, k] = getattr(self, kind)(k)
        return self.made[kind, k]

    def first(self, k):
        return self.get("cell", k + 1) - self.get("cell", k)

    def second(self, k):
        return self.get("first", k + 1) - self.get("first", k)

    def third(self, k):
        return self.get("second", k + 1) - self.get("second", k)

    def fourth(self, k):
        return self.get("third", k) - self.get("third", k - 1)

    def square(self, k):
        return self.get("second", k) * self.get("second", k)

    def half(self, k):
        return (0.5 * self.get("second", k)) * self.get("second", k + 1)

    def base(self, k):
        return self.get("third", k) * self.get("third", k) * (2.0 / 3.0) + 0.5 * EPS

    def low(self, k):
        return self.get("base", k) - self.get("half", k)

    def ind_a(self, k):
        return self.get("low", k) + self.get("square", k + 1)

    def ind_b(self, k):
        return self.get("base", k) + self.get("half", k)

    def ind_c(self, k):
        return self.get("low", k) + self.get("square", k)

    def weight_a(self, k):
        r = recip(self.get("ind_a", k))
        return r * r

    def weight_b(self, k):
        r = recip(self.get("ind_b", k))
        return r * r * 6.0

    def weight_c(self, k):
        r = recip(self.get("ind_c", k))
        return r * r

    def triple_a(self, k):
        return self.get("weight_a", k) * 3.0

    def triple_c(self, k):
        return self.get("weight_c", k) * 3.0

    def twice(self, k):
        return self.get("fourth", k) + self.get("fourth", k)


def recip(x):
    return pl.reciprocal(x, approx=True)


def advect_line(cell, flow_of):
    get = Line(cell).get
    for c in range(8):
        flow, size = flow_of(c)
        up = flow > 0
        ra = recip(jnp.where(up, get("ind_a", c), get("ind_c", c + 3)))
        rb = recip(jnp.where(up, get("ind_b", c + 1), get("ind_b", c + 2)))
        rc = recip(jnp.where(up, get("ind_c", c + 2), get("ind_a", c + 1)))
        wa = ra * ra
        wb = rb * rb * 6.0
        wc = rc * rc * 3.0
        far = jnp.where(up, get("fourth", c + 1), get("fourth", c + 3))
        num = wa * (far + far) + wc * get("fourth", c + 2)
        corr = num * recip(wa + wb + wc)
        linear = 3.0 * (get("cell", c + 4) - get("cell", c + 2)) - jnp.where(up, get("third", c + 1), get("third", c + 2))
        yield flow * linear - size * corr


def reinit_line(cell, sign_of):
    get = Line(cell).get
    for c in range(8):
        sign = sign_of(c)
        linear = 3.0 * (get("cell", c + 4) - get("cell", c + 2))
        mid = get("fourth", c + 2)
        wa, wb, wc = get("weight_a", c), get("weight_b", c + 1), get("triple_c", c + 2)
        corr_b = (wa * get("twice", c + 1) + wc * mid) * recip(wa + wb + wc)
        wa, wb, wc = get("weight_c", c + 3), get("weight_b", c + 2), get("triple_a", c + 1)
        corr_f = (wa * get("twice", c + 3) + wc * mid) * recip(wa + wb + wc)
        back = linear - get("third", c + 1) - corr_b
        fore = get("third", c + 2) - linear - corr_f
        m = jnp.maximum(jnp.maximum(sign * back, sign * fore), 0.0)
        yield m * m


def split_rows(value):
    hi = value.astype(BF16)
    lo = (value - hi.astype(F32)).astype(BF16)
    return jnp.concatenate([hi, lo], axis=0)


def two_part_dot(lhs, rhs):
    res = jnp.dot(lhs, rhs, preferred_element_type=F32)
    blocks = res.shape[0] // (2 * BLOCK)
    return [
        res[2 * BLOCK * k : 2 * BLOCK * k + BLOCK] + res[2 * BLOCK * k + BLOCK : 2 * BLOCK * (k + 1)]
        for k in range(blocks)
    ]


def kernel(
    n_band, n_sub, low,
    ls_ref, vel_ref, nb_ref, adv_out, out_ref,
    p0, pc, adv, sgn, vel, vz, size, az, ay,
    halo_xa, halo_xb, halo_ya, halo_yb, halo_za, halo_zb, faces_x, faces_y, faces_z, came_x, came_y,
    local_m, pack_x, pack_y, unpack_x, unpack_y, tri, pres,
    nb_s, ids_s, krow, kcol, send_x, send_y, recv_x, recv_y, ar_send, ar_near, ar_far, step_s,
    in_sem, out_sem, tx_x, rx_x, tx_y, rx_y, ar_tx, ar_rx,
):
    band = lax.axis_index("band")
    sub = lax.axis_index("sub")
    n_high = n_band // low
    n_near = low * n_sub
    band_up, band_dn = lax.rem(band + 1, n_band), lax.rem(band + n_band - 1, n_band)
    sub_up, sub_dn = lax.rem(sub + 1, n_sub), lax.rem(sub + n_sub - 1, n_sub)
    band_low = lax.rem(band, low)

    def near_peer(d):
        return (band - band_low + lax.rem(band_low + d // n_sub, low), lax.rem(sub + d % n_sub, n_sub))

    def far_peer(d):
        return (lax.rem(band + d * low, n_band), sub)

    def lanes(g):
        return pl.ds(g * LANES, LANES)

    in_copies = []
    for g in range(GROUPS):
        in_copies.append(pltpu.make_async_copy(ls_ref.at[:, :, lanes(g)], p0.at[g], in_sem.at[12 + g]))
    for k in range(3):
        for g in range(GROUPS):
            in_copies.append(
                pltpu.make_async_copy(vel_ref.at[k, :, :, lanes(g)], vel.at[k, g], in_sem.at[4 * k + g])
            )
    for copy in in_copies:
        copy.start()

    peers = [(band_up, sub), (band_dn, sub)]
    peers += [near_peer(d) for d in range(1, n_near)]
    peers += [far_peer(d) for d in range(1, n_high)]
    barrier = pltpu.get_barrier_semaphore()
    for peer in peers:
        pl.semaphore_signal(barrier, inc=1, device_id=peer, device_id_type=MESH)

    nb_s[...] = jnp.full((8, TILES_DEV), -1, jnp.int32)
    nb_s[0:6, :] = nb_ref[...]
    nb = nb_s[...]
    base = (band * n_sub + sub) * TILES_DEV
    present = nb >= 0
    is_local = (nb >= base) & (nb < base + TILES_DEV)
    remote = present & jnp.logical_not(is_local)
    ids_s[0] = jnp.where(is_local, nb - base, -1)
    presf = jnp.where(present, 1.0, 0.0)
    for d in range(6):
        for g in range(GROUPS):
            pres[d, g] = jnp.broadcast_to(presf[d : d + 1, g * LANES : (g + 1) * LANES], (16, LANES))

    def fill_tri(k, carry):
        rows = pl.ds(pl.multiple_of(16 * k, 16), 16)
        iota = lax.broadcasted_iota(jnp.int32, (16, TILES_DEV), 0) + 16 * k
        lane = lax.broadcasted_iota(jnp.int32, (16, TILES_DEV), 1)
        tri[rows, :] = jnp.where(iota < lane, 1.0, 0.0).astype(BF16)
        return carry

    lax.fori_loop(0, TILES_DEV // 16, fill_tri, 0)
    flags = jnp.where(remote, 1.0, 0.0)
    flags16 = jnp.concatenate([flags, jnp.zeros_like(flags)], axis=0).astype(BF16)
    place = jnp.dot(flags16, tri[...], preferred_element_type=F32)[0:8]
    keys = jnp.where(remote, nb.astype(F32), 1e9)
    krow[...] = jnp.zeros_like(krow)
    krow[0:4, :] = keys[0:4]
    krow[4:8, :] = jnp.where(remote, place, -1.0)[0:4]
    for c in range(GROUPS):
        kcol[c * LANES : (c + 1) * LANES, :] = krow[:, c * LANES : (c + 1) * LANES].T

    def ar_copies(r):
        peer, slots, n = ((near_peer, ar_near, n_near), (far_peer, ar_far, n_high))[r]
        first = (0, n_near)[r]
        return [
            pltpu.make_async_remote_copy(
                src_ref=ar_send.at[r],
                dst_ref=slots.at[d - 1],
                send_sem=ar_tx.at[first + d - 1],
                recv_sem=ar_rx.at[first + d - 1],
                device_id=peer(d),
                device_id_type=MESH,
            )
            for d in range(1, n)
        ], slots

    def ar_start(r, value):
        ar_send[r] = value
        for copy in ar_copies(r)[0]:
            copy.start()

    def ar_finish(r):
        value = ar_send[r]
        copies, slots = ar_copies(r)
        for k, copy in enumerate(copies):
            copy.wait()
            value = jnp.maximum(value, slots[k])
        return value

    def copy_x(t, d, r):
        return pltpu.make_async_remote_copy(
            src_ref=send_x.at[d, r],
            dst_ref=recv_x.at[t, 1 - d, r],
            send_sem=tx_x.at[d, r],
            recv_sem=rx_x.at[t, d, r],
            device_id=((band_dn, sub), (band_up, sub))[d],
            device_id_type=MESH,
        )

    def copy_y(t, d):
        return pltpu.make_async_remote_copy(
            src_ref=send_y.at[d],
            dst_ref=recv_y.at[t, 1 - d],
            send_sem=tx_y.at[d],
            recv_sem=rx_y.at[t, d],
            device_id=((band, sub_dn), (band, sub_up))[d],
            device_id_type=MESH,
        )

    def fill_pack(k, carry):
        lane_x = lax.broadcasted_iota(jnp.int32, (16, SLOTS_X), 1).astype(F32)
        lane_y = lax.broadcasted_iota(jnp.int32, (16, LANES), 1).astype(F32)
        for j in range(4):
            rows = pl.ds(pl.multiple_of(64 * k + 16 * j, 16), 16)
            for d in range(2):
                pack_x[d, rows, :] = jnp.where(kcol[rows, 4 + d : 5 + d] == lane_x, 1.0, 0.0).astype(BF16)
                pack_y[d, rows, :] = jnp.where(kcol[rows, 6 + d : 7 + d] == lane_y, 1.0, 0.0).astype(BF16)
        return carry

    lax.fori_loop(0, TILES_DEV // 64, fill_pack, 0)

    def put_face(ref, lead, l, col, hi, lo):
        ref[(*lead, pl.ds(pl.multiple_of(16 * l, 16), 16), col)] = hi
        ref[(*lead, pl.ds(pl.multiple_of(BLOCK + 16 * l, 16), 16), col)] = lo

    def outer_block(k):
        return [(pl.multiple_of(48 * k, 16), 16)], ((1 - k, k), (1 - k, k + 1))

    third_block = [(16, 8), (40, 8)], ((1, 2), (0, 0))
    fourth_block = [(24, 16)], ()

    def take(ref, lead, rows):
        pieces = [ref[(*lead, pl.ds(start, size), slice(None))] for start, size in rows]
        return pieces[0] if len(pieces) == 1 else jnp.concatenate(pieces, axis=0)

    def put(ref, lead, rows, value):
        first = 0
        for start, size in rows:
            ref[(*lead, pl.ds(start, size), slice(None))] = value[first : first + size]
            first += size

    def put_faces_xy(g, c, y_faces):
        col = pl.ds(g * LANES, LANES)
        kept = []

        def add(x, value):
            hi = value.astype(BF16)
            rest = value - hi.astype(F32)
            kept.append((value, rest))
            if x not in (3, 4):
                put_face(faces_x, (0 if x > 4 else 1, c), x - 5 if x > 4 else x, col, hi, rest.astype(BF16))
            if x % 2 == 0:
                return
            for j, (d, layer) in enumerate(y_faces):
                hi, lo = [
                    jnp.concatenate([part[8 * j : 8 * j + 8] for part in parts], axis=0).astype(BF16)
                    for parts in zip(*kept[x - 1 : x + 1])
                ]
                put_face(faces_y, (d, x // 2), layer, col, hi, lo)

        return add

    def pack_block_x(c):
        for d in range(2):
            send_x[d, c] = two_part_dot(faces_x[1 - d, c], pack_x[d])[0]

    def pack_y_faces():
        for d in range(2):
            parts = two_part_dot(faces_y[1 - d].reshape(8 * BLOCK, TILES_DEV), pack_y[d])
            send_y[d] = sum(pltpu.roll(parts[i], i * SLOTS_Y, 1) if i else parts[i] for i in range(4))

    def copy_in(c, block):
        rows, y_faces = block
        for g in range(GROUPS):
            faces = put_faces_xy(g, c, y_faces)
            for x in range(8):
                value = take(p0, (g, x), rows)
                put(pc, (g, x), rows, value)
                faces(x, value)
        pack_block_x(c)

    def copy_in_outer(k, carry):
        copy_in(k, outer_block(k))
        return carry

    for copy in in_copies[:GROUPS]:
        copy.wait()
    lax.fori_loop(0, 2, copy_in_outer, 0)
    copy_in(2, third_block)
    pack_y_faces()
    copy_in(3, fourth_block)

    for copy in in_copies[GROUPS:]:
        copy.wait()

    def speeds(idx, top):
        g, x = idx // 8, lax.rem(idx, 8)
        for y in range(8):
            rows = slice(8 * y, 8 * y + 8)
            sizes = [jnp.abs(vel[k, g, x, rows, :]) for k in range(3)]
            top = jnp.maximum(top, sizes[0] + sizes[1] + sizes[2])
            size[0, g, x, rows, :] = sizes[0]
            size[1, g, x, rows, :] = sizes[1]
        for z in range(8):
            turned = vel[2, g, x, pl.ds(z, 8, stride=8), :]
            vz[g, x, 8 * z : 8 * z + 8, :] = turned
            size[2, g, x, 8 * z : 8 * z + 8, :] = jnp.abs(turned)
        return top

    top = lax.fori_loop(0, GROUPS * 8, speeds, jnp.zeros((8, LANES), F32))

    pl.semaphore_wait(barrier, len(peers))

    ar_start(0, top)
    for d in range(2):
        copy_y(0, d).start()
    for c in range(4):
        for d in range(2):
            copy_x(0, d, c).start()

    def fill(k, carry):
        for j in range(2):
            rows = pl.ds(pl.multiple_of(32 * k + 16 * j, 16), 16)
            iota = lax.broadcasted_iota(jnp.int32, (16, TILES_DEV), 0) + (32 * k + 16 * j)
            for d in range(6):
                local_m[d, rows, :] = jnp.where(iota == ids_s[0, d : d + 1, :], 1.0, 0.0).astype(BF16)
        return carry

    lax.fori_loop(0, TILES_DEV // 32, fill, 0)

    def count(k, carry):
        for j in range(8):
            rows = pl.ds(pl.multiple_of(64 * k + 8 * j, 8), 8)
            carry = tuple(
                total + jnp.where(kcol[rows, d : d + 1] < krow[d : d + 1, :], 1.0, 0.0)
                for d, total in enumerate(carry)
            )
        return carry

    zero = jnp.zeros((8, TILES_DEV), F32)
    counts = lax.fori_loop(0, TILES_DEV // 64, count, (zero,) * 4)
    for d in range(4):
        rank = jnp.sum(counts[d], axis=0, keepdims=True).astype(jnp.int32)
        ids_s[1, d : d + 1, :] = jnp.where(remote[d : d + 1], rank, -1)

    def fill_unpack(dest, first):
        def body(k, carry):
            for j in range(2):
                rows = pl.ds(pl.multiple_of(32 * k + 16 * j, 16), 16)
                iota = lax.broadcasted_iota(jnp.int32, (16, TILES_DEV), 0) + (32 * k + 16 * j)
                for d in range(2):
                    dest[d, rows, :] = jnp.where(iota == ids_s[1, first + d : first + d + 1, :], 1.0, 0.0).astype(BF16)
            return carry

        lax.fori_loop(0, dest.shape[1] // 32, body, 0)

    fill_unpack(unpack_x, 0)
    fill_unpack(unpack_y, 2)

    def turned_pair(ref, g, i, k):
        return jnp.concatenate([ref[g, 2 * i + j, pl.ds(k, 8, stride=8), :] for j in range(2)], axis=0)

    def pair(ref, g, i, k):
        return ref[g, 2 * i : 2 * i + 2, 8 * k : 8 * k + 8, :].reshape(16, LANES)

    def put_faces_z(groups):
        for g in groups:
            col = pl.ds(g * LANES, LANES)
            for i in range(4):
                for d, start in ((0, 5), (1, 0)):
                    for l in range(3):
                        value = turned_pair(pc, g, i, start + l)
                        hi = value.astype(BF16)
                        put_face(faces_z, (d, i), l, col, hi, (value - hi.astype(F32)).astype(BF16))

    def group_of(res, g):
        return res[:, g * LANES : (g + 1) * LANES]

    def gather_z(d, half, halo):
        faces = faces_z[d].reshape(8 * BLOCK, TILES_DEV)
        for i, res in enumerate(two_part_dot(faces, local_m[4 + d, :, 2 * half * LANES : 2 * (half + 1) * LANES])):
            for g in range(2):
                halo[d, g, i] = group_of(res, g)

    def gather_z_from(source):
        columns = slice(2 * source * LANES, 2 * (source + 1) * LANES)
        for d in range(2):
            faces = faces_z[d].reshape(8 * BLOCK, TILES_DEV)[:, columns]
            for i, res in enumerate(two_part_dot(faces, local_m[4 + d, columns, : 2 * LANES])):
                for g in range(2):
                    part = group_of(res, g)
                    halo_za[d, g, i] = halo_za[d, g, i] + part if source else part

    def gather_y(d):
        for i, res in enumerate(two_part_dot(faces_y[d].reshape(8 * BLOCK, TILES_DEV), local_m[2 + d])):
            for g in range(GROUPS):
                (halo_ya, halo_yb)[g // 2][d, g % 2, i] = group_of(res, g)

    def gather_x(d):
        for r, res in enumerate(two_part_dot(faces_x[d].reshape(8 * BLOCK, TILES_DEV), local_m[d])):
            for g in range(GROUPS):
                (halo_xa, halo_xb)[r // 2][d, r % 2, g] = group_of(res, g)

    def split_y(t):
        for d in range(2):
            parts = split_rows(recv_y[t, d])
            wide = parts.astype(F32)
            for i in range(4):
                block = pltpu.roll(wide, LANES - i * SLOTS_Y, 1).astype(BF16) if i else parts
                came_y[d, 2 * BLOCK * i : 2 * BLOCK * (i + 1), :] = block

    def split_x(t, half):
        for d in range(2):
            for k in range(2):
                came_x[d, half, 2 * BLOCK * k : 2 * BLOCK * (k + 1), :] = split_rows(recv_x[t, d, 2 * half + k])

    def unpack_half_y(d, half, halo):
        matrix = unpack_y[d, :, 2 * half * LANES : 2 * (half + 1) * LANES]
        for i, res in enumerate(two_part_dot(came_y[d], matrix)):
            for g in range(2):
                halo[d, g, i] = halo[d, g, i] + group_of(res, g)

    def unpack_half_x(d, half, halo):
        for k, res in enumerate(two_part_dot(came_x[d, half], unpack_x[d])):
            for g in range(GROUPS):
                halo[d, k, g] = halo[d, k, g] + group_of(res, g)

    def padded(halo, a, b, there, g, cells):
        masks = {}

        def cell(k):
            if 3 <= k < 11:
                return cells(k - 3)
            side, l, edge = (0, k, 0) if k < 3 else (1, k - 11, 7)
            if side not in masks:
                masks[side] = pres[there + side, g] > 0, cells(edge)
            return jnp.where(masks[side][0], halo[side, a, b, 16 * l : 16 * l + 16, :], masks[side][1])

        return cell

    def z_lines(line, extra, half, k, halo):
        g = 2 * half + k
        for i in range(4):
            cells = functools.partial(turned_pair, pc, g, i)
            for z, value in enumerate(line(padded(halo, k, i, 4, g, cells), functools.partial(extra, g, i))):
                az[g, 2 * i : 2 * i + 2, 8 * z : 8 * z + 8, :] = value.reshape(2, 8, LANES)

    def y_lines(line, extra, half, k, halo):
        g = 2 * half + k
        for i in range(4):
            cells = functools.partial(pair, pc, g, i)
            for y, value in enumerate(line(padded(halo, k, i, 2, g, cells), functools.partial(extra, g, i))):
                total = value + turned_pair(az, g, i, y)
                ay[g, 2 * i : 2 * i + 2, 8 * y : 8 * y + 8, :] = total.reshape(2, 8, LANES)

    def x_lines(line, extra, finish, c, block, halo, k, groups=range(GROUPS), last=False):
        rows, y_faces = block
        ahead = [take(pc, (groups[0], x), rows) for x in range(8)]
        for g in groups:
            cells = ahead
            if g + 1 in groups:
                ahead = [take(pc, (g + 1, x), rows) for x in range(8)]
            faces = put_faces_xy(g, c, y_faces)
            values = line(padded(halo, k, g, 0, g, cells.__getitem__), lambda x: extra(g, x, rows))
            for x, value in enumerate(values):
                fresh = finish(g, x, rows, cells[x], value + take(ay, (g, x), rows))
                if not last:
                    faces(x, fresh)

    def twice(body):
        def step(k, carry):
            body(k)
            return carry

        lax.fori_loop(0, 2, step, 0)

    def copy_out(g, start, size):
        rows = pl.ds(start, size)
        which = {0: 0, 48: 1, 16: 2}[start]
        return pltpu.make_async_copy(
            pc.at[g, :, rows], out_ref.at[:, rows, lanes(g)], out_sem.at[GROUPS * (1 + which) + g]
        )

    def run(t, line, extra_z, extra_y, extra_x, finish, after_z=None, after_y=None, last=False):
        gather_z_from(1)

        def z_first(k):
            gather_z(k, 1, halo_zb)
            z_lines(line, extra_z, 0, k, halo_za)

        def z_second(k):
            gather_y(k)
            z_lines(line, extra_z, 1, k, halo_zb)

        twice(z_first)
        if after_z is not None:
            after_z()
        twice(z_second)
        for d in range(2):
            copy_y(t, d).wait()
        split_y(t)
        unpack_half_y(0, 0, halo_ya)
        unpack_half_y(1, 0, halo_ya)

        def y_first(k):
            gather_x(k)
            unpack_half_y(k, 1, halo_yb)
            y_lines(line, extra_y, 0, k, halo_ya)

        def y_second(k):
            unpack_half_x(k, 0, halo_xa)
            y_lines(line, extra_y, 1, k, halo_yb)

        twice(y_first)
        for r in range(2):
            for d in range(2):
                copy_x(t, d, r).wait()
        split_x(t, 0)
        twice(y_second)
        if after_y is not None:
            after_y()
        for r in range(2, 4):
            for d in range(2):
                copy_x(t, d, r).wait()

        split_x(t, 1)

        def send_on(copies):
            for copy in copies():
                copy.start()

        def x_outer(k):
            unpack_half_x(k, 1, halo_xb)
            if not last:
                pack_block_x(lax.rem(k + 3, 4))
            x_lines(line, extra_x, finish, k, outer_block(k), halo_xa, k, last=last)

        twice(x_outer)
        if last:
            out = [copy_out(g, start, 16) for start in (0, 48) for g in range(GROUPS)]
            for copy in out:
                copy.start()
            x_lines(line, extra_x, finish, 2, third_block, halo_xb, 0, last=True)
            x_lines(line, extra_x, finish, 3, fourth_block, halo_xb, 1, last=True)
            out += [copy_out(g, 16, 32) for g in range(GROUPS)]
            for copy in out[2 * GROUPS :]:
                copy.start()
            for copy in out:
                copy.wait()
            return

        send_on(lambda: [copy_x(t + 1, d, 0) for d in range(2)])
        pack_block_x(1)
        x_lines(line, extra_x, finish, 2, third_block, halo_xb, 0)
        send_on(lambda: [copy_x(t + 1, d, 1) for d in range(2)])
        pack_y_faces()
        x_lines(line, extra_x, finish, 3, fourth_block, halo_xb, 1, range(2))
        send_on(lambda: [copy_y(t + 1, d) for d in range(2)])
        pack_block_x(2)
        put_faces_z(range(2))
        gather_z_from(0)
        x_lines(line, extra_x, finish, 3, fourth_block, halo_xb, 1, range(2, 4))
        send_on(lambda: [copy_x(t + 1, d, 2) for d in range(2)])
        pack_block_x(3)
        put_faces_z(range(2, 4))
        send_on(lambda: [copy_x(t + 1, d, 3) for d in range(2)])

    put_faces_z(range(GROUPS))
    gather_z_from(0)

    def advect_step(t, carry):
        def after_z():
            @pl.when(t == 0)
            def _():
                ar_start(1, ar_finish(0))

        def after_y():
            @pl.when(t == 0)
            def _():
                top = ar_finish(1)
                top = jnp.max(jnp.max(top, axis=1, keepdims=True), axis=0, keepdims=True)
                step_s[...] = jnp.broadcast_to((CFL / 6.0) / top, (16, LANES))

        old = jnp.where(t == 0, 0.0, jnp.where(t == 1, 0.75, 1.0 / 3.0))
        new = jnp.where(t == 0, 1.0, jnp.where(t == 1, 0.25, 2.0 / 3.0))

        def finish(g, x, rows, cell, total):
            value = old * take(p0, (g, x), rows) + new * (cell - step_s[...] * total)
            put(pc, (g, x), rows, value)
            put(adv, (g, x), rows, value)
            put(sgn, (g, x), rows, jnp.where(value > 0, 1.0, -1.0))
            return value

        run(
            t,
            advect_line,
            lambda g, i, z: (pair(vz, g, i, z), pair(size.at[2], g, i, z)),
            lambda g, i, y: (pair(vel.at[1], g, i, y), pair(size.at[1], g, i, y)),
            lambda g, x, rows: (take(vel, (0, g, x), rows), take(size, (0, g, x), rows)),
            finish,
            after_z,
            after_y,
        )
        return carry

    lax.fori_loop(0, STAGES, advect_step, 0)

    adv_copies = [
        pltpu.make_async_copy(adv.at[g], adv_out.at[:, :, lanes(g)], out_sem.at[g]) for g in range(GROUPS)
    ]
    for copy in adv_copies:
        copy.start()

    def reinit_step(k, last):
        def finish(g, x, rows, cell, total):
            v = take(adv, (g, x), rows)
            sign = v * lax.rsqrt(v * v + 1.0)
            root = total * (1.0 / 36.0) + ROOT_EPS
            value = cell + (DTAU * sign) * (1.0 - root * lax.rsqrt(root))
            put(pc, (g, x), rows, value)
            return value

        run(
            STAGES + k,
            reinit_line,
            lambda g, i, z: turned_pair(sgn, g, i, z),
            lambda g, i, y: pair(sgn, g, i, y),
            lambda g, x, rows: take(sgn, (g, x), rows),
            finish,
            last=last,
        )

    for k in range(REINIT):
        reinit_step(k, k == REINIT - 1)
    for copy in adv_copies:
        copy.wait()


def hand_over(a_ref, b_ref, x_ref, y_ref, buf, sem):
    ins, outs = [], []
    for k in range(4):
        part = pl.ds(2 * k, 2)
        for i, (src, dst) in enumerate(((a_ref, x_ref), (b_ref, y_ref))):
            ins.append(pltpu.make_async_copy(src.at[part], buf.at[i, part], sem.at[0, 2 * k + i]))
            outs.append(pltpu.make_async_copy(buf.at[i, part], dst.at[part], sem.at[1, 2 * k + i]))
    for copy in ins:
        copy.start()
    for arrived, onward in zip(ins, outs):
        arrived.wait()
        onward.start()
    for copy in outs:
        copy.wait()


def solution(mesh):
    n_band, n_sub = mesh.shape["band"], mesh.shape["sub"]
    low = min(2, n_band)
    cells = (GROUPS, 8, 64, LANES)

    def local(level_set, velocity, neighbours):
        whole = jax.ShapeDtypeStruct((8, 64, TILES_DEV), F32)
        anywhere = pl.BlockSpec(memory_space=pl.ANY)
        advected, reinitialized = pl.pallas_call(
            functools.partial(kernel, n_band, n_sub, low),
            out_shape=(whole, whole),
            in_specs=[anywhere, anywhere, pl.BlockSpec(memory_space=pltpu.VMEM)],
            out_specs=(anywhere, anywhere),
            scratch_shapes=[
                pltpu.VMEM(cells, F32),
                pltpu.VMEM(cells, F32),
                pltpu.VMEM(cells, F32),
                pltpu.VMEM(cells, F32),
                pltpu.VMEM((3,) + cells, F32),
                pltpu.VMEM(cells, F32),
                pltpu.VMEM((3,) + cells, F32),
                pltpu.VMEM(cells, F32),
                pltpu.VMEM(cells, F32),
                *[pltpu.VMEM((2, 2, GROUPS, BLOCK, LANES), F32)] * 2,
                *[pltpu.VMEM((2, 2, 4, BLOCK, LANES), F32)] * 4,
                pltpu.VMEM((2, 4, 2 * BLOCK, TILES_DEV), BF16),
                pltpu.VMEM((2, 4, 2 * BLOCK, TILES_DEV), BF16),
                pltpu.VMEM((2, 4, 2 * BLOCK, TILES_DEV), BF16),
                pltpu.VMEM((2, 2, 4 * BLOCK, SLOTS_X), BF16),
                pltpu.VMEM((2, 8 * BLOCK, LANES), BF16),
                pltpu.VMEM((6, TILES_DEV, TILES_DEV), BF16),
                pltpu.VMEM((2, TILES_DEV, SLOTS_X), BF16),
                pltpu.VMEM((2, TILES_DEV, LANES), BF16),
                pltpu.VMEM((2, SLOTS_X, TILES_DEV), BF16),
                pltpu.VMEM((2, LANES, TILES_DEV), BF16),
                pltpu.VMEM((TILES_DEV, TILES_DEV), BF16),
                pltpu.VMEM((6, GROUPS, 16, LANES), F32),
                pltpu.VMEM((8, TILES_DEV), jnp.int32),
                pltpu.VMEM((2, 8, TILES_DEV), jnp.int32),
                pltpu.VMEM((LANES, TILES_DEV), F32),
                pltpu.VMEM((TILES_DEV, LANES), F32),
                pltpu.VMEM((2, 4, BLOCK, SLOTS_X), F32),
                pltpu.VMEM((2, BLOCK, LANES), F32),
                pltpu.VMEM((STEPS, 2, 4, BLOCK, SLOTS_X), F32),
                pltpu.VMEM((STEPS, 2, BLOCK, LANES), F32),
                pltpu.VMEM((2, 8, LANES), F32),
                pltpu.VMEM((max(1, low * n_sub - 1), 8, LANES), F32),
                pltpu.VMEM((max(1, n_band // low - 1), 8, LANES), F32),
                pltpu.VMEM((16, LANES), F32),
                pltpu.SemaphoreType.DMA((16,)),
                pltpu.SemaphoreType.DMA((5 * GROUPS,)),
                pltpu.SemaphoreType.DMA((2, 4)),
                pltpu.SemaphoreType.DMA((STEPS, 2, 4)),
                pltpu.SemaphoreType.DMA((2,)),
                pltpu.SemaphoreType.DMA((STEPS, 2)),
                pltpu.SemaphoreType.DMA((low * n_sub + n_band // low,)),
                pltpu.SemaphoreType.DMA((low * n_sub + n_band // low,)),
            ],
            compiler_params=pltpu.CompilerParams(
                collective_id=0, has_side_effects=True, vmem_limit_bytes=56 * 2**20
            ),
        )(level_set.reshape(8, 64, TILES_DEV), velocity.reshape(3, 8, 64, TILES_DEV), neighbours)
        advected, reinitialized = pl.pallas_call(
            hand_over,
            out_shape=(whole, whole),
            in_specs=[anywhere, anywhere],
            out_specs=(anywhere, anywhere),
            scratch_shapes=[pltpu.VMEM((2, 8, 64, TILES_DEV), F32), pltpu.SemaphoreType.DMA((2, 8))],
        )(advected, reinitialized)
        return advected.reshape(8, 8, 8, TILES_DEV), reinitialized.reshape(8, 8, 8, TILES_DEV)

    return jax.shard_map(
        local,
        mesh=mesh,
        in_specs=(
            P(None, None, None, ("band", "sub")),
            P(None, None, None, None, ("band", "sub")),
            P(None, ("band", "sub")),
        ),
        out_specs=(P(None, None, None, ("band", "sub")), P(None, None, None, ("band", "sub"))),
        check_vma=False,
    )
```
